32 devices in a mesh: groups: 1, ep: 32 (over z, y, x, core).
Axes of the slice: x: 2, y: 2, z: 4, core: 2. Of those that a mesh axis runs over, the one named last changes fastest.
Arguments:
- hidden: bfloat16 [2, 128, 7168], P(None, ('groups', 'ep')), may hold values from -6 to 6
- norm_gain: float32 [7168], replicated, may hold values from 0.25 to 1.75
- router: bfloat16 [7168, 6], replicated, may hold values from -0.25 to 0.25
- expert_ids: int32 [2, 128, 2], P(None, ('groups', 'ep')), may hold values from 0 to 5, all different within a row
- replica: int32 [2, 128, 2], P(None, ('groups', 'ep')), may hold values from 0 to 1
- copy_table: int32 [6, 2], replicated, may hold values from 0 to 7, as said below
- gate_w: bfloat16 [7168, 8192], P(None, 'ep'), may hold values from -0.0625 to 0.0625
- up_w: bfloat16 [7168, 8192], P(None, 'ep'), may hold values from -0.0625 to 0.0625
- down_w: bfloat16 [8192, 7168], P('ep'), may hold values from -0.1875 to 0.1875
- query: bfloat16 [2, 128, 64, 576], P(None, ('groups', 'ep')), may hold values from -96 to 96
- cache: bfloat16 [128, 64, 576], P(('groups', 'ep')), may hold values from -6 to 6
- lengths: int32 [128], P(('groups', 'ep')), may hold values from 2 to 62
- fresh_kv: bfloat16 [2, 128, 576], P(None, ('groups', 'ep')), may hold values from -6 to 6
Outputs:
- attended: bfloat16 [2, 128, 64, 512], P(None, ('groups', 'ep'))
- moe_out: bfloat16 [2, 128, 7168], P(None, ('groups', 'ep'))
The draws below stay inside these ranges and needn't reach their ends.
Inputs may be any that keep to these rules, and one draw needn't show every extreme that they name: `copy_table`: column 0 names a different copy for every expert; column 1 equals column 0 except for 2 experts, whose column 1 names the remaining copies, so every copy appears.
All inputs are finite; a program needn't handle non-finite values.
Results may differ from the reference program's by a relative error of at most 0.012.
Values may be sent and summed in bfloat16 or wider, within the bound.
No kernel may reach another device: no remote copies, remote signals or barrier semaphores. Data moves between devices by JAX's collectives and lax.ppermute only.
A program may use at most 128 MiB of HBM per device.

```python
import jax
import jax.numpy as jnp
from jax import lax

D = 7168
H = 64
KV = 512
FW = 1024
TOP = 2
ROWS = 4
CACHE = 64
SPAN = 4
HD = 256
LAT = 576
PHYS = 8
REDUND = 2
EXPERTS = 6
CAP = 2
TOKENS = 128


def draw_query(key, part):
    key = jax.random.fold_in(key, 7)
    values = jnp.clip(jax.random.normal(key, (2, TOKENS, H, LAT), jnp.float32), -6.0, 6.0)
    return values.astype(jnp.bfloat16)


def draw_cache(key, part):
    key = jax.random.fold_in(key, 5)
    values = jnp.clip(jax.random.normal(key, (TOKENS, CACHE, LAT), jnp.float32), -6.0, 6.0)
    return values.astype(jnp.bfloat16)


def draw_copy_table(key, part):
    key = jax.random.fold_in(key, 11)
    order_key, hot_key = jax.random.split(key)
    order = jax.random.permutation(order_key, PHYS)
    hot_experts = jax.random.permutation(hot_key, EXPERTS)[:REDUND]
    first = order[:EXPERTS]
    second = first.at[hot_experts].set(order[EXPERTS:])
    return jnp.stack([first, second], axis=1).astype(jnp.int32)


def place_ends(array, rng, low, high):
    shape = array.shape
    spot = [jax.random.randint(jax.random.fold_in(rng, axis), (), 0, shape[axis]) for axis in range(len(shape))]
    array = array.at[tuple(spot)].set(low)
    longest = shape.index(max(shape))
    spot[longest] = (spot[longest] + 1) % shape[longest]
    return array.at[tuple(spot)].set(high)


def level_of(own_key, shape, cuts, least, largest):
    level = 1.0
    for dim, shards_of in cuts:
        steps = jax.random.uniform(jax.random.fold_in(jax.random.fold_in(own_key, 6), dim), (shards_of,), jnp.float32, least / len(cuts), largest / len(cuts))
        level = level * jnp.repeat(jnp.exp(steps), shape[dim] // shards_of).reshape((-1,) + (1,) * (len(shape) - 1 - dim))
    return level


def distinct(stream_key, rows, count, top, lift):
    sequence = jax.random.permutation(jax.random.fold_in(stream_key, 1), count)
    favour = sequence
    for power in range(3):
        favour = favour * favour // count
    favour = favour * lift // count
    lots = jax.random.randint(jax.random.fold_in(stream_key, 2), (rows, count), 0, 4096) + favour
    fixed_rows = jax.random.permutation(jax.random.fold_in(stream_key, 3), rows)[jnp.arange(count) % rows]
    lots = jnp.where(jnp.arange(rows)[:, None] == fixed_rows[None, :], 1 << 14, lots)
    merit = lots * count + jnp.arange(count)
    return lax.top_k(merit.astype(jnp.int32), top)[1].astype(jnp.int32)


def gaussian(own_key, shape, scale, bound, pieces=(), kind=jnp.bfloat16):
    level = level_of(own_key, shape, pieces, -0.22, 0.18) if pieces else 1.0
    drawn = jax.random.normal(own_key, shape, jnp.float32) * scale * level
    return jnp.minimum(jnp.maximum(drawn, -bound), bound).astype(kind)


def setup_inputs(seed: int = 0, part: int = 0) -> dict:
    arg_keys = jax.random.split(jax.random.key(seed), 14)
    own_keys = jax.random.split(jax.random.fold_in(arg_keys[13], part), 14)
    return {
        "hidden": gaussian(own_keys[0], (2, TOKENS, D), 1.0, 6.0, ((1, 32),)),
        "norm_gain": jnp.clip(1.0 + 0.15 * jax.random.normal(arg_keys[1], (D,), jnp.float32), 0.25, 1.75),
        "router": gaussian(arg_keys[2], (D, EXPERTS), (D // 16) ** -0.5, 0.25),
        "expert_ids": distinct(own_keys[3], 2 * TOKENS, EXPERTS, TOP, 5461).reshape((2, TOKENS, TOP)),
        "replica": place_ends(jax.random.randint(own_keys[4], (2, TOKENS, TOP), 0, 2), jax.random.fold_in(own_keys[4], 1), 0, 1).astype(jnp.int32),
        "copy_table": draw_copy_table(jax.random.fold_in(arg_keys[13], 71), part),
        "gate_w": gaussian(arg_keys[6], (D, PHYS * FW), D ** -0.5, 0.0625, ((1, 32),)),
        "up_w": gaussian(arg_keys[7], (D, PHYS * FW), D ** -0.5, 0.0625, ((1, 32),)),
        "down_w": gaussian(arg_keys[8], (PHYS * FW, D), FW ** -0.5, 0.1875, ((0, 32),)),
        "query": draw_query(jax.random.fold_in(jax.random.fold_in(arg_keys[13], part), 71), part),
        "cache": draw_cache(jax.random.fold_in(jax.random.fold_in(arg_keys[13], part), 71), part),
        "lengths": place_ends(jax.random.randint(own_keys[11], (TOKENS,), 2, CACHE - 1), jax.random.fold_in(own_keys[11], 1), 2, (CACHE - 1) - 1).astype(jnp.int32),
        "fresh_kv": gaussian(own_keys[12], (2, TOKENS, LAT), 1.0, 6.0, ((1, 32),)),
    }


softmax_scale = 192.0 ** (-0.5)
routed_scale = 2.5
norm_eps = 1e-06
masked_score = -1e+30

def attend(queries, cache, lengths, fresh):
    query_f = queries.astype(jnp.float32)
    cache_f = cache.astype(jnp.float32)
    fresh_f = fresh.astype(jnp.float32)
    old_scores = jnp.einsum('nhl,ncl->nhc', query_f, cache_f) * softmax_scale
    new_scores = jnp.einsum('nhl,nml->nhm', query_f, fresh_f) * softmax_scale
    positions = lax.broadcasted_iota(jnp.int32, old_scores.shape, 2)
    valid = positions < lengths[:, None, None]
    old_scores = jnp.where(valid, old_scores, masked_score)
    highest = jnp.maximum(lax.optimization_barrier(jnp.max(old_scores, axis=2)), lax.optimization_barrier(jnp.max(new_scores, axis=2)))[:, :, None]
    old_terms = jnp.where(valid, jnp.exp(old_scores - highest), 0.0)
    new_terms = jnp.exp(new_scores - highest)
    total = lax.optimization_barrier(jnp.sum(old_terms, axis=2, keepdims=True)) + lax.optimization_barrier(jnp.sum(new_terms, axis=2, keepdims=True))
    old_probs = (old_terms / total).astype(jnp.bfloat16).astype(jnp.float32)
    new_probs = (new_terms / total).astype(jnp.bfloat16).astype(jnp.float32)
    output = jnp.einsum('nhc,ncv->nhv', old_probs, cache_f[:, :, :KV])
    output = output + jnp.einsum('nhm,nmv->nhv', new_probs, fresh_f[:, :, :KV])
    return output.astype(jnp.bfloat16)

def mixture(hidden, norm_gain, router, expert_ids, replica, copy_table, gate_stack, up_stack, down_stack):
    token_count = hidden.shape[0]
    source_count = token_count // ROWS
    pair_count = ROWS * TOP
    hidden_f = hidden.astype(jnp.float32)
    mean_square = lax.optimization_barrier(jnp.mean(hidden_f * hidden_f, axis=1, keepdims=True))
    normed = (hidden_f * lax.rsqrt(mean_square + norm_eps) * norm_gain).astype(jnp.bfloat16)
    scores = jax.nn.sigmoid(jnp.dot(normed, router, preferred_element_type=jnp.float32))
    picked = jnp.take_along_axis(scores, expert_ids, axis=1)
    weights = routed_scale * picked / lax.optimization_barrier(jnp.sum(picked, axis=1, keepdims=True))
    copies = copy_table[expert_ids, replica].reshape(source_count, pair_count).astype(jnp.int32)
    onehot = (copies[:, :, None] == jnp.arange(PHYS, dtype=jnp.int32)[None, None, :]).astype(jnp.int32)
    slot_index = lax.optimization_barrier(jnp.sum(jnp.cumsum(onehot, axis=1) * onehot, axis=2)) - 1
    sources = jnp.arange(source_count, dtype=jnp.int32)[:, None]
    drop_lane = source_count * CAP
    lane = jnp.where(slot_index < CAP, sources * CAP + slot_index, drop_lane).astype(jnp.int32)
    assigned = jnp.repeat(normed, TOP, axis=0).reshape(source_count, pair_count, D)
    buffers = jnp.zeros((PHYS, drop_lane + 1, D), jnp.bfloat16).at[copies, lane].set(assigned)[:, :drop_lane]

    def expert(operands):
        rows_in, gate_part, up_part, down_part = operands
        gate = jnp.dot(rows_in, gate_part, preferred_element_type=jnp.float32)
        upper = jnp.dot(rows_in, up_part, preferred_element_type=jnp.float32)
        inner = (jax.nn.silu(gate) * upper).astype(jnp.bfloat16)
        split_inner = inner.astype(jnp.float32).reshape(inner.shape[0], SPAN, HD)
        split_down = down_part.astype(jnp.float32).reshape(SPAN, HD, D)
        partials = jnp.einsum('rjh,jhd->rjd', split_inner, split_down).astype(jnp.bfloat16)
        return lax.optimization_barrier(jnp.sum(partials.astype(jnp.float32), axis=1))
    copy_out = lax.map(expert, (buffers, gate_stack, up_stack, down_stack))
    padded = jnp.concatenate([copy_out, jnp.zeros((PHYS, 1, D), jnp.float32)], axis=1)
    gathered = padded[copies, lane].reshape(token_count, TOP, D)
    return lax.optimization_barrier(jnp.sum(weights[:, :, None] * gathered, axis=1)).astype(jnp.bfloat16)

def reference(hidden, norm_gain, router, expert_ids, replica, copy_table, gate_w, up_w, down_w, query, cache, lengths, fresh_kv):
    gate_stack = gate_w.reshape(D, PHYS, FW).transpose(1, 0, 2)
    up_stack = up_w.reshape(D, PHYS, FW).transpose(1, 0, 2)
    down_stack = down_w.reshape(PHYS, FW, D)
    attended = []
    moe_parts = []
    for decode_step in range(2):
        moe_parts.append(mixture(hidden[decode_step], norm_gain, router, expert_ids[decode_step], replica[decode_step], copy_table, gate_stack, up_stack, down_stack))
        fresh = jnp.moveaxis(fresh_kv[:decode_step + 1], 0, 1)
        attended.append(attend(query[decode_step], cache, lengths, fresh))
    return (jnp.stack(attended), jnp.stack(moe_parts))
```

```python
import jax
import jax.numpy as jnp
from jax import lax
from jax.experimental import pallas as pl
from jax.experimental.pallas import tpu as pltpu
from jax.sharding import PartitionSpec as P

KV = 512
SPAN = 4

softmax_scale = 192.0 ** (-0.5)
routed_scale = 2.5
norm_eps = 1e-06
masked_score = -1e30


def flipped(value, low_core, high_core):
    pairs = [(e, e ^ (high_core if e % 2 else low_core)) for e in range(lax.axis_size("ep"))]
    return lax.ppermute(value, "ep", pairs)


def attend(queries, cache, lengths, fresh):
    old_scores = (
        jnp.einsum("nhl,ncl->nhc", queries, cache, preferred_element_type=jnp.float32)
        * softmax_scale
    )
    new_scores = (
        jnp.einsum("nhl,nml->nhm", queries, fresh, preferred_element_type=jnp.float32)
        * softmax_scale
    )
    positions = lax.broadcasted_iota(jnp.int32, old_scores.shape, 2)
    valid = positions < lengths[:, None, None]
    old_scores = jnp.where(valid, old_scores, masked_score)
    highest = jnp.maximum(jnp.max(old_scores, axis=2), jnp.max(new_scores, axis=2))[:, :, None]
    old_terms = jnp.where(valid, jnp.exp(old_scores - highest), 0.0)
    new_terms = jnp.exp(new_scores - highest)
    total = jnp.sum(old_terms, axis=2, keepdims=True) + jnp.sum(new_terms, axis=2, keepdims=True)
    old_probs = (old_terms / total).astype(jnp.bfloat16)
    new_probs = (new_terms / total).astype(jnp.bfloat16)
    output = jnp.einsum(
        "nhc,ncv->nhv", old_probs, cache[:, :, :KV], preferred_element_type=jnp.float32
    )
    output = output + jnp.einsum(
        "nhm,nmv->nhv", new_probs, fresh[:, :, :KV], preferred_element_type=jnp.float32
    )
    return output.astype(jnp.bfloat16)


def expert_kernel(*refs):
    rows_refs = refs[:-9]
    gate_ref, up_ref, down_ref, out_ref, gate_v, up_v, down_v, rows_v, sems = refs[-9:]
    depth, hidden_units = gate_ref.shape
    parts = gate_v.shape[0]
    step = depth // parts
    copies = []
    for i in range(parts):
        ds = pl.ds(i * step, step)
        copies.append(
            (
                pltpu.make_async_copy(gate_ref.at[ds, :], gate_v.at[i], sems.at[0, i]),
                pltpu.make_async_copy(up_ref.at[ds, :], up_v.at[i], sems.at[1, i]),
            )
        )
    downs = [
        pltpu.make_async_copy(down_ref.at[:, pl.ds(i * step, step)], down_v.at[i], sems.at[2, i])
        for i in range(parts)
    ]
    for pair in copies:
        pair[0].start()
        pair[1].start()
    for copy in downs:
        copy.start()
    at = 0
    for ref in rows_refs:
        rows_v[pl.ds(at, ref.shape[0]), :] = ref[...]
        at += ref.shape[0]
    gate = jnp.zeros((at, hidden_units), jnp.float32)
    upper = jnp.zeros((at, hidden_units), jnp.float32)
    for i in range(parts):
        copies[i][0].wait()
        copies[i][1].wait()
        x = rows_v[:, pl.ds(i * step, step)]
        gate += jnp.dot(x, gate_v[i], preferred_element_type=jnp.float32)
        upper += jnp.dot(x, up_v[i], preferred_element_type=jnp.float32)
    inner = (gate / (1.0 + jnp.exp(-gate)) * upper).astype(jnp.bfloat16)
    for i in range(parts):
        downs[i].wait()
        out_ref[:, pl.ds(i * step, step)] = jnp.dot(
            inner, down_v[i], preferred_element_type=jnp.float32
        ).astype(jnp.bfloat16)


def experts(row_parts, gate_w, up_w, down_w):
    rows = sum(part.shape[0] for part in row_parts)
    depth, hidden_units = gate_w.shape
    parts = 7
    step = depth // parts
    vmem = pl.BlockSpec(memory_space=pltpu.VMEM)
    hbm = pl.BlockSpec(memory_space=pl.ANY)
    return pl.pallas_call(
        expert_kernel,
        out_shape=jax.ShapeDtypeStruct((rows, depth), jnp.bfloat16),
        in_specs=[vmem] * len(row_parts) + [hbm] * 3,
        out_specs=vmem,
        scratch_shapes=[
            pltpu.VMEM((parts, step, hidden_units), jnp.bfloat16),
            pltpu.VMEM((parts, step, hidden_units), jnp.bfloat16),
            pltpu.VMEM((parts, hidden_units, step), jnp.bfloat16),
            pltpu.VMEM((rows, depth), jnp.bfloat16),
            pltpu.SemaphoreType.DMA((3, parts)),
        ],
        compiler_params=pltpu.CompilerParams(vmem_limit_bytes=(16 << 20) + rows * depth * 12),
        cost_estimate=pl.CostEstimate(
            flops=6 * rows * depth * hidden_units,
            bytes_accessed=6 * depth * hidden_units + 4 * rows * depth,
            transcendentals=rows * hidden_units,
        ),
        name="experts",
    )(*row_parts, gate_w, up_w, down_w)


def routing(chosen, scores, copy_table, targets, slots):
    ids, replica = chosen[0], chosen[1]
    expert_count = scores.shape[-1]
    sources, steps, rows, top = ids.shape
    chooser = ids[..., None] == lax.broadcasted_iota(jnp.int32, (*ids.shape, expert_count), 4)
    picked = jnp.sum(jnp.where(chooser, scores[:, :, :, None, :], 0.0), axis=4)
    weights = routed_scale * picked / jnp.sum(picked, axis=3, keepdims=True)
    table = jnp.where(replica[..., None] == 0, copy_table[:, 0], copy_table[:, 1])
    copies = jnp.sum(jnp.where(chooser, table, 0), axis=4)
    flat = copies.reshape(sources, steps, rows * top)
    same = flat[..., :, None] == flat[..., None, :]
    earlier = lax.broadcasted_iota(jnp.int32, same.shape, 3) < lax.broadcasted_iota(
        jnp.int32, same.shape, 2
    )
    slot = jnp.sum((same & earlier).astype(jnp.int32), axis=3).reshape(copies.shape)
    shape = (targets.shape[0], slots, sources, steps, rows, top)
    hit = (copies == targets[:, None, None, None, None, None]) & (
        slot == lax.broadcasted_iota(jnp.int32, shape, 1)
    )
    place = jnp.sum(hit.astype(jnp.float32), axis=5)
    weigh = jnp.sum(jnp.where(hit, weights, 0.0), axis=5)
    blocks = sources * steps
    own = jnp.eye(blocks, dtype=jnp.float32)

    def spread(values):
        values = values.reshape(targets.shape[0], slots, blocks, rows)
        wide = values.transpose(0, 2, 1, 3)[:, :, :, None, :] * own[None, :, None, :, None]
        return wide.reshape(targets.shape[0] * blocks * slots, blocks * rows)

    return spread(place), spread(weigh)


def mixture(hidden, norm_gain, router, expert_ids, replica, copy_table, gate_w, up_w, down_w):
    axis_count = lax.axis_size("ep")
    groups = axis_count // SPAN
    messages = groups // 2
    steps, row_count, depth = hidden.shape
    top_count = expert_ids.shape[2]
    slots = max(2, 2 * row_count * top_count // groups)
    index = lax.axis_index("ep")
    core = index % 2
    group = index // SPAN
    deltas = [(groups - 1 - 2 * m, groups - 2 - 2 * m) for m in range(messages)]

    raw = hidden.reshape(steps * row_count, depth)
    chosen = jnp.stack([expert_ids, replica])
    other_raw = flipped(raw, 1, 1)
    other_chosen = flipped(chosen, 1, 1)
    both_chosen = jnp.stack([chosen, other_chosen], axis=1)
    hidden_f = jnp.concatenate([raw, other_raw], axis=0).astype(jnp.float32)
    mean_square = jnp.mean(hidden_f * hidden_f, axis=1, keepdims=True)
    normed = (hidden_f * lax.rsqrt(mean_square + norm_eps) * norm_gain).astype(jnp.bfloat16)
    scores = jax.nn.sigmoid(jnp.dot(normed, router, preferred_element_type=jnp.float32))
    targets = group ^ jnp.where(
        core == 0, jnp.array([d[0] for d in deltas]), jnp.array([d[1] for d in deltas])
    )
    place, weigh = routing(
        both_chosen, scores.reshape(2, steps, row_count, -1), copy_table, targets, slots
    )
    packed = jnp.dot(
        place.astype(jnp.bfloat16), normed, preferred_element_type=jnp.float32
    ).astype(jnp.bfloat16)
    size = packed.shape[0] // messages

    def rounds(values):
        parts = [
            flipped(values[m * size : (m + 1) * size], SPAN * low, SPAN * high)
            for m, (low, high) in enumerate(deltas)
        ]
        return jnp.concatenate(parts, axis=0)

    near = rounds(packed)
    far = flipped(near, 2, 2)
    near_other = flipped(near, 1, 1)
    far_other = flipped(far, 1, 1)
    lane = near.shape[0]
    partial = experts([near, far, near_other, far_other], gate_w, up_w, down_w)
    summed = partial[: 2 * lane].astype(jnp.float32) + flipped(partial[2 * lane :], 1, 1).astype(
        jnp.float32
    )
    total = summed[:lane] + flipped(summed[lane:].astype(jnp.bfloat16), 2, 2).astype(jnp.float32)
    returned = rounds(total.astype(jnp.bfloat16))
    result = jnp.dot(
        weigh.T,
        returned.astype(jnp.float32),
        precision=lax.Precision.HIGHEST,
        preferred_element_type=jnp.float32,
    )
    half = steps * row_count
    result = result[:half] + flipped(result[half:].astype(jnp.bfloat16), 1, 1).astype(jnp.float32)
    return result.astype(jnp.bfloat16).reshape(steps, row_count, depth)


def per_device(
    hidden,
    norm_gain,
    router,
    expert_ids,
    replica,
    copy_table,
    gate_w,
    up_w,
    down_w,
    query,
    cache,
    lengths,
    fresh_kv,
):
    moe_out = mixture(
        hidden, norm_gain, router, expert_ids, replica, copy_table, gate_w, up_w, down_w
    )
    attended = []
    for decode_step in range(2):
        fresh = jnp.moveaxis(fresh_kv[: decode_step + 1], 0, 1)
        attended.append(attend(query[decode_step], cache, lengths, fresh))
    return (jnp.stack(attended), moe_out)


def solution(mesh):
    return jax.shard_map(
        per_device,
        mesh=mesh,
        in_specs=(
            P(None, ("groups", "ep"), None),
            P(),
            P(),
            P(None, ("groups", "ep"), None),
            P(None, ("groups", "ep"), None),
            P(),
            P(None, "ep"),
            P(None, "ep"),
            P("ep", None),
            P(None, ("groups", "ep"), None, None),
            P(("groups", "ep"), None, None),
            P(("groups", "ep")),
            P(None, ("groups", "ep"), None),
        ),
        out_specs=(P(None, ("groups", "ep"), None, None), P(None, ("groups", "ep"), None)),
        check_vma=False,
    )
```

```python
import functools

import jax
import jax.numpy as jnp
from jax import lax
from jax.experimental import pallas as pl
from jax.experimental.pallas import tpu as pltpu
from jax.sharding import PartitionSpec as P

KV = 512
SPAN = 4

softmax_scale = 192.0 ** (-0.5)
routed_scale = 2.5
norm_eps = 1e-06
masked_score = -1e30


def flipped(value, low_core, high_core):
    pairs = [(e, e ^ (high_core if e % 2 else low_core)) for e in range(lax.axis_size("ep"))]
    return lax.ppermute(value, "ep", pairs)


def attend_kernel(lengths_ref, query_ref, cache_ref, fresh_ref, out_ref):
    steps, tokens, heads, _ = query_ref.shape
    slots = cache_ref.shape[1]
    pad = 128 - slots
    for n in range(tokens):
        row = lax.broadcasted_iota(jnp.int32, (pad, 1), 0)
        extra = jnp.zeros((pad, fresh_ref.shape[2]), jnp.float32)
        for s in range(steps):
            block = fresh_ref[s].astype(jnp.float32)
            which = lax.broadcasted_iota(jnp.int32, block.shape, 0) == n
            one = jnp.sum(jnp.where(which, block, 0.0), axis=0, keepdims=True)
            extra = jnp.where(row == s, one, extra)
        keys = jnp.concatenate([cache_ref[n], extra.astype(jnp.bfloat16)], axis=0)
        queries = jnp.concatenate([query_ref[s, n] for s in range(steps)], axis=0)
        scores = (
            lax.dot_general(
                queries, keys, (((1,), (1,)), ((), ())), preferred_element_type=jnp.float32
            )
            * softmax_scale
        )
        position = lax.broadcasted_iota(jnp.int32, scores.shape, 1)
        step = lax.broadcasted_iota(jnp.int32, scores.shape, 0) // heads
        valid = (position < lengths_ref[n]) | (
            (position >= slots) & (position - slots <= step)
        )
        scores = jnp.where(valid, scores, masked_score)
        terms = jnp.exp(scores - jnp.max(scores, axis=1, keepdims=True))
        terms = jnp.where(valid, terms, 0.0)
        probs = (terms / jnp.sum(terms, axis=1, keepdims=True)).astype(jnp.bfloat16)
        mixed = jnp.dot(probs, keys[:, :KV], preferred_element_type=jnp.float32)
        for s in range(steps):
            out_ref[s, n] = mixed[s * heads : (s + 1) * heads].astype(jnp.bfloat16)


def attend(query, cache, lengths, fresh):
    steps, tokens, heads, width = query.shape
    vmem = pl.BlockSpec(memory_space=pltpu.VMEM)
    return pl.pallas_call(
        attend_kernel,
        out_shape=jax.ShapeDtypeStruct((steps, tokens, heads, KV), jnp.bfloat16),
        in_specs=[pl.BlockSpec(memory_space=pltpu.SMEM)] + [vmem] * 3,
        out_specs=vmem,
        compiler_params=pltpu.CompilerParams(vmem_limit_bytes=12 << 20),
        cost_estimate=pl.CostEstimate(
            flops=4 * steps * tokens * heads * 128 * width,
            bytes_accessed=2 * (2 * query.size + cache.size),
            transcendentals=steps * tokens * heads * 128,
        ),
        name="attention",
    )(lengths, query, cache, fresh)


def expert_kernel(mine_ref, other_ref, gate_ref, up_ref, down_ref, out_ref, send_ref, rows_v):
    rows = mine_ref.shape[0]
    depth, hidden_units = gate_ref.shape
    rows_v[:rows, :] = mine_ref[...]
    rows_v[rows:, :] = other_ref[...]
    parts = 7
    step = depth // parts
    gate = jnp.zeros((2 * rows, hidden_units), jnp.float32)
    upper = jnp.zeros((2 * rows, hidden_units), jnp.float32)
    for i in range(parts):
        ds = pl.ds(i * step, step)
        x = rows_v[:, ds]
        gate += jnp.dot(x, gate_ref[ds, :], preferred_element_type=jnp.float32)
        upper += jnp.dot(x, up_ref[ds, :], preferred_element_type=jnp.float32)
    inner = (gate / (1.0 + jnp.exp(-gate)) * upper).astype(jnp.bfloat16)
    for i in range(parts):
        ds = pl.ds(i * step, step)
        partial = jnp.dot(inner, down_ref[:, ds], preferred_element_type=jnp.float32)
        out_ref[:, ds] = partial[:rows].astype(jnp.bfloat16)
        send_ref[:, ds] = partial[rows:].astype(jnp.bfloat16)


def experts(mine, other, gate_w, up_w, down_w):
    rows, depth = mine.shape
    hidden_units = gate_w.shape[1]
    vmem = pl.BlockSpec(memory_space=pltpu.VMEM)
    return pl.pallas_call(
        expert_kernel,
        out_shape=[jax.ShapeDtypeStruct((rows, depth), jnp.bfloat16)] * 2,
        in_specs=[vmem] * 5,
        out_specs=[vmem] * 2,
        scratch_shapes=[pltpu.VMEM((2 * rows, depth), jnp.bfloat16)],
        compiler_params=pltpu.CompilerParams(vmem_limit_bytes=(16 << 20) + rows * depth * 24),
        cost_estimate=pl.CostEstimate(
            flops=12 * rows * depth * hidden_units,
            bytes_accessed=6 * depth * hidden_units + 8 * rows * depth,
            transcendentals=2 * rows * hidden_units,
        ),
        name="experts",
    )(mine, other, gate_w, up_w, down_w)


def pack_kernel(
    slots,
    groups,
    table_ref,
    ids_ref,
    replica_ref,
    other_ids_ref,
    other_replica_ref,
    raw_ref,
    other_ref,
    gain_ref,
    normed_ref,
    place_ref,
    choose_ref,
    *refs,
):
    message_refs, raw_v = refs[:-1], refs[-1]
    steps, tokens, depth = raw_ref.shape
    top = ids_ref.shape[2]
    index = lax.axis_index("ep")
    core = lax.rem(index, 2)
    group = lax.div(index, SPAN)
    message_rows = 2 * steps * slots
    for b, ref in enumerate((raw_ref, other_ref)):
        for s in range(steps):
            at = (b * steps + s) * tokens
            raw_v[at : at + tokens, :] = ref[s].astype(jnp.float32)
    raw = raw_v[...]
    mean_square = jnp.mean(raw * raw, axis=1, keepdims=True)
    normed = (raw * lax.rsqrt(mean_square + norm_eps) * gain_ref[...]).astype(jnp.bfloat16)
    normed_ref[...] = normed

    row = lax.broadcasted_iota(jnp.int32, place_ref.shape[1:], 0)
    column = lax.broadcasted_iota(jnp.int32, place_ref.shape[1:], 1)
    expert = lax.broadcasted_iota(jnp.int32, choose_ref.shape[1:], 0)
    token = lax.broadcasted_iota(jnp.int32, choose_ref.shape[1:], 1)
    place_row = [jnp.full(place_ref.shape[1:], -1, jnp.int32) for _ in range(top)]
    choice = [jnp.full(choose_ref.shape[1:], -1, jnp.int32) for _ in range(top)]
    for b, (ids, replicas) in enumerate(
        ((ids_ref, replica_ref), (other_ids_ref, other_replica_ref))
    ):
        for s in range(steps):
            block = b * steps + s
            earlier = []
            for t in range(tokens):
                for k in range(top):
                    copy = table_ref[ids[s, t, k], replicas[s, t, k]]
                    slot = sum([(copy == c).astype(jnp.int32) for c in earlier], jnp.int32(0))
                    earlier.append(copy)
                    delta = copy ^ group
                    kept = ((delta & 1) != core) & (slot < slots)
                    at = ((groups - 1 - delta) >> 1) * message_rows + block * slots + slot
                    at = jnp.where(kept, at, -1)
                    here = block * tokens + t
                    place_row[k] = jnp.where(column == here, at, place_row[k])
                    choice[k] = jnp.where(token == here, ids[s, t, k], choice[k])
    total = jnp.zeros(place_ref.shape[1:], jnp.float32)
    for k in range(top):
        hit = (place_row[k] == row).astype(jnp.float32)
        place_ref[k] = hit
        choose_ref[k] = (choice[k] == expert).astype(jnp.float32)
        total = total + hit
    packed = jnp.dot(total.astype(jnp.bfloat16), normed, preferred_element_type=jnp.float32)
    for m, ref in enumerate(message_refs):
        ref[...] = packed[m * message_rows : (m + 1) * message_rows].astype(jnp.bfloat16)


def pack(slots, groups, hidden, other, gain, copy_table, own_choice, other_choice, experts_total):
    steps, tokens, depth = hidden.shape
    top = own_choice[0].shape[2]
    messages = groups // 2
    message_rows = 2 * steps * slots
    columns = 2 * steps * tokens
    vmem = pl.BlockSpec(memory_space=pltpu.VMEM)
    smem = pl.BlockSpec(memory_space=pltpu.SMEM)
    shape = jax.ShapeDtypeStruct
    out = pl.pallas_call(
        functools.partial(pack_kernel, slots, groups),
        out_shape=[
            shape((columns, depth), jnp.bfloat16),
            shape((top, messages * message_rows, columns), jnp.float32),
            shape((top, experts_total, columns), jnp.float32),
        ]
        + [shape((message_rows, depth), jnp.bfloat16)] * messages,
        in_specs=[smem] * 5 + [vmem] * 3,
        out_specs=[vmem] * (3 + messages),
        scratch_shapes=[pltpu.VMEM((columns, depth), jnp.float32)],
        compiler_params=pltpu.CompilerParams(
            vmem_limit_bytes=(8 << 20) + 4 * messages * message_rows * depth * 2
        ),
        name="pack",
    )(copy_table, *own_choice, *other_choice, hidden, other, gain)
    return out[0], out[1], out[2], out[3:]


def weigh_kernel(normed_ref, router_ref, place_ref, choose_ref, weigh_ref):
    scores = jax.nn.sigmoid(
        lax.dot_general(
            router_ref[...],
            normed_ref[...],
            (((1,), (1,)), ((), ())),
            preferred_element_type=jnp.float32,
        )
    )
    top = place_ref.shape[0]
    picked = [jnp.sum(choose_ref[k] * scores, axis=0, keepdims=True) for k in range(top)]
    total = sum(picked[1:], picked[0])
    weigh = jnp.zeros(weigh_ref.shape, jnp.float32)
    for k in range(top):
        weigh = weigh + place_ref[k] * (routed_scale * picked[k] / total)
    weigh_ref[...] = weigh


def weigh(normed, router_t, place, choose):
    vmem = pl.BlockSpec(memory_space=pltpu.VMEM)
    return pl.pallas_call(
        weigh_kernel,
        out_shape=jax.ShapeDtypeStruct(place.shape[1:], jnp.float32),
        in_specs=[vmem] * 4,
        out_specs=vmem,
        cost_estimate=pl.CostEstimate(
            flops=2 * normed.size * 256, bytes_accessed=2 * normed.size, transcendentals=256
        ),
        name="weigh",
    )(normed, router_t, place, choose)


def combine_kernel(weigh_ref, *refs):
    part_refs, own_ref, send_ref = refs[:-2], refs[-2], refs[-1]
    weights = weigh_ref[...]
    high = weights.astype(jnp.bfloat16)
    left = weights - high.astype(jnp.float32)
    middle = left.astype(jnp.bfloat16)
    low = (left - middle.astype(jnp.float32)).astype(jnp.bfloat16)
    rows = jnp.concatenate([ref[...].astype(jnp.float32) for ref in part_refs], axis=0)
    rows = rows.astype(jnp.bfloat16)
    pieces = [
        lax.dot_general(w, rows, (((0,), (0,)), ((), ())), preferred_element_type=jnp.float32)
        for w in (high, middle, low)
    ]
    result = pieces[0] + (pieces[1] + pieces[2])
    half = own_ref.shape[0]
    own_ref[...] = result[:half]
    send_ref[...] = result[half:].astype(jnp.bfloat16)


def combine(weights, parts):
    depth = parts[0].shape[1]
    half = weights.shape[1] // 2
    vmem = pl.BlockSpec(memory_space=pltpu.VMEM)
    return pl.pallas_call(
        combine_kernel,
        out_shape=[
            jax.ShapeDtypeStruct((half, depth), jnp.float32),
            jax.ShapeDtypeStruct((half, depth), jnp.bfloat16),
        ],
        in_specs=[vmem] * (1 + len(parts)),
        out_specs=[vmem] * 2,
        compiler_params=pltpu.CompilerParams(
            vmem_limit_bytes=(8 << 20) + 8 * weights.shape[0] * depth
        ),
        name="combine",
    )(weights, *parts)


def finish_kernel(own_ref, received_ref, out_ref):
    result = own_ref[...] + received_ref[...].astype(jnp.float32)
    steps, tokens, _ = out_ref.shape
    for s in range(steps):
        out_ref[s] = result[s * tokens : (s + 1) * tokens].astype(jnp.bfloat16)


def finish(own, received, shape):
    vmem = pl.BlockSpec(memory_space=pltpu.VMEM)
    return pl.pallas_call(
        finish_kernel,
        out_shape=jax.ShapeDtypeStruct(shape, jnp.bfloat16),
        in_specs=[vmem] * 2,
        out_specs=vmem,
        name="finish",
    )(own, received)


def mixture(hidden, norm_gain, router, expert_ids, replica, copy_table, gate_w, up_w, down_w):
    groups = lax.axis_size("ep") // SPAN
    messages = groups // 2
    tokens = hidden.shape[1]
    slots = max(2, 2 * tokens * expert_ids.shape[2] // groups)
    deltas = [(groups - 1 - 2 * m, groups - 2 - 2 * m) for m in range(messages)]

    def swapped(value):
        return flipped(value, 1, 1)

    other_choice = (swapped(expert_ids), swapped(replica))
    normed, place, choose, packed = pack(
        slots,
        groups,
        hidden,
        swapped(hidden),
        norm_gain[None, :],
        copy_table,
        (expert_ids, replica),
        other_choice,
        router.shape[1],
    )

    def rounds(parts):
        return [
            flipped(part, SPAN * low, SPAN * high) for part, (low, high) in zip(parts, deltas)
        ]

    near = jnp.concatenate(rounds(packed), axis=0)
    weights = weigh(normed, router.T, place, choose)
    far = flipped(near, 2, 2)
    near_own, near_send = experts(near, swapped(near), gate_w, up_w, down_w)
    near_sum = near_own.astype(jnp.float32) + swapped(near_send).astype(jnp.float32)
    far_own, far_send = experts(far, swapped(far), gate_w, up_w, down_w)
    far_sum = far_own.astype(jnp.float32) + swapped(far_send).astype(jnp.float32)
    total = near_sum + flipped(far_sum.astype(jnp.bfloat16), 2, 2).astype(jnp.float32)
    total = total.astype(jnp.bfloat16)
    size = total.shape[0] // messages
    returned = rounds([total[m * size : (m + 1) * size] for m in range(messages)])
    own, send = combine(weights, returned)
    return finish(own, swapped(send), hidden.shape)


def per_device(
    hidden,
    norm_gain,
    router,
    expert_ids,
    replica,
    copy_table,
    gate_w,
    up_w,
    down_w,
    query,
    cache,
    lengths,
    fresh_kv,
):
    moe_out = mixture(
        hidden, norm_gain, router, expert_ids, replica, copy_table, gate_w, up_w, down_w
    )
    attended = attend(query, cache, lengths, fresh_kv)
    return (attended, moe_out)


def solution(mesh):
    return jax.shard_map(
        per_device,
        mesh=mesh,
        in_specs=(
            P(None, ("groups", "ep"), None),
            P(),
            P(),
            P(None, ("groups", "ep"), None),
            P(None, ("groups", "ep"), None),
            P(),
            P(None, "ep"),
            P(None, "ep"),
            P("ep", None),
            P(None, ("groups", "ep"), None, None),
            P(("groups", "ep"), None, None),
            P(("groups", "ep")),
            P(None, ("groups", "ep"), None),
        ),
        out_specs=(P(None, ("groups", "ep"), None, None), P(None, ("groups", "ep"), None)),
        check_vma=False,
    )
```

```python
import functools

import jax
import jax.numpy as jnp
from jax import lax
from jax.experimental import pallas as pl
from jax.experimental.pallas import tpu as pltpu
from jax.sharding import PartitionSpec as P

KV = 512
SPAN = 4

softmax_scale = 192.0 ** (-0.5)
routed_scale = 2.5
norm_eps = 1e-06
masked_score = -1e30
EXPERT_PARTS = 7
MARK = jax.ShapeDtypeStruct((8, 128), jnp.float32)


def flipped(value, low_core, high_core):
    pairs = [(e, e ^ (high_core if e % 2 else low_core)) for e in range(lax.axis_size("ep"))]
    return lax.ppermute(value, "ep", pairs)


def attend_kernel(lengths_ref, query_ref, cache_ref, fresh_ref, out_ref, mark_ref):
    mark_ref[...] = jnp.zeros(mark_ref.shape, mark_ref.dtype)
    steps, tokens, heads, _ = query_ref.shape
    slots = cache_ref.shape[1]
    pad = 128 - slots
    for n in range(tokens):
        row = lax.broadcasted_iota(jnp.int32, (pad, 1), 0)
        extra = jnp.zeros((pad, fresh_ref.shape[2]), jnp.float32)
        for s in range(steps):
            block = fresh_ref[s].astype(jnp.float32)
            which = lax.broadcasted_iota(jnp.int32, block.shape, 0) == n
            one = jnp.sum(jnp.where(which, block, 0.0), axis=0, keepdims=True)
            extra = jnp.where(row == s, one, extra)
        keys = jnp.concatenate([cache_ref[n], extra.astype(jnp.bfloat16)], axis=0)
        queries = jnp.concatenate([query_ref[s, n] for s in range(steps)], axis=0)
        scores = (
            lax.dot_general(
                queries, keys, (((1,), (1,)), ((), ())), preferred_element_type=jnp.float32
            )
            * softmax_scale
        )
        position = lax.broadcasted_iota(jnp.int32, scores.shape, 1)
        step = lax.broadcasted_iota(jnp.int32, scores.shape, 0) // heads
        valid = (position < lengths_ref[n]) | (
            (position >= slots) & (position - slots <= step)
        )
        scores = jnp.where(valid, scores, masked_score)
        terms = jnp.exp(scores - jnp.max(scores, axis=1, keepdims=True))
        terms = jnp.where(valid, terms, 0.0)
        probs = (terms / jnp.sum(terms, axis=1, keepdims=True)).astype(jnp.bfloat16)
        mixed = jnp.dot(probs, keys[:, :KV], preferred_element_type=jnp.float32)
        for s in range(steps):
            out_ref[s, n] = mixed[s * heads : (s + 1) * heads].astype(jnp.bfloat16)


def attend(query, cache, lengths, fresh):
    steps, tokens, heads, width = query.shape
    vmem = pl.BlockSpec(memory_space=pltpu.VMEM)
    return pl.pallas_call(
        attend_kernel,
        out_shape=[jax.ShapeDtypeStruct((steps, tokens, heads, KV), jnp.bfloat16), MARK],
        in_specs=[pl.BlockSpec(memory_space=pltpu.SMEM)] + [vmem] * 3,
        out_specs=[vmem] * 2,
        compiler_params=pltpu.CompilerParams(vmem_limit_bytes=12 << 20),
        cost_estimate=pl.CostEstimate(
            flops=4 * steps * tokens * heads * 128 * width,
            bytes_accessed=2 * (2 * query.size + cache.size),
            transcendentals=steps * tokens * heads * 128,
        ),
        name="attention",
    )(lengths, query, cache, fresh)


def load_kernel(gate_ref, up_ref, down_ref, _, gate_v, up_v, down_v, mark_ref, sems):
    copies = [
        pltpu.make_async_copy(source, target, sems.at[i])
        for i, (source, target) in enumerate(
            ((gate_ref, gate_v), (up_ref, up_v), (down_ref, down_v))
        )
    ]
    for copy in copies:
        copy.start()
    mark_ref[...] = jnp.zeros(mark_ref.shape, mark_ref.dtype)
    for copy in copies:
        copy.wait()


def load(weights, earlier):
    vmem = pl.BlockSpec(memory_space=pltpu.VMEM)
    anywhere = pl.BlockSpec(memory_space=pl.ANY)
    *held, mark = pl.pallas_call(
        load_kernel,
        out_shape=[jax.ShapeDtypeStruct(w.shape, w.dtype) for w in weights] + [MARK],
        in_specs=[anywhere] * 4,
        out_specs=[vmem] * 4,
        scratch_shapes=[pltpu.SemaphoreType.DMA((3,))],
        compiler_params=pltpu.CompilerParams(vmem_limit_bytes=40 << 20),
        name="load",
    )(*weights, earlier)
    return held, mark


def expert_kernel(count, *refs):
    part_refs, refs = refs[:count], refs[count:]
    gate_ref, up_ref, down_ref, _, *out_refs, mark_ref, rows_v = refs
    size = out_refs[0].shape[0]
    step = rows_v.shape[1] // EXPERT_PARTS
    rows = part_refs[0].shape[0]
    for i, ref in enumerate(part_refs):
        rows_v[i * rows : (i + 1) * rows, :] = ref[...]
    mark_ref[...] = jnp.zeros(mark_ref.shape, mark_ref.dtype)
    gate, upper = 0.0, 0.0
    for i in range(EXPERT_PARTS):
        ds = pl.ds(i * step, step)
        x = rows_v[:, ds]
        gate = gate + jnp.dot(x, gate_ref[ds, :], preferred_element_type=jnp.float32)
        upper = upper + jnp.dot(x, up_ref[ds, :], preferred_element_type=jnp.float32)
    inner = (gate / (1.0 + jnp.exp(-gate)) * upper).astype(jnp.bfloat16)
    for i in range(EXPERT_PARTS):
        ds = pl.ds(i * step, step)
        partial = jnp.dot(inner, down_ref[:, ds], preferred_element_type=jnp.float32)
        for j, ref in enumerate(out_refs):
            ref[:, ds] = partial[j * size : (j + 1) * size].astype(jnp.bfloat16)


def experts(parts, weights, earlier, size):
    rows, depth = parts[0].shape
    count = len(parts)
    outs = count * rows // size
    vmem = pl.BlockSpec(memory_space=pltpu.VMEM)
    out = pl.pallas_call(
        functools.partial(expert_kernel, count),
        out_shape=[jax.ShapeDtypeStruct((size, depth), jnp.bfloat16)] * outs + [MARK],
        in_specs=[vmem] * (count + 3) + [pl.BlockSpec(memory_space=pl.ANY)],
        out_specs=[vmem] * (outs + 1),
        scratch_shapes=[pltpu.VMEM((count * rows, depth), jnp.bfloat16)],
        compiler_params=pltpu.CompilerParams(
            vmem_limit_bytes=(16 << 20) + count * rows * depth * 8
        ),
        name="experts",
    )(*parts, *weights, earlier)
    return out[:outs], out[outs]


def join_kernel(count, *refs):
    out_ref = refs[-1]
    rows, depth = out_ref.shape
    step = depth // EXPERT_PARTS
    for i in range(EXPERT_PARTS):
        ds = pl.ds(i * step, step)
        joined = jnp.concatenate([ref[:, ds].astype(jnp.float32) for ref in refs[:count]], axis=0)
        out_ref[:, ds] = joined.astype(jnp.bfloat16)


def join(parts, earlier):
    depth = parts[0].shape[1]
    rows = sum(part.shape[0] for part in parts)
    vmem = pl.BlockSpec(memory_space=pltpu.VMEM)
    return pl.pallas_call(
        functools.partial(join_kernel, len(parts)),
        out_shape=jax.ShapeDtypeStruct((rows, depth), jnp.bfloat16),
        in_specs=[vmem] * len(parts) + [pl.BlockSpec(memory_space=pl.ANY)] * len(earlier),
        out_specs=vmem,
        compiler_params=pltpu.CompilerParams(vmem_limit_bytes=(2 << 20) + 8 * rows * depth),
        name="join",
    )(*parts, *earlier)


def after_kernel(value_ref, earlier_ref, out_ref):
    out_ref[...] = value_ref[...]


def after(value, earlier):
    vmem = pl.BlockSpec(memory_space=pltpu.VMEM)
    return pl.pallas_call(
        after_kernel,
        out_shape=jax.ShapeDtypeStruct(value.shape, value.dtype),
        in_specs=[vmem, pl.BlockSpec(memory_space=pl.ANY)],
        out_specs=vmem,
        compiler_params=pltpu.CompilerParams(vmem_limit_bytes=(2 << 20) + 6 * value.size),
        name="after",
    )(value, earlier)


def add_kernel(count, messages, *refs):
    terms, part_refs = refs[:count], refs[-messages:]
    depth = terms[0].shape[1]
    size = part_refs[0].shape[0]
    step = depth // EXPERT_PARTS
    for i in range(EXPERT_PARTS):
        ds = pl.ds(i * step, step)
        total = terms[0][:, ds].astype(jnp.float32)
        for ref in terms[1:]:
            total = total + ref[:, ds].astype(jnp.float32)
        for m, ref in enumerate(part_refs):
            ref[:, ds] = total[m * size : (m + 1) * size].astype(jnp.bfloat16)


def add(terms, messages, earlier):
    rows, depth = terms[0].shape
    vmem = pl.BlockSpec(memory_space=pltpu.VMEM)
    return pl.pallas_call(
        functools.partial(add_kernel, len(terms), messages),
        out_shape=[jax.ShapeDtypeStruct((rows // messages, depth), jnp.bfloat16)] * messages,
        in_specs=[vmem] * len(terms) + [pl.BlockSpec(memory_space=pl.ANY)] * len(earlier),
        out_specs=[vmem] * messages,
        compiler_params=pltpu.CompilerParams(vmem_limit_bytes=(4 << 20) + 16 * rows * depth),
        name="add",
    )(*terms, *earlier)


def pack_kernel(
    slots,
    groups,
    table_ref,
    ids_ref,
    replica_ref,
    other_ids_ref,
    other_replica_ref,
    raw_ref,
    other_ref,
    gain_ref,
    normed_ref,
    place_ref,
    choose_ref,
    *refs,
):
    message_refs, raw_v = refs[:-1], refs[-1]
    steps, tokens, depth = raw_ref.shape
    top = ids_ref.shape[1]
    index = lax.axis_index("ep")
    core = lax.rem(index, 2)
    group = lax.div(index, SPAN)
    message_rows = 2 * steps * slots
    for b, ref in enumerate((raw_ref, other_ref)):
        for s in range(steps):
            at = (b * steps + s) * tokens
            raw_v[at : at + tokens, :] = ref[s].astype(jnp.float32)
    raw = raw_v[...]
    mean_square = jnp.mean(raw * raw, axis=1, keepdims=True)
    normed = (raw * lax.rsqrt(mean_square + norm_eps) * gain_ref[...]).astype(jnp.bfloat16)
    normed_ref[...] = normed

    row = lax.broadcasted_iota(jnp.int32, place_ref.shape[1:], 0)
    column = lax.broadcasted_iota(jnp.int32, place_ref.shape[1:], 1)
    expert = lax.broadcasted_iota(jnp.int32, choose_ref.shape[1:], 0)
    token = lax.broadcasted_iota(jnp.int32, choose_ref.shape[1:], 1)
    place_row = [jnp.full(place_ref.shape[1:], -1, jnp.int32) for _ in range(top)]
    choice = [jnp.full(choose_ref.shape[1:], -1, jnp.int32) for _ in range(top)]
    for b, (ids, replicas) in enumerate(
        ((ids_ref, replica_ref), (other_ids_ref, other_replica_ref))
    ):
        for s in range(steps):
            block = b * steps + s
            earlier = []
            for t in range(tokens):
                for k in range(top):
                    copy = table_ref[replicas[s, k, t], ids[s, k, t]]
                    slot = sum([(copy == c).astype(jnp.int32) for c in earlier], jnp.int32(0))
                    earlier.append(copy)
                    delta = copy ^ group
                    kept = ((delta & 1) != core) & (slot < slots)
                    at = ((groups - 1 - delta) >> 1) * message_rows + block * slots + slot
                    at = jnp.where(kept, at, -1)
                    here = block * tokens + t
                    place_row[k] = jnp.where(column == here, at, place_row[k])
                    choice[k] = jnp.where(token == here, ids[s, k, t], choice[k])
    total = jnp.zeros(place_ref.shape[1:], jnp.float32)
    for k in range(top):
        hit = (place_row[k] == row).astype(jnp.float32)
        place_ref[k] = hit
        choose_ref[k] = (choice[k] == expert).astype(jnp.float32)
        total = total + hit
    packed = jnp.dot(total.astype(jnp.bfloat16), normed, preferred_element_type=jnp.float32)
    for m, ref in enumerate(message_refs):
        ref[...] = packed[m * message_rows : (m + 1) * message_rows].astype(jnp.bfloat16)


def pack(slots, groups, hidden, other, gain, copy_table, own_choice, other_choice, experts_total):
    steps, tokens, depth = hidden.shape
    top = own_choice[0].shape[1]
    messages = groups // 2
    message_rows = 2 * steps * slots
    columns = 2 * steps * tokens
    vmem = pl.BlockSpec(memory_space=pltpu.VMEM)
    smem = pl.BlockSpec(memory_space=pltpu.SMEM)
    shape = jax.ShapeDtypeStruct
    out = pl.pallas_call(
        functools.partial(pack_kernel, slots, groups),
        out_shape=[
            shape((columns, depth), jnp.bfloat16),
            shape((top, messages * message_rows, columns), jnp.float32),
            shape((top, experts_total, columns), jnp.float32),
        ]
        + [shape((message_rows, depth), jnp.bfloat16)] * messages,
        in_specs=[smem] * 5 + [vmem] * 3,
        out_specs=[vmem] * (3 + messages),
        scratch_shapes=[pltpu.VMEM((columns, depth), jnp.float32)],
        compiler_params=pltpu.CompilerParams(
            vmem_limit_bytes=62 << 20
        ),
        name="pack",
    )(copy_table, *own_choice, *other_choice, hidden, other, gain)
    return out[0], out[1], out[2], out[3:]


def weigh_kernel(normed_ref, router_ref, place_ref, choose_ref, weigh_ref):
    scores = jax.nn.sigmoid(
        lax.dot_general(
            router_ref[...],
            normed_ref[...],
            (((1,), (1,)), ((), ())),
            preferred_element_type=jnp.float32,
        )
    )
    top = place_ref.shape[0]
    picked = [jnp.sum(choose_ref[k] * scores, axis=0, keepdims=True) for k in range(top)]
    total = sum(picked[1:], picked[0])
    weigh = jnp.zeros(weigh_ref.shape, jnp.float32)
    for k in range(top):
        weigh = weigh + place_ref[k] * (routed_scale * picked[k] / total)
    weigh_ref[...] = weigh


def weigh(normed, router_t, place, choose):
    vmem = pl.BlockSpec(memory_space=pltpu.VMEM)
    return pl.pallas_call(
        weigh_kernel,
        out_shape=jax.ShapeDtypeStruct(place.shape[1:], jnp.float32),
        in_specs=[vmem] * 4,
        out_specs=vmem,
        cost_estimate=pl.CostEstimate(
            flops=2 * normed.size * 256, bytes_accessed=2 * normed.size, transcendentals=256
        ),
        compiler_params=pltpu.CompilerParams(vmem_limit_bytes=4 << 20),
        name="weigh",
    )(normed, router_t, place, choose)


def combine_kernel(weigh_ref, *refs):
    part_refs, own_ref, send_ref = refs[:-2], refs[-2], refs[-1]
    weights = weigh_ref[...]
    high = weights.astype(jnp.bfloat16)
    left = weights - high.astype(jnp.float32)
    middle = left.astype(jnp.bfloat16)
    low = (left - middle.astype(jnp.float32)).astype(jnp.bfloat16)
    rows = jnp.concatenate([ref[...].astype(jnp.float32) for ref in part_refs], axis=0)
    rows = rows.astype(jnp.bfloat16)
    pieces = [
        lax.dot_general(w, rows, (((0,), (0,)), ((), ())), preferred_element_type=jnp.float32)
        for w in (high, middle, low)
    ]
    result = pieces[0] + (pieces[1] + pieces[2])
    half = own_ref.shape[0]
    own_ref[...] = result[:half]
    send_ref[...] = result[half:].astype(jnp.bfloat16)


def combine(weights, parts):
    depth = parts[0].shape[1]
    half = weights.shape[1] // 2
    vmem = pl.BlockSpec(memory_space=pltpu.VMEM)
    return pl.pallas_call(
        combine_kernel,
        out_shape=[
            jax.ShapeDtypeStruct((half, depth), jnp.float32),
            jax.ShapeDtypeStruct((half, depth), jnp.bfloat16),
        ],
        in_specs=[vmem] * (1 + len(parts)),
        out_specs=[vmem] * 2,
        compiler_params=pltpu.CompilerParams(
            vmem_limit_bytes=(8 << 20) + 8 * weights.shape[0] * depth
        ),
        name="combine",
    )(weights, *parts)


def finish_kernel(own_ref, received_ref, out_ref):
    result = own_ref[...] + received_ref[...].astype(jnp.float32)
    steps, tokens, _ = out_ref.shape
    for s in range(steps):
        out_ref[s] = result[s * tokens : (s + 1) * tokens].astype(jnp.bfloat16)


def finish(own, received, shape):
    vmem = pl.BlockSpec(memory_space=pltpu.VMEM)
    return pl.pallas_call(
        finish_kernel,
        out_shape=jax.ShapeDtypeStruct(shape, jnp.bfloat16),
        in_specs=[vmem] * 2,
        out_specs=vmem,
        compiler_params=pltpu.CompilerParams(vmem_limit_bytes=4 << 20),
        name="finish",
    )(own, received)


def mixture(
    hidden, norm_gain, router, expert_ids, replica, copy_table, gate_w, up_w, down_w, attended_mark
):
    groups = lax.axis_size("ep") // SPAN
    messages = groups // 2
    tokens = hidden.shape[1]
    slots = max(2, 2 * tokens * expert_ids.shape[2] // groups)
    deltas = [(groups - 1 - 2 * m, groups - 2 - 2 * m) for m in range(messages)]

    def swapped(value):
        return flipped(value, 1, 1)

    own_choice = (expert_ids.transpose(0, 2, 1), replica.transpose(0, 2, 1))
    other_choice = (swapped(own_choice[0]), swapped(own_choice[1]))
    normed, place, choose, packed = pack(
        slots,
        groups,
        hidden,
        swapped(hidden),
        norm_gain[None, :],
        copy_table.T,
        own_choice,
        other_choice,
        router.shape[1],
    )

    def rounds(parts):
        return [
            flipped(part, SPAN * low, SPAN * high) for part, (low, high) in zip(parts, deltas)
        ]

    weights = weigh(normed, router.T, place, choose)
    expert_weights = (gate_w, up_w, down_w)
    half = messages // 2
    size = packed[0].shape[0]
    received = rounds(packed)
    held, mark = load(expert_weights, place)
    near = join(received, [mark])
    far = flipped(near, 2, 2)
    near_out, mark = experts([near, swapped(near)], held, mark, half * size)
    far_out, mark = experts([far, swapped(after(far, mark))], held, mark, half * size)
    (far_sum_a,) = add([far_out[0], swapped(far_out[2])], 1, [])
    (far_sum_b,) = add([far_out[1], swapped(far_out[3])], 1, [])
    total_a = add(
        [near_out[0], swapped(near_out[2]), flipped(far_sum_a, 2, 2)],
        half,
        [mark, weights, attended_mark],
    )
    total_b = add([near_out[1], swapped(near_out[3]), flipped(far_sum_b, 2, 2)], half, [total_a[0]])
    returned = rounds([*total_a, *total_b])
    own, send = combine(weights, returned)
    return finish(own, swapped(send), hidden.shape)


def per_device(
    hidden,
    norm_gain,
    router,
    expert_ids,
    replica,
    copy_table,
    gate_w,
    up_w,
    down_w,
    query,
    cache,
    lengths,
    fresh_kv,
):
    attended, attended_mark = attend(query, cache, lengths, fresh_kv)
    moe_out = mixture(
        hidden,
        norm_gain,
        router,
        expert_ids,
        replica,
        copy_table,
        gate_w,
        up_w,
        down_w,
        attended_mark,
    )
    return (attended, moe_out)


def solution(mesh):
    return jax.shard_map(
        per_device,
        mesh=mesh,
        in_specs=(
            P(None, ("groups", "ep"), None),
            P(),
            P(),
            P(None, ("groups", "ep"), None),
            P(None, ("groups", "ep"), None),
            P(),
            P(None, "ep"),
            P(None, "ep"),
            P("ep", None),
            P(None, ("groups", "ep"), None, None),
            P(("groups", "ep"), None, None),
            P(("groups", "ep")),
            P(None, ("groups", "ep"), None),
        ),
        out_specs=(P(None, ("groups", "ep"), None, None), P(None, ("groups", "ep"), None)),
        check_vma=False,
    )
```

```python
import functools

import jax
import jax.numpy as jnp
from jax import lax
from jax.experimental import pallas as pl
from jax.experimental.pallas import tpu as pltpu
from jax.sharding import PartitionSpec as P

KV = 512
SPAN = 4

softmax_scale = 192.0 ** (-0.5)
routed_scale = 2.5
norm_eps = 1e-06
masked_score = -1e30
EXPERT_PARTS = 7
MARK = jax.ShapeDtypeStruct((8, 128), jnp.float32)


def flipped(value, low_core, high_core):
    pairs = [(e, e ^ (high_core if e % 2 else low_core)) for e in range(lax.axis_size("ep"))]
    return lax.ppermute(value, "ep", pairs)


def lanes(groups):
    hops = [(d & 1) + (d >> 1) for d in range(groups)]
    chosen = ([], [])
    for d in sorted(range(groups), key=lambda d: (-hops[d], -d)):
        sums = [sum(hops[e] for e in lane) for lane in chosen]
        lane = 0 if sums[0] <= sums[1] else 1
        if 2 * len(chosen[lane]) == groups:
            lane = 1 - lane
        chosen[lane].append(d)
    return list(zip(*chosen))


def attend_kernel(lengths_ref, query_ref, cache_ref, fresh_ref, out_ref, mark_ref):
    mark_ref[...] = jnp.zeros(mark_ref.shape, mark_ref.dtype)
    steps, tokens, heads, _ = query_ref.shape
    slots = cache_ref.shape[1]
    pad = 128 - slots
    for n in range(tokens):
        row = lax.broadcasted_iota(jnp.int32, (pad, 1), 0)
        extra = jnp.zeros((pad, fresh_ref.shape[2]), jnp.float32)
        for s in range(steps):
            block = fresh_ref[s].astype(jnp.float32)
            which = lax.broadcasted_iota(jnp.int32, block.shape, 0) == n
            one = jnp.sum(jnp.where(which, block, 0.0), axis=0, keepdims=True)
            extra = jnp.where(row == s, one, extra)
        keys = jnp.concatenate([cache_ref[n], extra.astype(jnp.bfloat16)], axis=0)
        queries = jnp.concatenate([query_ref[s, n] for s in range(steps)], axis=0)
        scores = (
            lax.dot_general(
                queries, keys, (((1,), (1,)), ((), ())), preferred_element_type=jnp.float32
            )
            * softmax_scale
        )
        position = lax.broadcasted_iota(jnp.int32, scores.shape, 1)
        step = lax.broadcasted_iota(jnp.int32, scores.shape, 0) // heads
        valid = (position < lengths_ref[n]) | (
            (position >= slots) & (position - slots <= step)
        )
        scores = jnp.where(valid, scores, masked_score)
        terms = jnp.exp(scores - jnp.max(scores, axis=1, keepdims=True))
        terms = jnp.where(valid, terms, 0.0)
        probs = (terms / jnp.sum(terms, axis=1, keepdims=True)).astype(jnp.bfloat16)
        mixed = jnp.dot(probs, keys[:, :KV], preferred_element_type=jnp.float32)
        for s in range(steps):
            out_ref[s, n] = mixed[s * heads : (s + 1) * heads].astype(jnp.bfloat16)


def attend(query, cache, lengths, fresh):
    steps, tokens, heads, width = query.shape
    vmem = pl.BlockSpec(memory_space=pltpu.VMEM)
    return pl.pallas_call(
        attend_kernel,
        out_shape=[jax.ShapeDtypeStruct((steps, tokens, heads, KV), jnp.bfloat16), MARK],
        in_specs=[pl.BlockSpec(memory_space=pltpu.SMEM)] + [vmem] * 3,
        out_specs=[vmem] * 2,
        compiler_params=pltpu.CompilerParams(vmem_limit_bytes=12 << 20),
        cost_estimate=pl.CostEstimate(
            flops=4 * steps * tokens * heads * 128 * width,
            bytes_accessed=2 * (2 * query.size + cache.size),
            transcendentals=steps * tokens * heads * 128,
        ),
        name="attention",
    )(lengths, query, cache, fresh)


def load_kernel(gate_ref, up_ref, down_ref, _, gate_v, up_v, down_v, mark_ref, sems):
    copies = [
        pltpu.make_async_copy(source, target, sems.at[i])
        for i, (source, target) in enumerate(
            ((gate_ref, gate_v), (up_ref, up_v), (down_ref, down_v))
        )
    ]
    for copy in copies:
        copy.start()
    mark_ref[...] = jnp.zeros(mark_ref.shape, mark_ref.dtype)
    for copy in copies:
        copy.wait()


def load(weights, earlier):
    vmem = pl.BlockSpec(memory_space=pltpu.VMEM)
    anywhere = pl.BlockSpec(memory_space=pl.ANY)
    *held, mark = pl.pallas_call(
        load_kernel,
        out_shape=[jax.ShapeDtypeStruct(w.shape, w.dtype) for w in weights] + [MARK],
        in_specs=[anywhere] * 4,
        out_specs=[vmem] * 4,
        scratch_shapes=[pltpu.SemaphoreType.DMA((3,))],
        compiler_params=pltpu.CompilerParams(vmem_limit_bytes=40 << 20),
        name="load",
    )(*weights, earlier)
    return held, mark


def expert_kernel(count, *refs):
    part_refs, refs = refs[:count], refs[count:]
    gate_ref, up_ref, down_ref, _, *out_refs, mark_ref, rows_v = refs
    size = out_refs[0].shape[0]
    step = rows_v.shape[1] // EXPERT_PARTS
    rows = part_refs[0].shape[0]
    for i, ref in enumerate(part_refs):
        rows_v[i * rows : (i + 1) * rows, :] = ref[...]
    mark_ref[...] = jnp.zeros(mark_ref.shape, mark_ref.dtype)
    gate, upper = 0.0, 0.0
    for i in range(EXPERT_PARTS):
        ds = pl.ds(i * step, step)
        x = rows_v[:, ds]
        gate = gate + jnp.dot(x, gate_ref[ds, :], preferred_element_type=jnp.float32)
        upper = upper + jnp.dot(x, up_ref[ds, :], preferred_element_type=jnp.float32)
    inner = (gate / (1.0 + jnp.exp(-gate)) * upper).astype(jnp.bfloat16)
    for i in range(EXPERT_PARTS):
        ds = pl.ds(i * step, step)
        partial = jnp.dot(inner, down_ref[:, ds], preferred_element_type=jnp.float32)
        for j, ref in enumerate(out_refs):
            ref[:, ds] = partial[j * size : (j + 1) * size].astype(jnp.bfloat16)


def experts(parts, weights, earlier, size):
    rows, depth = parts[0].shape
    count = len(parts)
    outs = count * rows // size
    vmem = pl.BlockSpec(memory_space=pltpu.VMEM)
    out = pl.pallas_call(
        functools.partial(expert_kernel, count),
        out_shape=[jax.ShapeDtypeStruct((size, depth), jnp.bfloat16)] * outs + [MARK],
        in_specs=[vmem] * (count + 3) + [pl.BlockSpec(memory_space=pl.ANY)],
        out_specs=[vmem] * (outs + 1),
        scratch_shapes=[pltpu.VMEM((count * rows, depth), jnp.bfloat16)],
        compiler_params=pltpu.CompilerParams(
            vmem_limit_bytes=(16 << 20) + count * rows * depth * 8
        ),
        name="experts",
    )(*parts, *weights, earlier)
    return out[:outs], out[outs]


def join_kernel(count, *refs):
    out_ref = refs[-1]
    rows, depth = out_ref.shape
    step = depth // EXPERT_PARTS
    for i in range(EXPERT_PARTS):
        ds = pl.ds(i * step, step)
        joined = jnp.concatenate([ref[:, ds].astype(jnp.float32) for ref in refs[:count]], axis=0)
        out_ref[:, ds] = joined.astype(jnp.bfloat16)


def join(parts, earlier):
    depth = parts[0].shape[1]
    rows = sum(part.shape[0] for part in parts)
    vmem = pl.BlockSpec(memory_space=pltpu.VMEM)
    return pl.pallas_call(
        functools.partial(join_kernel, len(parts)),
        out_shape=jax.ShapeDtypeStruct((rows, depth), jnp.bfloat16),
        in_specs=[vmem] * len(parts) + [pl.BlockSpec(memory_space=pl.ANY)] * len(earlier),
        out_specs=vmem,
        compiler_params=pltpu.CompilerParams(vmem_limit_bytes=(2 << 20) + 8 * rows * depth),
        name="join",
    )(*parts, *earlier)


def after_kernel(value_ref, earlier_ref, out_ref):
    out_ref[...] = value_ref[...]


def after(value, earlier):
    vmem = pl.BlockSpec(memory_space=pltpu.VMEM)
    return pl.pallas_call(
        after_kernel,
        out_shape=jax.ShapeDtypeStruct(value.shape, value.dtype),
        in_specs=[vmem, pl.BlockSpec(memory_space=pl.ANY)],
        out_specs=vmem,
        compiler_params=pltpu.CompilerParams(vmem_limit_bytes=(2 << 20) + 6 * value.size),
        name="after",
    )(value, earlier)


def add_kernel(count, messages, *refs):
    terms, part_refs = refs[:count], refs[-messages:]
    depth = terms[0].shape[1]
    size = part_refs[0].shape[0]
    step = depth // EXPERT_PARTS
    for i in range(EXPERT_PARTS):
        ds = pl.ds(i * step, step)
        total = terms[0][:, ds].astype(jnp.float32)
        for ref in terms[1:]:
            total = total + ref[:, ds].astype(jnp.float32)
        for m, ref in enumerate(part_refs):
            ref[:, ds] = total[m * size : (m + 1) * size].astype(jnp.bfloat16)


def add(terms, messages, earlier):
    rows, depth = terms[0].shape
    vmem = pl.BlockSpec(memory_space=pltpu.VMEM)
    return pl.pallas_call(
        functools.partial(add_kernel, len(terms), messages),
        out_shape=[jax.ShapeDtypeStruct((rows // messages, depth), jnp.bfloat16)] * messages,
        in_specs=[vmem] * len(terms) + [pl.BlockSpec(memory_space=pl.ANY)] * len(earlier),
        out_specs=[vmem] * messages,
        compiler_params=pltpu.CompilerParams(vmem_limit_bytes=(4 << 20) + 16 * rows * depth),
        name="add",
    )(*terms, *earlier)


def pack_kernel(
    slots,
    deltas,
    table_ref,
    ids_ref,
    replica_ref,
    other_ids_ref,
    other_replica_ref,
    raw_ref,
    other_ref,
    gain_ref,
    normed_ref,
    place_ref,
    choose_ref,
    *refs,
):
    message_refs, raw_v = refs[:-1], refs[-1]
    steps, tokens, depth = raw_ref.shape
    top = ids_ref.shape[1]
    index = lax.axis_index("ep")
    core = lax.rem(index, 2)
    group = lax.div(index, SPAN)
    message_rows = 2 * steps * slots
    for b, ref in enumerate((raw_ref, other_ref)):
        for s in range(steps):
            at = (b * steps + s) * tokens
            raw_v[at : at + tokens, :] = ref[s].astype(jnp.float32)
    raw = raw_v[...]
    mean_square = jnp.mean(raw * raw, axis=1, keepdims=True)
    normed = (raw * lax.rsqrt(mean_square + norm_eps) * gain_ref[...]).astype(jnp.bfloat16)
    normed_ref[...] = normed

    row = lax.broadcasted_iota(jnp.int32, place_ref.shape[1:], 0)
    column = lax.broadcasted_iota(jnp.int32, place_ref.shape[1:], 1)
    expert = lax.broadcasted_iota(jnp.int32, choose_ref.shape[1:], 0)
    token = lax.broadcasted_iota(jnp.int32, choose_ref.shape[1:], 1)
    message = row // message_rows
    target = sum(
        [
            jnp.where(message == m, jnp.where(core == 0, low, high) - m, 0)
            for m, (low, high) in enumerate(deltas)
        ],
        message,
    )
    row = target * message_rows + row % message_rows
    place_row = [jnp.full(place_ref.shape[1:], -1, jnp.int32) for _ in range(top)]
    choice = [jnp.full(choose_ref.shape[1:], -1, jnp.int32) for _ in range(top)]
    for b, (ids, replicas) in enumerate(
        ((ids_ref, replica_ref), (other_ids_ref, other_replica_ref))
    ):
        for s in range(steps):
            block = b * steps + s
            earlier = []
            for t in range(tokens):
                for k in range(top):
                    copy = table_ref[replicas[s, k, t], ids[s, k, t]]
                    slot = sum([(copy == c).astype(jnp.int32) for c in earlier], jnp.int32(0))
                    earlier.append(copy)
                    delta = copy ^ group
                    at = delta * message_rows + block * slots + slot
                    at = jnp.where(slot < slots, at, -1)
                    here = block * tokens + t
                    place_row[k] = jnp.where(column == here, at, place_row[k])
                    choice[k] = jnp.where(token == here, ids[s, k, t], choice[k])
    total = jnp.zeros(place_ref.shape[1:], jnp.float32)
    for k in range(top):
        hit = (place_row[k] == row).astype(jnp.float32)
        place_ref[k] = hit
        choose_ref[k] = (choice[k] == expert).astype(jnp.float32)
        total = total + hit
    packed = jnp.dot(total.astype(jnp.bfloat16), normed, preferred_element_type=jnp.float32)
    for m, ref in enumerate(message_refs):
        ref[...] = packed[m * message_rows : (m + 1) * message_rows].astype(jnp.bfloat16)


def pack(slots, deltas, hidden, other, gain, copy_table, own_choice, other_choice, experts_total):
    steps, tokens, depth = hidden.shape
    top = own_choice[0].shape[1]
    messages = len(deltas)
    message_rows = 2 * steps * slots
    columns = 2 * steps * tokens
    vmem = pl.BlockSpec(memory_space=pltpu.VMEM)
    smem = pl.BlockSpec(memory_space=pltpu.SMEM)
    shape = jax.ShapeDtypeStruct
    out = pl.pallas_call(
        functools.partial(pack_kernel, slots, deltas),
        out_shape=[
            shape((columns, depth), jnp.bfloat16),
            shape((top, messages * message_rows, columns), jnp.float32),
            shape((top, experts_total, columns), jnp.float32),
        ]
        + [shape((message_rows, depth), jnp.bfloat16)] * messages,
        in_specs=[smem] * 5 + [vmem] * 3,
        out_specs=[vmem] * (3 + messages),
        scratch_shapes=[pltpu.VMEM((columns, depth), jnp.float32)],
        compiler_params=pltpu.CompilerParams(
            vmem_limit_bytes=62 << 20
        ),
        name="pack",
    )(copy_table, *own_choice, *other_choice, hidden, other, gain)
    return out[0], out[1], out[2], out[3:]


def weigh_kernel(normed_ref, router_ref, place_ref, choose_ref, weigh_ref):
    scores = jax.nn.sigmoid(
        lax.dot_general(
            router_ref[...],
            normed_ref[...],
            (((1,), (1,)), ((), ())),
            preferred_element_type=jnp.float32,
        )
    )
    top = place_ref.shape[0]
    picked = [jnp.sum(choose_ref[k] * scores, axis=0, keepdims=True) for k in range(top)]
    total = sum(picked[1:], picked[0])
    weigh = jnp.zeros(weigh_ref.shape, jnp.float32)
    for k in range(top):
        weigh = weigh + place_ref[k] * (routed_scale * picked[k] / total)
    weigh_ref[...] = weigh


def weigh(normed, router_t, place, choose):
    vmem = pl.BlockSpec(memory_space=pltpu.VMEM)
    return pl.pallas_call(
        weigh_kernel,
        out_shape=jax.ShapeDtypeStruct(place.shape[1:], jnp.float32),
        in_specs=[vmem] * 4,
        out_specs=vmem,
        cost_estimate=pl.CostEstimate(
            flops=2 * normed.size * 256, bytes_accessed=2 * normed.size, transcendentals=256
        ),
        compiler_params=pltpu.CompilerParams(vmem_limit_bytes=4 << 20),
        name="weigh",
    )(normed, router_t, place, choose)


def weighted(weights, part_refs):
    high = weights.astype(jnp.bfloat16)
    left = weights - high.astype(jnp.float32)
    middle = left.astype(jnp.bfloat16)
    low = (left - middle.astype(jnp.float32)).astype(jnp.bfloat16)
    rows = jnp.concatenate([ref[...].astype(jnp.float32) for ref in part_refs], axis=0)
    rows = rows.astype(jnp.bfloat16)
    pieces = [
        lax.dot_general(w, rows, (((0,), (0,)), ((), ())), preferred_element_type=jnp.float32)
        for w in (high, middle, low)
    ]
    return pieces[0] + (pieces[1] + pieces[2])


def first_half_kernel(weigh_ref, *refs):
    part_refs, out_ref = refs[:-1], refs[-1]
    out_ref[...] = weighted(weigh_ref[: weigh_ref.shape[0] // 2, :], part_refs)


def second_half_kernel(weigh_ref, first_ref, *refs):
    part_refs, own_ref, send_ref = refs[:-2], refs[-2], refs[-1]
    result = first_ref[...] + weighted(weigh_ref[weigh_ref.shape[0] // 2 :, :], part_refs)
    half = own_ref.shape[0]
    own_ref[...] = result[:half]
    send_ref[...] = result[half:].astype(jnp.bfloat16)


def combine(weights, parts):
    depth = parts[0].shape[1]
    tokens = weights.shape[1]
    vmem = pl.BlockSpec(memory_space=pltpu.VMEM)
    params = pltpu.CompilerParams(vmem_limit_bytes=(8 << 20) + 8 * weights.shape[0] * depth)
    middle = len(parts) // 2
    first = pl.pallas_call(
        first_half_kernel,
        out_shape=jax.ShapeDtypeStruct((tokens, depth), jnp.float32),
        in_specs=[vmem] * (1 + middle),
        out_specs=vmem,
        compiler_params=params,
        name="combine",
    )(weights, *parts[:middle])
    return pl.pallas_call(
        second_half_kernel,
        out_shape=[
            jax.ShapeDtypeStruct((tokens // 2, depth), jnp.float32),
            jax.ShapeDtypeStruct((tokens // 2, depth), jnp.bfloat16),
        ],
        in_specs=[vmem] * (2 + len(parts) - middle),
        out_specs=[vmem] * 2,
        compiler_params=params,
        name="combine",
    )(weights, first, *parts[middle:])


def finish_kernel(own_ref, received_ref, out_ref):
    result = own_ref[...] + received_ref[...].astype(jnp.float32)
    steps, tokens, _ = out_ref.shape
    for s in range(steps):
        out_ref[s] = result[s * tokens : (s + 1) * tokens].astype(jnp.bfloat16)


def finish(own, received, shape):
    vmem = pl.BlockSpec(memory_space=pltpu.VMEM)
    return pl.pallas_call(
        finish_kernel,
        out_shape=jax.ShapeDtypeStruct(shape, jnp.bfloat16),
        in_specs=[vmem] * 2,
        out_specs=vmem,
        compiler_params=pltpu.CompilerParams(vmem_limit_bytes=4 << 20),
        name="finish",
    )(own, received)


def mixture(
    hidden, norm_gain, router, expert_ids, replica, copy_table, gate_w, up_w, down_w, attended_mark
):
    groups = lax.axis_size("ep") // SPAN
    messages = groups // 2
    tokens = hidden.shape[1]
    slots = max(2, 2 * tokens * expert_ids.shape[2] // groups)
    deltas = lanes(groups)

    def swapped(value):
        return flipped(value, 1, 1)

    own_choice = (expert_ids.transpose(0, 2, 1), replica.transpose(0, 2, 1))
    other_choice = (swapped(own_choice[0]), swapped(own_choice[1]))
    normed, place, choose, packed = pack(
        slots,
        deltas,
        hidden,
        swapped(hidden),
        norm_gain[None, :],
        copy_table.T,
        own_choice,
        other_choice,
        router.shape[1],
    )

    def rounds(parts):
        return [
            flipped(part, SPAN * low, SPAN * high) for part, (low, high) in zip(parts, deltas)
        ]

    weights = weigh(normed, router.T, place, choose)
    expert_weights = (gate_w, up_w, down_w)
    half = messages // 2
    size = packed[0].shape[0]
    received = rounds(packed)
    held, mark = load(expert_weights, place)
    near = join(received, [mark])
    far = flipped(near, 2, 2)
    near_out, mark = experts([near, swapped(near)], held, mark, half * size)
    far_out, mark = experts([far, swapped(after(far, mark))], held, mark, half * size)
    (far_sum_a,) = add([far_out[0], swapped(far_out[2])], 1, [])
    (far_sum_b,) = add([far_out[1], swapped(far_out[3])], 1, [])
    total_a = add(
        [near_out[0], swapped(near_out[2]), flipped(far_sum_a, 2, 2)],
        half,
        [mark, weights, attended_mark],
    )
    total_b = add([near_out[1], swapped(near_out[3]), flipped(far_sum_b, 2, 2)], half, [total_a[0]])
    returned = rounds([*total_a, *total_b])
    own, send = combine(weights, returned)
    return finish(own, swapped(send), hidden.shape)


def per_device(
    hidden,
    norm_gain,
    router,
    expert_ids,
    replica,
    copy_table,
    gate_w,
    up_w,
    down_w,
    query,
    cache,
    lengths,
    fresh_kv,
):
    attended, attended_mark = attend(query, cache, lengths, fresh_kv)
    moe_out = mixture(
        hidden,
        norm_gain,
        router,
        expert_ids,
        replica,
        copy_table,
        gate_w,
        up_w,
        down_w,
        attended_mark,
    )
    return (attended, moe_out)


def solution(mesh):
    return jax.shard_map(
        per_device,
        mesh=mesh,
        in_specs=(
            P(None, ("groups", "ep"), None),
            P(),
            P(),
            P(None, ("groups", "ep"), None),
            P(None, ("groups", "ep"), None),
            P(),
            P(None, "ep"),
            P(None, "ep"),
            P("ep", None),
            P(None, ("groups", "ep"), None, None),
            P(("groups", "ep"), None, None),
            P(("groups", "ep")),
            P(None, ("groups", "ep"), None),
        ),
        out_specs=(P(None, ("groups", "ep"), None, None), P(None, ("groups", "ep"), None)),
        check_vma=False,
    )
```

```python
import functools

import jax
import jax.numpy as jnp
from jax import lax
from jax.experimental import pallas as pl
from jax.experimental.pallas import tpu as pltpu
from jax.sharding import PartitionSpec as P

KV = 512
SPAN = 4

softmax_scale = 192.0 ** (-0.5)
routed_scale = 2.5
norm_eps = 1e-06
masked_score = -1e30
EXPERT_PARTS = 7
MARK = jax.ShapeDtypeStruct((8, 128), jnp.float32)


def flipped(value, low_core, high_core):
    pairs = [(e, e ^ (high_core if e % 2 else low_core)) for e in range(lax.axis_size("ep"))]
    return lax.ppermute(value, "ep", pairs)


def lanes(groups):
    hops = [(d & 1) + (d >> 1) for d in range(groups)]
    chosen = ([], [])
    for d in sorted(range(groups), key=lambda d: (-hops[d], -d)):
        sums = [sum(hops[e] for e in lane) for lane in chosen]
        lane = 0 if sums[0] <= sums[1] else 1
        if 2 * len(chosen[lane]) == groups:
            lane = 1 - lane
        chosen[lane].append(d)
    return list(zip(*chosen))


def attend_kernel(lengths_ref, query_ref, cache_ref, fresh_ref, out_ref, mark_ref):
    mark_ref[...] = jnp.zeros(mark_ref.shape, mark_ref.dtype)
    steps, tokens, heads, _ = query_ref.shape
    slots = cache_ref.shape[1]
    pad = 128 - slots
    for n in range(tokens):
        row = lax.broadcasted_iota(jnp.int32, (pad, 1), 0)
        extra = jnp.zeros((pad, fresh_ref.shape[2]), jnp.float32)
        for s in range(steps):
            block = fresh_ref[s].astype(jnp.float32)
            which = lax.broadcasted_iota(jnp.int32, block.shape, 0) == n
            one = jnp.sum(jnp.where(which, block, 0.0), axis=0, keepdims=True)
            extra = jnp.where(row == s, one, extra)
        keys = jnp.concatenate([cache_ref[n], extra.astype(jnp.bfloat16)], axis=0)
        queries = jnp.concatenate([query_ref[s, n] for s in range(steps)], axis=0)
        scores = (
            lax.dot_general(
                queries, keys, (((1,), (1,)), ((), ())), preferred_element_type=jnp.float32
            )
            * softmax_scale
        )
        position = lax.broadcasted_iota(jnp.int32, scores.shape, 1)
        step = lax.broadcasted_iota(jnp.int32, scores.shape, 0) // heads
        valid = (position < lengths_ref[n]) | (
            (position >= slots) & (position - slots <= step)
        )
        scores = jnp.where(valid, scores, masked_score)
        terms = jnp.exp(scores - jnp.max(scores, axis=1, keepdims=True))
        terms = jnp.where(valid, terms, 0.0)
        probs = (terms / jnp.sum(terms, axis=1, keepdims=True)).astype(jnp.bfloat16)
        mixed = jnp.dot(probs, keys[:, :KV], preferred_element_type=jnp.float32)
        for s in range(steps):
            out_ref[s, n] = mixed[s * heads : (s + 1) * heads].astype(jnp.bfloat16)


def attend(query, cache, lengths, fresh):
    steps, tokens, heads, width = query.shape
    vmem = pl.BlockSpec(memory_space=pltpu.VMEM)
    return pl.pallas_call(
        attend_kernel,
        out_shape=[jax.ShapeDtypeStruct((steps, tokens, heads, KV), jnp.bfloat16), MARK],
        in_specs=[pl.BlockSpec(memory_space=pltpu.SMEM)] + [vmem] * 3,
        out_specs=[vmem] * 2,
        compiler_params=pltpu.CompilerParams(vmem_limit_bytes=12 << 20),
        cost_estimate=pl.CostEstimate(
            flops=4 * steps * tokens * heads * 128 * width,
            bytes_accessed=2 * (2 * query.size + cache.size),
            transcendentals=steps * tokens * heads * 128,
        ),
        name="attention",
    )(lengths, query, cache, fresh)


def load_kernel(gate_ref, up_ref, down_ref, _, gate_v, up_v, down_v, mark_ref, sems):
    copies = [
        pltpu.make_async_copy(source, target, sems.at[i])
        for i, (source, target) in enumerate(
            ((gate_ref, gate_v), (up_ref, up_v), (down_ref, down_v))
        )
    ]
    for copy in copies:
        copy.start()
    mark_ref[...] = jnp.zeros(mark_ref.shape, mark_ref.dtype)
    for copy in copies:
        copy.wait()


def load(weights, earlier):
    vmem = pl.BlockSpec(memory_space=pltpu.VMEM)
    anywhere = pl.BlockSpec(memory_space=pl.ANY)
    *held, mark = pl.pallas_call(
        load_kernel,
        out_shape=[jax.ShapeDtypeStruct(w.shape, w.dtype) for w in weights] + [MARK],
        in_specs=[anywhere] * 4,
        out_specs=[vmem] * 4,
        scratch_shapes=[pltpu.SemaphoreType.DMA((3,))],
        compiler_params=pltpu.CompilerParams(vmem_limit_bytes=40 << 20),
        name="load",
    )(*weights, earlier)
    return held, mark


def expert_kernel(count, *refs):
    part_refs, refs = refs[:count], refs[count:]
    gate_ref, up_ref, down_ref, _, *out_refs, mark_ref, rows_v = refs
    size = out_refs[0].shape[0]
    step = rows_v.shape[1] // EXPERT_PARTS
    rows = part_refs[0].shape[0]
    for i, ref in enumerate(part_refs):
        rows_v[i * rows : (i + 1) * rows, :] = ref[...]
    mark_ref[...] = jnp.zeros(mark_ref.shape, mark_ref.dtype)
    gate, upper = 0.0, 0.0
    for i in range(EXPERT_PARTS):
        ds = pl.ds(i * step, step)
        x = rows_v[:, ds]
        gate = gate + jnp.dot(x, gate_ref[ds, :], preferred_element_type=jnp.float32)
        upper = upper + jnp.dot(x, up_ref[ds, :], preferred_element_type=jnp.float32)
    inner = (gate / (1.0 + jnp.exp(-gate)) * upper).astype(jnp.bfloat16)
    for i in range(EXPERT_PARTS):
        ds = pl.ds(i * step, step)
        partial = jnp.dot(inner, down_ref[:, ds], preferred_element_type=jnp.float32)
        for j, ref in enumerate(out_refs):
            ref[:, ds] = partial[j * size : (j + 1) * size].astype(jnp.bfloat16)


def experts(parts, weights, earlier, size):
    rows, depth = parts[0].shape
    count = len(parts)
    outs = count * rows // size
    vmem = pl.BlockSpec(memory_space=pltpu.VMEM)
    out = pl.pallas_call(
        functools.partial(expert_kernel, count),
        out_shape=[jax.ShapeDtypeStruct((size, depth), jnp.bfloat16)] * outs + [MARK],
        in_specs=[vmem] * (count + 3) + [pl.BlockSpec(memory_space=pl.ANY)],
        out_specs=[vmem] * (outs + 1),
        scratch_shapes=[pltpu.VMEM((count * rows, depth), jnp.bfloat16)],
        compiler_params=pltpu.CompilerParams(
            vmem_limit_bytes=(16 << 20) + count * rows * depth * 8
        ),
        name="experts",
    )(*parts, *weights, earlier)
    return out[:outs], out[outs]


def join_kernel(count, *refs):
    out_ref = refs[-1]
    rows, depth = out_ref.shape
    step = depth // EXPERT_PARTS
    for i in range(EXPERT_PARTS):
        ds = pl.ds(i * step, step)
        joined = jnp.concatenate([ref[:, ds].astype(jnp.float32) for ref in refs[:count]], axis=0)
        out_ref[:, ds] = joined.astype(jnp.bfloat16)


def join(parts, earlier):
    depth = parts[0].shape[1]
    rows = sum(part.shape[0] for part in parts)
    vmem = pl.BlockSpec(memory_space=pltpu.VMEM)
    return pl.pallas_call(
        functools.partial(join_kernel, len(parts)),
        out_shape=jax.ShapeDtypeStruct((rows, depth), jnp.bfloat16),
        in_specs=[vmem] * len(parts) + [pl.BlockSpec(memory_space=pl.ANY)] * len(earlier),
        out_specs=vmem,
        compiler_params=pltpu.CompilerParams(vmem_limit_bytes=(2 << 20) + 8 * rows * depth),
        name="join",
    )(*parts, *earlier)


def after_kernel(pieces, value_ref, *refs):
    out_refs = refs[-pieces:]
    rows = out_refs[0].shape[0]
    for i, ref in enumerate(out_refs):
        ref[...] = value_ref[i * rows : (i + 1) * rows, :]


def after(value, earlier, pieces):
    rows, depth = value.shape
    vmem = pl.BlockSpec(memory_space=pltpu.VMEM)
    return pl.pallas_call(
        functools.partial(after_kernel, pieces),
        out_shape=[jax.ShapeDtypeStruct((rows // pieces, depth), value.dtype)] * pieces,
        in_specs=[vmem] + [pl.BlockSpec(memory_space=pl.ANY)] * len(earlier),
        out_specs=[vmem] * pieces,
        compiler_params=pltpu.CompilerParams(vmem_limit_bytes=(2 << 20) + 6 * value.size),
        name="after",
    )(value, *earlier)


def add_kernel(count, messages, *refs):
    terms, part_refs = refs[:count], refs[-messages:]
    depth = terms[0].shape[1]
    size = part_refs[0].shape[0]
    step = depth // EXPERT_PARTS
    for i in range(EXPERT_PARTS):
        ds = pl.ds(i * step, step)
        total = terms[0][:, ds].astype(jnp.float32)
        for ref in terms[1:]:
            total = total + ref[:, ds].astype(jnp.float32)
        for m, ref in enumerate(part_refs):
            ref[:, ds] = total[m * size : (m + 1) * size].astype(ref.dtype)


def add(terms, messages, earlier, kind=jnp.bfloat16):
    rows, depth = terms[0].shape
    vmem = pl.BlockSpec(memory_space=pltpu.VMEM)
    return pl.pallas_call(
        functools.partial(add_kernel, len(terms), messages),
        out_shape=[jax.ShapeDtypeStruct((rows // messages, depth), kind)] * messages,
        in_specs=[vmem] * len(terms) + [pl.BlockSpec(memory_space=pl.ANY)] * len(earlier),
        out_specs=[vmem] * messages,
        compiler_params=pltpu.CompilerParams(vmem_limit_bytes=(4 << 20) + 16 * rows * depth),
        name="add",
    )(*terms, *earlier)


def pack_kernel(
    slots,
    deltas,
    table_ref,
    ids_ref,
    replica_ref,
    other_ids_ref,
    other_replica_ref,
    raw_ref,
    other_ref,
    gain_ref,
    normed_ref,
    place_ref,
    choose_ref,
    *refs,
):
    message_refs, raw_v = refs[:-1], refs[-1]
    steps, tokens, depth = raw_ref.shape
    top = ids_ref.shape[1]
    index = lax.axis_index("ep")
    core = lax.rem(index, 2)
    group = lax.div(index, SPAN)
    message_rows = 2 * steps * slots
    for b, ref in enumerate((raw_ref, other_ref)):
        for s in range(steps):
            at = (b * steps + s) * tokens
            raw_v[at : at + tokens, :] = ref[s].astype(jnp.float32)
    raw = raw_v[...]
    mean_square = jnp.mean(raw * raw, axis=1, keepdims=True)
    normed = (raw * lax.rsqrt(mean_square + norm_eps) * gain_ref[...]).astype(jnp.bfloat16)
    normed_ref[...] = normed

    row = lax.broadcasted_iota(jnp.int32, place_ref.shape[1:], 0)
    column = lax.broadcasted_iota(jnp.int32, place_ref.shape[1:], 1)
    expert = lax.broadcasted_iota(jnp.int32, choose_ref.shape[1:], 0)
    token = lax.broadcasted_iota(jnp.int32, choose_ref.shape[1:], 1)
    message = row // message_rows
    target = sum(
        [
            jnp.where(message == m, jnp.where(core == 0, low, high) - m, 0)
            for m, (low, high) in enumerate(deltas)
        ],
        message,
    )
    row = target * message_rows + row % message_rows
    place_row = [jnp.full(place_ref.shape[1:], -1, jnp.int32) for _ in range(top)]
    choice = [jnp.full(choose_ref.shape[1:], -1, jnp.int32) for _ in range(top)]
    for b, (ids, replicas) in enumerate(
        ((ids_ref, replica_ref), (other_ids_ref, other_replica_ref))
    ):
        for s in range(steps):
            block = b * steps + s
            earlier = []
            for t in range(tokens):
                for k in range(top):
                    copy = table_ref[replicas[s, k, t], ids[s, k, t]]
                    slot = sum([(copy == c).astype(jnp.int32) for c in earlier], jnp.int32(0))
                    earlier.append(copy)
                    delta = copy ^ group
                    at = delta * message_rows + block * slots + slot
                    at = jnp.where(slot < slots, at, -1)
                    here = block * tokens + t
                    place_row[k] = jnp.where(column == here, at, place_row[k])
                    choice[k] = jnp.where(token == here, ids[s, k, t], choice[k])
    total = jnp.zeros(place_ref.shape[1:], jnp.float32)
    for k in range(top):
        hit = (place_row[k] == row).astype(jnp.float32)
        place_ref[k] = hit
        choose_ref[k] = (choice[k] == expert).astype(jnp.float32)
        total = total + hit
    packed = jnp.dot(total.astype(jnp.bfloat16), normed, preferred_element_type=jnp.float32)
    for m, ref in enumerate(message_refs):
        ref[...] = packed[m * message_rows : (m + 1) * message_rows].astype(jnp.bfloat16)


def pack(slots, deltas, hidden, other, gain, copy_table, own_choice, other_choice, experts_total):
    steps, tokens, depth = hidden.shape
    top = own_choice[0].shape[1]
    messages = len(deltas)
    message_rows = 2 * steps * slots
    columns = 2 * steps * tokens
    vmem = pl.BlockSpec(memory_space=pltpu.VMEM)
    smem = pl.BlockSpec(memory_space=pltpu.SMEM)
    shape = jax.ShapeDtypeStruct
    out = pl.pallas_call(
        functools.partial(pack_kernel, slots, deltas),
        out_shape=[
            shape((columns, depth), jnp.bfloat16),
            shape((top, messages * message_rows, columns), jnp.float32),
            shape((top, experts_total, columns), jnp.float32),
        ]
        + [shape((message_rows, depth), jnp.bfloat16)] * messages,
        in_specs=[smem] * 5 + [vmem] * 3,
        out_specs=[vmem] * (3 + messages),
        scratch_shapes=[pltpu.VMEM((columns, depth), jnp.float32)],
        compiler_params=pltpu.CompilerParams(
            vmem_limit_bytes=62 << 20
        ),
        name="pack",
    )(copy_table, *own_choice, *other_choice, hidden, other, gain)
    return out[0], out[1], out[2], out[3:]


def weigh_kernel(normed_ref, router_ref, place_ref, choose_ref, weigh_ref):
    scores = jax.nn.sigmoid(
        lax.dot_general(
            router_ref[...],
            normed_ref[...],
            (((1,), (1,)), ((), ())),
            preferred_element_type=jnp.float32,
        )
    )
    top = place_ref.shape[0]
    picked = [jnp.sum(choose_ref[k] * scores, axis=0, keepdims=True) for k in range(top)]
    total = sum(picked[1:], picked[0])
    weigh = jnp.zeros(weigh_ref.shape, jnp.float32)
    for k in range(top):
        weigh = weigh + place_ref[k] * (routed_scale * picked[k] / total)
    weigh_ref[...] = weigh


def weigh(normed, router_t, place, choose):
    vmem = pl.BlockSpec(memory_space=pltpu.VMEM)
    return pl.pallas_call(
        weigh_kernel,
        out_shape=jax.ShapeDtypeStruct(place.shape[1:], jnp.float32),
        in_specs=[vmem] * 4,
        out_specs=vmem,
        cost_estimate=pl.CostEstimate(
            flops=2 * normed.size * 256, bytes_accessed=2 * normed.size, transcendentals=256
        ),
        compiler_params=pltpu.CompilerParams(vmem_limit_bytes=4 << 20),
        name="weigh",
    )(normed, router_t, place, choose)


def weighted(weights, part_refs):
    high = weights.astype(jnp.bfloat16)
    left = weights - high.astype(jnp.float32)
    middle = left.astype(jnp.bfloat16)
    low = (left - middle.astype(jnp.float32)).astype(jnp.bfloat16)
    rows = jnp.concatenate([ref[...].astype(jnp.float32) for ref in part_refs], axis=0)
    rows = rows.astype(jnp.bfloat16)
    pieces = [
        lax.dot_general(w, rows, (((0,), (0,)), ((), ())), preferred_element_type=jnp.float32)
        for w in (high, middle, low)
    ]
    return pieces[0] + (pieces[1] + pieces[2])


def first_half_kernel(weigh_ref, *refs):
    part_refs, out_ref = refs[:-1], refs[-1]
    out_ref[...] = weighted(weigh_ref[: weigh_ref.shape[0] // 2, :], part_refs)


def second_half_kernel(weigh_ref, first_ref, *refs):
    part_refs, own_ref, send_ref = refs[:-2], refs[-2], refs[-1]
    result = first_ref[...] + weighted(weigh_ref[weigh_ref.shape[0] // 2 :, :], part_refs)
    half = own_ref.shape[0]
    own_ref[...] = result[:half]
    send_ref[...] = result[half:].astype(jnp.bfloat16)


def combine(weights, parts):
    depth = parts[0].shape[1]
    tokens = weights.shape[1]
    vmem = pl.BlockSpec(memory_space=pltpu.VMEM)
    params = pltpu.CompilerParams(vmem_limit_bytes=(8 << 20) + 8 * weights.shape[0] * depth)
    middle = len(parts) // 2
    first = pl.pallas_call(
        first_half_kernel,
        out_shape=jax.ShapeDtypeStruct((tokens, depth), jnp.float32),
        in_specs=[vmem] * (1 + middle),
        out_specs=vmem,
        compiler_params=params,
        name="combine",
    )(weights, *parts[:middle])
    return pl.pallas_call(
        second_half_kernel,
        out_shape=[
            jax.ShapeDtypeStruct((tokens // 2, depth), jnp.float32),
            jax.ShapeDtypeStruct((tokens // 2, depth), jnp.bfloat16),
        ],
        in_specs=[vmem] * (2 + len(parts) - middle),
        out_specs=[vmem] * 2,
        compiler_params=params,
        name="combine",
    )(weights, first, *parts[middle:])


def finish_kernel(own_ref, received_ref, out_ref):
    result = own_ref[...] + received_ref[...].astype(jnp.float32)
    steps, tokens, _ = out_ref.shape
    for s in range(steps):
        out_ref[s] = result[s * tokens : (s + 1) * tokens].astype(jnp.bfloat16)


def finish(own, received, shape):
    vmem = pl.BlockSpec(memory_space=pltpu.VMEM)
    return pl.pallas_call(
        finish_kernel,
        out_shape=jax.ShapeDtypeStruct(shape, jnp.bfloat16),
        in_specs=[vmem] * 2,
        out_specs=vmem,
        compiler_params=pltpu.CompilerParams(vmem_limit_bytes=4 << 20),
        name="finish",
    )(own, received)


def mixture(
    hidden, norm_gain, router, expert_ids, replica, copy_table, gate_w, up_w, down_w, attended_mark
):
    groups = lax.axis_size("ep") // SPAN
    messages = groups // 2
    tokens = hidden.shape[1]
    slots = max(2, 2 * tokens * expert_ids.shape[2] // groups)
    deltas = lanes(groups)

    def swapped(value):
        return flipped(value, 1, 1)

    own_choice = (expert_ids.transpose(0, 2, 1), replica.transpose(0, 2, 1))
    other_choice = (swapped(own_choice[0]), swapped(own_choice[1]))
    normed, place, choose, packed = pack(
        slots,
        deltas,
        hidden,
        swapped(hidden),
        norm_gain[None, :],
        copy_table.T,
        own_choice,
        other_choice,
        router.shape[1],
    )

    def rounds(parts):
        return [
            flipped(part, SPAN * low, SPAN * high) for part, (low, high) in zip(parts, deltas)
        ]

    weights = weigh(normed, router.T, place, choose)
    expert_weights = (gate_w, up_w, down_w)
    half = messages // 2
    size = packed[0].shape[0]
    received = rounds(packed)
    held, mark = load(expert_weights, place)
    near = join(received, [mark])
    far = flipped(near, 2, 2)
    near_out, mark = experts([near, swapped(near)], held, mark, half * size)
    (far_next,) = after(far, [mark, weights, attended_mark], 1)
    far_out, mark = experts([far, swapped(far_next)], held, mark, half * size)
    far_a_out, far_b_out = far_out[::2], far_out[1::2]
    far_sums = add([far_a_out[0], swapped(far_a_out[1])], half, [])
    far_sums += add([far_b_out[0], swapped(far_b_out[1])], half, [])
    near_sums = add([near_out[0], swapped(near_out[2])], half, [], jnp.float32)
    near_sums += add([near_out[1], swapped(near_out[3])], half, [], jnp.float32)
    totals = []
    earlier = [mark]
    for near_sum, far_sum in zip(near_sums, far_sums):
        totals += add([near_sum, flipped(far_sum, 2, 2)], messages // len(far_sums), earlier)
        earlier = totals[-1:]
    returned = rounds(totals)
    own, send = combine(weights, returned)
    return finish(own, swapped(send), hidden.shape)


def per_device(
    hidden,
    norm_gain,
    router,
    expert_ids,
    replica,
    copy_table,
    gate_w,
    up_w,
    down_w,
    query,
    cache,
    lengths,
    fresh_kv,
):
    attended, attended_mark = attend(query, cache, lengths, fresh_kv)
    moe_out = mixture(
        hidden,
        norm_gain,
        router,
        expert_ids,
        replica,
        copy_table,
        gate_w,
        up_w,
        down_w,
        attended_mark,
    )
    return (attended, moe_out)


def solution(mesh):
    return jax.shard_map(
        per_device,
        mesh=mesh,
        in_specs=(
            P(None, ("groups", "ep"), None),
            P(),
            P(),
            P(None, ("groups", "ep"), None),
            P(None, ("groups", "ep"), None),
            P(),
            P(None, "ep"),
            P(None, "ep"),
            P("ep", None),
            P(None, ("groups", "ep"), None, None),
            P(("groups", "ep"), None, None),
            P(("groups", "ep")),
            P(None, ("groups", "ep"), None),
        ),
        out_specs=(P(None, ("groups", "ep"), None, None), P(None, ("groups", "ep"), None)),
        check_vma=False,
    )
```

```python
import functools

import jax
import jax.numpy as jnp
from jax import lax
from jax.experimental import pallas as pl
from jax.experimental.pallas import tpu as pltpu
from jax.sharding import PartitionSpec as P

KV = 512
SPAN = 4

softmax_scale = 192.0 ** (-0.5)
routed_scale = 2.5
norm_eps = 1e-06
masked_score = -1e30
EXPERT_PARTS = 7
MARK = jax.ShapeDtypeStruct((8, 128), jnp.float32)


def flipped(value, low_core, high_core):
    pairs = [(e, e ^ (high_core if e % 2 else low_core)) for e in range(lax.axis_size("ep"))]
    return lax.ppermute(value, "ep", pairs)


def lanes(groups):
    hops = [(d & 1) + (d >> 1) for d in range(groups)]
    chosen = ([], [])
    for d in sorted(range(2, groups), key=lambda d: (-hops[d], -d)):
        sums = [sum(hops[e] for e in lane) for lane in chosen]
        lane = 0 if sums[0] <= sums[1] else 1
        if 2 * len(chosen[lane]) == groups - 2:
            lane = 1 - lane
        chosen[lane].append(d)
    return [*zip(*chosen), (0, 1)]


def attend_kernel(lengths_ref, query_ref, cache_ref, fresh_ref, out_ref, mark_ref):
    mark_ref[...] = jnp.zeros(mark_ref.shape, mark_ref.dtype)
    steps, tokens, heads, _ = query_ref.shape
    slots = cache_ref.shape[1]
    pad = 128 - slots
    for n in range(tokens):
        row = lax.broadcasted_iota(jnp.int32, (pad, 1), 0)
        extra = jnp.zeros((pad, fresh_ref.shape[2]), jnp.float32)
        for s in range(steps):
            block = fresh_ref[s].astype(jnp.float32)
            which = lax.broadcasted_iota(jnp.int32, block.shape, 0) == n
            one = jnp.sum(jnp.where(which, block, 0.0), axis=0, keepdims=True)
            extra = jnp.where(row == s, one, extra)
        keys = jnp.concatenate([cache_ref[n], extra.astype(jnp.bfloat16)], axis=0)
        queries = jnp.concatenate([query_ref[s, n] for s in range(steps)], axis=0)
        scores = (
            lax.dot_general(
                queries, keys, (((1,), (1,)), ((), ())), preferred_element_type=jnp.float32
            )
            * softmax_scale
        )
        position = lax.broadcasted_iota(jnp.int32, scores.shape, 1)
        step = lax.broadcasted_iota(jnp.int32, scores.shape, 0) // heads
        valid = (position < lengths_ref[n]) | (
            (position >= slots) & (position - slots <= step)
        )
        scores = jnp.where(valid, scores, masked_score)
        terms = jnp.exp(scores - jnp.max(scores, axis=1, keepdims=True))
        terms = jnp.where(valid, terms, 0.0)
        probs = (terms / jnp.sum(terms, axis=1, keepdims=True)).astype(jnp.bfloat16)
        mixed = jnp.dot(probs, keys[:, :KV], preferred_element_type=jnp.float32)
        for s in range(steps):
            out_ref[s, n] = mixed[s * heads : (s + 1) * heads].astype(jnp.bfloat16)


def attend(query, cache, lengths, fresh):
    steps, tokens, heads, width = query.shape
    vmem = pl.BlockSpec(memory_space=pltpu.VMEM)
    return pl.pallas_call(
        attend_kernel,
        out_shape=[jax.ShapeDtypeStruct((steps, tokens, heads, KV), jnp.bfloat16), MARK],
        in_specs=[pl.BlockSpec(memory_space=pltpu.SMEM)] + [vmem] * 3,
        out_specs=[vmem] * 2,
        compiler_params=pltpu.CompilerParams(vmem_limit_bytes=12 << 20),
        cost_estimate=pl.CostEstimate(
            flops=4 * steps * tokens * heads * 128 * width,
            bytes_accessed=2 * (2 * query.size + cache.size),
            transcendentals=steps * tokens * heads * 128,
        ),
        name="attention",
    )(lengths, query, cache, fresh)


def load_kernel(gate_ref, up_ref, down_ref, _, gate_v, up_v, down_v, mark_ref, sems):
    copies = [
        pltpu.make_async_copy(source, target, sems.at[i])
        for i, (source, target) in enumerate(
            ((gate_ref, gate_v), (up_ref, up_v), (down_ref, down_v))
        )
    ]
    for copy in copies:
        copy.start()
    mark_ref[...] = jnp.zeros(mark_ref.shape, mark_ref.dtype)
    for copy in copies:
        copy.wait()


def load(weights, earlier):
    vmem = pl.BlockSpec(memory_space=pltpu.VMEM)
    anywhere = pl.BlockSpec(memory_space=pl.ANY)
    *held, mark = pl.pallas_call(
        load_kernel,
        out_shape=[jax.ShapeDtypeStruct(w.shape, w.dtype) for w in weights] + [MARK],
        in_specs=[anywhere] * 4,
        out_specs=[vmem] * 4,
        scratch_shapes=[pltpu.SemaphoreType.DMA((3,))],
        compiler_params=pltpu.CompilerParams(vmem_limit_bytes=40 << 20),
        name="load",
    )(*weights, earlier)
    return held, mark


def expert_kernel(count, *refs):
    part_refs, refs = refs[:count], refs[count:]
    gate_ref, up_ref, down_ref, _, *out_refs, mark_ref, rows_v = refs
    size = out_refs[0].shape[0]
    step = rows_v.shape[1] // EXPERT_PARTS
    rows = part_refs[0].shape[0]
    for i, ref in enumerate(part_refs):
        rows_v[i * rows : (i + 1) * rows, :] = ref[...]
    mark_ref[...] = jnp.zeros(mark_ref.shape, mark_ref.dtype)
    gate, upper = 0.0, 0.0
    for i in range(EXPERT_PARTS):
        ds = pl.ds(i * step, step)
        x = rows_v[:, ds]
        gate = gate + jnp.dot(x, gate_ref[ds, :], preferred_element_type=jnp.float32)
        upper = upper + jnp.dot(x, up_ref[ds, :], preferred_element_type=jnp.float32)
    inner = (gate / (1.0 + jnp.exp(-gate)) * upper).astype(jnp.bfloat16)
    for i in range(EXPERT_PARTS):
        ds = pl.ds(i * step, step)
        partial = jnp.dot(inner, down_ref[:, ds], preferred_element_type=jnp.float32)
        for j, ref in enumerate(out_refs):
            ref[:, ds] = partial[j * size : (j + 1) * size].astype(jnp.bfloat16)


def experts(parts, weights, earlier, size):
    rows, depth = parts[0].shape
    count = len(parts)
    outs = count * rows // size
    vmem = pl.BlockSpec(memory_space=pltpu.VMEM)
    out = pl.pallas_call(
        functools.partial(expert_kernel, count),
        out_shape=[jax.ShapeDtypeStruct((size, depth), jnp.bfloat16)] * outs + [MARK],
        in_specs=[vmem] * (count + 3) + [pl.BlockSpec(memory_space=pl.ANY)],
        out_specs=[vmem] * (outs + 1),
        scratch_shapes=[pltpu.VMEM((count * rows, depth), jnp.bfloat16)],
        compiler_params=pltpu.CompilerParams(
            vmem_limit_bytes=(16 << 20) + count * rows * depth * 8
        ),
        name="experts",
    )(*parts, *weights, earlier)
    return out[:outs], out[outs]


def join_kernel(count, *refs):
    out_ref = refs[-1]
    rows, depth = out_ref.shape
    step = depth // EXPERT_PARTS
    for i in range(EXPERT_PARTS):
        ds = pl.ds(i * step, step)
        joined = jnp.concatenate([ref[:, ds].astype(jnp.float32) for ref in refs[:count]], axis=0)
        out_ref[:, ds] = joined.astype(jnp.bfloat16)


def join(parts, earlier):
    depth = parts[0].shape[1]
    rows = sum(part.shape[0] for part in parts)
    vmem = pl.BlockSpec(memory_space=pltpu.VMEM)
    return pl.pallas_call(
        functools.partial(join_kernel, len(parts)),
        out_shape=jax.ShapeDtypeStruct((rows, depth), jnp.bfloat16),
        in_specs=[vmem] * len(parts) + [pl.BlockSpec(memory_space=pl.ANY)] * len(earlier),
        out_specs=vmem,
        compiler_params=pltpu.CompilerParams(vmem_limit_bytes=(2 << 20) + 8 * rows * depth),
        name="join",
    )(*parts, *earlier)


def add_kernel(count, messages, *refs):
    terms, part_refs = refs[:count], refs[-messages:]
    depth = terms[0].shape[1]
    size = part_refs[0].shape[0]
    step = depth // EXPERT_PARTS
    for i in range(EXPERT_PARTS):
        ds = pl.ds(i * step, step)
        total = terms[0][:, ds].astype(jnp.float32)
        for ref in terms[1:]:
            total = total + ref[:, ds].astype(jnp.float32)
        for m, ref in enumerate(part_refs):
            ref[:, ds] = total[m * size : (m + 1) * size].astype(ref.dtype)


def add(terms, messages, earlier, kind=jnp.bfloat16):
    rows, depth = terms[0].shape
    vmem = pl.BlockSpec(memory_space=pltpu.VMEM)
    return pl.pallas_call(
        functools.partial(add_kernel, len(terms), messages),
        out_shape=[jax.ShapeDtypeStruct((rows // messages, depth), kind)] * messages,
        in_specs=[vmem] * len(terms) + [pl.BlockSpec(memory_space=pl.ANY)] * len(earlier),
        out_specs=[vmem] * messages,
        compiler_params=pltpu.CompilerParams(vmem_limit_bytes=(4 << 20) + 16 * rows * depth),
        name="add",
    )(*terms, *earlier)


def pack_kernel(
    slots,
    deltas,
    table_ref,
    ids_ref,
    replica_ref,
    other_ids_ref,
    other_replica_ref,
    raw_ref,
    other_ref,
    gain_ref,
    normed_ref,
    place_ref,
    choose_ref,
    *refs,
):
    message_refs, raw_v = refs[:-1], refs[-1]
    steps, tokens, depth = raw_ref.shape
    top = ids_ref.shape[1]
    index = lax.axis_index("ep")
    core = lax.rem(index, 2)
    group = lax.div(index, SPAN)
    message_rows = 2 * steps * slots
    for b, ref in enumerate((raw_ref, other_ref)):
        for s in range(steps):
            at = (b * steps + s) * tokens
            raw_v[at : at + tokens, :] = ref[s].astype(jnp.float32)
    raw = raw_v[...]
    mean_square = jnp.mean(raw * raw, axis=1, keepdims=True)
    normed = (raw * lax.rsqrt(mean_square + norm_eps) * gain_ref[...]).astype(jnp.bfloat16)
    normed_ref[...] = normed

    row = lax.broadcasted_iota(jnp.int32, place_ref.shape[1:], 0)
    column = lax.broadcasted_iota(jnp.int32, place_ref.shape[1:], 1)
    expert = lax.broadcasted_iota(jnp.int32, choose_ref.shape[1:], 0)
    token = lax.broadcasted_iota(jnp.int32, choose_ref.shape[1:], 1)
    message = row // message_rows
    target = sum(
        [
            jnp.where(message == m, jnp.where(core == 0, low, high) - m, 0)
            for m, (low, high) in enumerate(deltas)
        ],
        message,
    )
    row = target * message_rows + row % message_rows
    place_row = [jnp.full(place_ref.shape[1:], -1, jnp.int32) for _ in range(top)]
    choice = [jnp.full(choose_ref.shape[1:], -1, jnp.int32) for _ in range(top)]
    for b, (ids, replicas) in enumerate(
        ((ids_ref, replica_ref), (other_ids_ref, other_replica_ref))
    ):
        for s in range(steps):
            block = b * steps + s
            earlier = []
            for t in range(tokens):
                for k in range(top):
                    copy = table_ref[replicas[s, k, t], ids[s, k, t]]
                    slot = sum([(copy == c).astype(jnp.int32) for c in earlier], jnp.int32(0))
                    earlier.append(copy)
                    delta = copy ^ group
                    at = delta * message_rows + block * slots + slot
                    at = jnp.where(slot < slots, at, -1)
                    here = block * tokens + t
                    place_row[k] = jnp.where(column == here, at, place_row[k])
                    choice[k] = jnp.where(token == here, ids[s, k, t], choice[k])
    total = jnp.zeros(place_ref.shape[1:], jnp.float32)
    for k in range(top):
        hit = (place_row[k] == row).astype(jnp.float32)
        place_ref[k] = hit
        choose_ref[k] = (choice[k] == expert).astype(jnp.float32)
        total = total + hit
    packed = jnp.dot(total.astype(jnp.bfloat16), normed, preferred_element_type=jnp.float32)
    for m, ref in enumerate(message_refs):
        ref[...] = packed[m * message_rows : (m + 1) * message_rows].astype(jnp.bfloat16)


def pack(slots, deltas, hidden, other, gain, copy_table, own_choice, other_choice, experts_total):
    steps, tokens, depth = hidden.shape
    top = own_choice[0].shape[1]
    messages = len(deltas)
    message_rows = 2 * steps * slots
    columns = 2 * steps * tokens
    vmem = pl.BlockSpec(memory_space=pltpu.VMEM)
    smem = pl.BlockSpec(memory_space=pltpu.SMEM)
    shape = jax.ShapeDtypeStruct
    out = pl.pallas_call(
        functools.partial(pack_kernel, slots, deltas),
        out_shape=[
            shape((columns, depth), jnp.bfloat16),
            shape((top, messages * message_rows, columns), jnp.float32),
            shape((top, experts_total, columns), jnp.float32),
        ]
        + [shape((message_rows, depth), jnp.bfloat16)] * messages,
        in_specs=[smem] * 5 + [vmem] * 3,
        out_specs=[vmem] * (3 + messages),
        scratch_shapes=[pltpu.VMEM((columns, depth), jnp.float32)],
        compiler_params=pltpu.CompilerParams(
            vmem_limit_bytes=62 << 20
        ),
        name="pack",
    )(copy_table, *own_choice, *other_choice, hidden, other, gain)
    return out[0], out[1], out[2], out[3:]


def weigh_kernel(normed_ref, router_ref, place_ref, choose_ref, weigh_ref):
    scores = jax.nn.sigmoid(
        lax.dot_general(
            router_ref[...],
            normed_ref[...],
            (((1,), (1,)), ((), ())),
            preferred_element_type=jnp.float32,
        )
    )
    top = place_ref.shape[0]
    picked = [jnp.sum(choose_ref[k] * scores, axis=0, keepdims=True) for k in range(top)]
    total = sum(picked[1:], picked[0])
    weigh = jnp.zeros(weigh_ref.shape, jnp.float32)
    for k in range(top):
        weigh = weigh + place_ref[k] * (routed_scale * picked[k] / total)
    weigh_ref[...] = weigh


def weigh(normed, router_t, place, choose):
    vmem = pl.BlockSpec(memory_space=pltpu.VMEM)
    return pl.pallas_call(
        weigh_kernel,
        out_shape=jax.ShapeDtypeStruct(place.shape[1:], jnp.float32),
        in_specs=[vmem] * 4,
        out_specs=vmem,
        cost_estimate=pl.CostEstimate(
            flops=2 * normed.size * 256, bytes_accessed=2 * normed.size, transcendentals=256
        ),
        compiler_params=pltpu.CompilerParams(vmem_limit_bytes=4 << 20),
        name="weigh",
    )(normed, router_t, place, choose)


def weighted(weights, part_refs):
    high = weights.astype(jnp.bfloat16)
    left = weights - high.astype(jnp.float32)
    middle = left.astype(jnp.bfloat16)
    low = (left - middle.astype(jnp.float32)).astype(jnp.bfloat16)
    rows = jnp.concatenate([ref[...].astype(jnp.float32) for ref in part_refs], axis=0)
    rows = rows.astype(jnp.bfloat16)
    pieces = [
        lax.dot_general(w, rows, (((0,), (0,)), ((), ())), preferred_element_type=jnp.float32)
        for w in (high, middle, low)
    ]
    return pieces[0] + (pieces[1] + pieces[2])


def first_half_kernel(weigh_ref, *refs):
    part_refs, out_ref = refs[:-1], refs[-1]
    out_ref[...] = weighted(weigh_ref[: weigh_ref.shape[0] // 2, :], part_refs)


def second_half_kernel(weigh_ref, first_ref, *refs):
    part_refs, own_ref, send_ref = refs[:-2], refs[-2], refs[-1]
    size = part_refs[0].shape[0]
    weights = weigh_ref[weigh_ref.shape[0] // 2 :, :]
    weights = jnp.concatenate([weights, weights[-size:]], axis=0)
    result = first_ref[...] + weighted(weights, part_refs)
    half = own_ref.shape[0]
    own_ref[...] = result[:half]
    send_ref[...] = result[half:].astype(jnp.bfloat16)


def combine(weights, parts):
    depth = parts[0].shape[1]
    tokens = weights.shape[1]
    vmem = pl.BlockSpec(memory_space=pltpu.VMEM)
    params = pltpu.CompilerParams(vmem_limit_bytes=(8 << 20) + 8 * weights.shape[0] * depth)
    middle = (len(parts) - 1) // 2
    first = pl.pallas_call(
        first_half_kernel,
        out_shape=jax.ShapeDtypeStruct((tokens, depth), jnp.float32),
        in_specs=[vmem] * (1 + middle),
        out_specs=vmem,
        compiler_params=params,
        name="combine",
    )(weights, *parts[:middle])
    return pl.pallas_call(
        second_half_kernel,
        out_shape=[
            jax.ShapeDtypeStruct((tokens // 2, depth), jnp.float32),
            jax.ShapeDtypeStruct((tokens // 2, depth), jnp.bfloat16),
        ],
        in_specs=[vmem] * (2 + len(parts) - middle),
        out_specs=[vmem] * 2,
        compiler_params=params,
        name="combine",
    )(weights, first, *parts[middle:])


def finish_kernel(own_ref, received_ref, out_ref):
    result = own_ref[...] + received_ref[...].astype(jnp.float32)
    steps, tokens, _ = out_ref.shape
    for s in range(steps):
        out_ref[s] = result[s * tokens : (s + 1) * tokens].astype(jnp.bfloat16)


def finish(own, received, shape):
    vmem = pl.BlockSpec(memory_space=pltpu.VMEM)
    return pl.pallas_call(
        finish_kernel,
        out_shape=jax.ShapeDtypeStruct(shape, jnp.bfloat16),
        in_specs=[vmem] * 2,
        out_specs=vmem,
        compiler_params=pltpu.CompilerParams(vmem_limit_bytes=4 << 20),
        name="finish",
    )(own, received)


def mixture(
    hidden, norm_gain, router, expert_ids, replica, copy_table, gate_w, up_w, down_w, attended_mark
):
    groups = lax.axis_size("ep") // SPAN
    messages = groups // 2
    tokens = hidden.shape[1]
    slots = max(2, 2 * tokens * expert_ids.shape[2] // groups)
    deltas = lanes(groups)

    def swapped(value):
        return flipped(value, 1, 1)

    own_choice = (expert_ids.transpose(0, 2, 1), replica.transpose(0, 2, 1))
    other_choice = (swapped(own_choice[0]), swapped(own_choice[1]))
    normed, place, choose, packed = pack(
        slots,
        deltas,
        hidden,
        swapped(hidden),
        norm_gain[None, :],
        copy_table.T,
        own_choice,
        other_choice,
        router.shape[1],
    )

    def rounds(parts):
        return [
            flipped(part, SPAN * low, SPAN * high) for part, (low, high) in zip(parts, deltas)
        ]

    def to_near(part):
        return flipped(part, 0, SPAN)

    def to_far(part):
        return flipped(part, 2, SPAN + 2)

    weights = weigh(normed, router.T, place, choose)
    expert_weights = (gate_w, up_w, down_w)
    half = messages // 2
    size = packed[0].shape[0]
    received = rounds(packed[:-1])
    near_last, far_last = to_near(packed[-1]), to_far(packed[-1])
    held, mark = load(expert_weights, place)
    near = join([*received, near_last], [mark, far_last])
    far = flipped(join(received, [mark, far_last]), 2, 2)
    near_out, mark = experts([near, swapped(near)], held, mark, half * size)
    near_sums = [
        *add([near_out[0], swapped(near_out[2])], half, [], jnp.float32),
        *add([near_out[1], swapped(near_out[3])], half, [], jnp.float32),
    ]
    returned_near = to_near(near_sums[-1].astype(jnp.bfloat16))
    far = join([far, far_last], [mark, weights, attended_mark])
    far_out, mark = experts([far, swapped(far)], held, mark, half * size)
    far_sums = [
        *add([far_out[0], swapped(far_out[2])], half, []),
        *add([far_out[1], swapped(far_out[3])], half, []),
    ]
    totals = []
    earlier = [mark]
    for near_sum, far_sum in zip(near_sums[:-1], far_sums[:-1]):
        totals += add([near_sum, flipped(far_sum, 2, 2)], 1, earlier)
        earlier = totals[-1:]
    returned = [*rounds(totals), returned_near, to_far(far_sums[-1])]
    own, send = combine(weights, returned)
    return finish(own, swapped(send), hidden.shape)


def per_device(
    hidden,
    norm_gain,
    router,
    expert_ids,
    replica,
    copy_table,
    gate_w,
    up_w,
    down_w,
    query,
    cache,
    lengths,
    fresh_kv,
):
    attended, attended_mark = attend(query, cache, lengths, fresh_kv)
    moe_out = mixture(
        hidden,
        norm_gain,
        router,
        expert_ids,
        replica,
        copy_table,
        gate_w,
        up_w,
        down_w,
        attended_mark,
    )
    return (attended, moe_out)


def solution(mesh):
    return jax.shard_map(
        per_device,
        mesh=mesh,
        in_specs=(
            P(None, ("groups", "ep"), None),
            P(),
            P(),
            P(None, ("groups", "ep"), None),
            P(None, ("groups", "ep"), None),
            P(),
            P(None, "ep"),
            P(None, "ep"),
            P("ep", None),
            P(None, ("groups", "ep"), None, None),
            P(("groups", "ep"), None, None),
            P(("groups", "ep")),
            P(None, ("groups", "ep"), None),
        ),
        out_specs=(P(None, ("groups", "ep"), None, None), P(None, ("groups", "ep"), None)),
        check_vma=False,
    )
```

```python
import functools

import jax
import jax.numpy as jnp
from jax import lax
from jax.experimental import pallas as pl
from jax.experimental.pallas import tpu as pltpu
from jax.sharding import PartitionSpec as P

KV = 512
SPAN = 4

softmax_scale = 192.0 ** (-0.5)
routed_scale = 2.5
norm_eps = 1e-06
masked_score = -1e30
EXPERT_PARTS = 7
MARK = jax.ShapeDtypeStruct((8, 128), jnp.float32)


def flipped(value, low_core, high_core):
    pairs = [(e, e ^ (high_core if e % 2 else low_core)) for e in range(lax.axis_size("ep"))]
    return lax.ppermute(value, "ep", pairs)


def lanes(groups):
    hops = [(d & 1) + (d >> 1) for d in range(groups)]
    chosen = ([], [])
    for d in sorted(range(2, groups), key=lambda d: (-hops[d], -d)):
        sums = [sum(hops[e] for e in lane) for lane in chosen]
        lane = 0 if sums[0] <= sums[1] else 1
        if 2 * len(chosen[lane]) == groups - 2:
            lane = 1 - lane
        chosen[lane].append(d)
    return [*zip(*chosen), (0, 1)]


def attend_kernel(lengths_ref, query_ref, cache_ref, fresh_ref, out_ref, mark_ref):
    mark_ref[...] = jnp.zeros(mark_ref.shape, mark_ref.dtype)
    steps, tokens, heads, _ = query_ref.shape
    slots = cache_ref.shape[1]
    pad = 128 - slots
    for n in range(tokens):
        row = lax.broadcasted_iota(jnp.int32, (pad, 1), 0)
        extra = jnp.zeros((pad, fresh_ref.shape[2]), jnp.float32)
        for s in range(steps):
            block = fresh_ref[s].astype(jnp.float32)
            which = lax.broadcasted_iota(jnp.int32, block.shape, 0) == n
            one = jnp.sum(jnp.where(which, block, 0.0), axis=0, keepdims=True)
            extra = jnp.where(row == s, one, extra)
        keys = jnp.concatenate([cache_ref[n], extra.astype(jnp.bfloat16)], axis=0)
        queries = jnp.concatenate([query_ref[s, n] for s in range(steps)], axis=0)
        scores = (
            lax.dot_general(
                queries, keys, (((1,), (1,)), ((), ())), preferred_element_type=jnp.float32
            )
            * softmax_scale
        )
        position = lax.broadcasted_iota(jnp.int32, scores.shape, 1)
        step = lax.broadcasted_iota(jnp.int32, scores.shape, 0) // heads
        valid = (position < lengths_ref[n]) | (
            (position >= slots) & (position - slots <= step)
        )
        scores = jnp.where(valid, scores, masked_score)
        terms = jnp.exp(scores - jnp.max(scores, axis=1, keepdims=True))
        terms = jnp.where(valid, terms, 0.0)
        probs = (terms / jnp.sum(terms, axis=1, keepdims=True)).astype(jnp.bfloat16)
        mixed = jnp.dot(probs, keys[:, :KV], preferred_element_type=jnp.float32)
        for s in range(steps):
            out_ref[s, n] = mixed[s * heads : (s + 1) * heads].astype(jnp.bfloat16)


def attend(query, cache, lengths, fresh):
    steps, tokens, heads, width = query.shape
    vmem = pl.BlockSpec(memory_space=pltpu.VMEM)
    return pl.pallas_call(
        attend_kernel,
        out_shape=[jax.ShapeDtypeStruct((steps, tokens, heads, KV), jnp.bfloat16), MARK],
        in_specs=[pl.BlockSpec(memory_space=pltpu.SMEM)] + [vmem] * 3,
        out_specs=[vmem] * 2,
        compiler_params=pltpu.CompilerParams(vmem_limit_bytes=12 << 20),
        cost_estimate=pl.CostEstimate(
            flops=4 * steps * tokens * heads * 128 * width,
            bytes_accessed=2 * (2 * query.size + cache.size),
            transcendentals=steps * tokens * heads * 128,
        ),
        name="attention",
    )(lengths, query, cache, fresh)


def load_kernel(gate_ref, up_ref, down_ref, _, gate_v, up_v, down_v, mark_ref, sems):
    copies = [
        pltpu.make_async_copy(source, target, sems.at[i])
        for i, (source, target) in enumerate(
            ((gate_ref, gate_v), (up_ref, up_v), (down_ref, down_v))
        )
    ]
    for copy in copies:
        copy.start()
    mark_ref[...] = jnp.zeros(mark_ref.shape, mark_ref.dtype)
    for copy in copies:
        copy.wait()


def load(weights, earlier):
    vmem = pl.BlockSpec(memory_space=pltpu.VMEM)
    anywhere = pl.BlockSpec(memory_space=pl.ANY)
    *held, mark = pl.pallas_call(
        load_kernel,
        out_shape=[jax.ShapeDtypeStruct(w.shape, w.dtype) for w in weights] + [MARK],
        in_specs=[anywhere] * 4,
        out_specs=[vmem] * 4,
        scratch_shapes=[pltpu.SemaphoreType.DMA((3,))],
        compiler_params=pltpu.CompilerParams(vmem_limit_bytes=40 << 20),
        name="load",
    )(*weights, earlier)
    return held, mark


def expert_kernel(count, *refs):
    part_refs, refs = refs[:count], refs[count:]
    gate_ref, up_ref, down_ref, _, *out_refs, mark_ref, rows_v = refs
    size = out_refs[0].shape[0]
    step = rows_v.shape[1] // EXPERT_PARTS
    rows = part_refs[0].shape[0]
    for i, ref in enumerate(part_refs):
        rows_v[i * rows : (i + 1) * rows, :] = ref[...]
    mark_ref[...] = jnp.zeros(mark_ref.shape, mark_ref.dtype)
    gate, upper = 0.0, 0.0
    for i in range(EXPERT_PARTS):
        ds = pl.ds(i * step, step)
        x = rows_v[:, ds]
        gate = gate + jnp.dot(x, gate_ref[ds, :], preferred_element_type=jnp.float32)
        upper = upper + jnp.dot(x, up_ref[ds, :], preferred_element_type=jnp.float32)
    inner = (gate / (1.0 + jnp.exp(-gate)) * upper).astype(jnp.bfloat16)
    for i in range(EXPERT_PARTS):
        ds = pl.ds(i * step, step)
        partial = jnp.dot(inner, down_ref[:, ds], preferred_element_type=jnp.float32)
        for j, ref in enumerate(out_refs):
            ref[:, ds] = partial[j * size : (j + 1) * size].astype(jnp.bfloat16)


def experts(parts, weights, earlier, size):
    rows, depth = parts[0].shape
    count = len(parts)
    outs = count * rows // size
    vmem = pl.BlockSpec(memory_space=pltpu.VMEM)
    out = pl.pallas_call(
        functools.partial(expert_kernel, count),
        out_shape=[jax.ShapeDtypeStruct((size, depth), jnp.bfloat16)] * outs + [MARK],
        in_specs=[vmem] * (count + 3) + [pl.BlockSpec(memory_space=pl.ANY)],
        out_specs=[vmem] * (outs + 1),
        scratch_shapes=[pltpu.VMEM((count * rows, depth), jnp.bfloat16)],
        compiler_params=pltpu.CompilerParams(
            vmem_limit_bytes=(16 << 20) + count * rows * depth * 8
        ),
        name="experts",
    )(*parts, *weights, earlier)
    return out[:outs], out[outs]


def join_kernel(count, *refs):
    out_ref = refs[-1]
    rows, depth = out_ref.shape
    step = depth // EXPERT_PARTS
    for i in range(EXPERT_PARTS):
        ds = pl.ds(i * step, step)
        joined = jnp.concatenate([ref[:, ds].astype(jnp.float32) for ref in refs[:count]], axis=0)
        out_ref[:, ds] = joined.astype(jnp.bfloat16)


def join(parts, earlier):
    depth = parts[0].shape[1]
    rows = sum(part.shape[0] for part in parts)
    vmem = pl.BlockSpec(memory_space=pltpu.VMEM)
    return pl.pallas_call(
        functools.partial(join_kernel, len(parts)),
        out_shape=jax.ShapeDtypeStruct((rows, depth), jnp.bfloat16),
        in_specs=[vmem] * len(parts) + [pl.BlockSpec(memory_space=pl.ANY)] * len(earlier),
        out_specs=vmem,
        compiler_params=pltpu.CompilerParams(vmem_limit_bytes=(2 << 20) + 8 * rows * depth),
        name="join",
    )(*parts, *earlier)


def add_kernel(count, messages, *refs):
    terms, part_refs = refs[:count], refs[-messages:]
    depth = terms[0].shape[1]
    size = part_refs[0].shape[0]
    step = depth // EXPERT_PARTS
    for i in range(EXPERT_PARTS):
        ds = pl.ds(i * step, step)
        total = terms[0][:, ds].astype(jnp.float32)
        for ref in terms[1:]:
            total = total + ref[:, ds].astype(jnp.float32)
        for m, ref in enumerate(part_refs):
            ref[:, ds] = total[m * size : (m + 1) * size].astype(ref.dtype)


def add(terms, messages, earlier, kind=jnp.bfloat16):
    rows, depth = terms[0].shape
    vmem = pl.BlockSpec(memory_space=pltpu.VMEM)
    return pl.pallas_call(
        functools.partial(add_kernel, len(terms), messages),
        out_shape=[jax.ShapeDtypeStruct((rows // messages, depth), kind)] * messages,
        in_specs=[vmem] * len(terms) + [pl.BlockSpec(memory_space=pl.ANY)] * len(earlier),
        out_specs=[vmem] * messages,
        compiler_params=pltpu.CompilerParams(vmem_limit_bytes=(4 << 20) + 16 * rows * depth),
        name="add",
    )(*terms, *earlier)


def pack_kernel(
    slots,
    deltas,
    table_ref,
    ids_ref,
    replica_ref,
    other_ids_ref,
    other_replica_ref,
    raw_ref,
    other_ref,
    gain_ref,
    normed_ref,
    place_ref,
    choose_ref,
    *refs,
):
    message_refs, raw_v = refs[:-1], refs[-1]
    steps, tokens, depth = raw_ref.shape
    top = ids_ref.shape[1]
    index = lax.axis_index("ep")
    core = lax.rem(index, 2)
    group = lax.div(index, SPAN)
    message_rows = 2 * steps * slots
    for b, ref in enumerate((raw_ref, other_ref)):
        for s in range(steps):
            at = (b * steps + s) * tokens
            raw_v[at : at + tokens, :] = ref[s].astype(jnp.float32)
    raw = raw_v[...]
    mean_square = jnp.mean(raw * raw, axis=1, keepdims=True)
    normed = (raw * lax.rsqrt(mean_square + norm_eps) * gain_ref[...]).astype(jnp.bfloat16)
    normed_ref[...] = normed

    row = lax.broadcasted_iota(jnp.int32, place_ref.shape[1:], 0)
    column = lax.broadcasted_iota(jnp.int32, place_ref.shape[1:], 1)
    expert = lax.broadcasted_iota(jnp.int32, choose_ref.shape[1:], 0)
    token = lax.broadcasted_iota(jnp.int32, choose_ref.shape[1:], 1)
    message = row // message_rows
    target = sum(
        [
            jnp.where(message == m, jnp.where(core == 0, low, high) - m, 0)
            for m, (low, high) in enumerate(deltas)
        ],
        message,
    )
    row = target * message_rows + row % message_rows
    place_row = [jnp.full(place_ref.shape[1:], -1, jnp.int32) for _ in range(top)]
    choice = [jnp.full(choose_ref.shape[1:], -1, jnp.int32) for _ in range(top)]
    for b, (ids, replicas) in enumerate(
        ((ids_ref, replica_ref), (other_ids_ref, other_replica_ref))
    ):
        for s in range(steps):
            block = b * steps + s
            earlier = []
            for t in range(tokens):
                for k in range(top):
                    copy = table_ref[replicas[s, k, t], ids[s, k, t]]
                    slot = sum([(copy == c).astype(jnp.int32) for c in earlier], jnp.int32(0))
                    earlier.append(copy)
                    delta = copy ^ group
                    at = delta * message_rows + block * slots + slot
                    at = jnp.where(slot < slots, at, -1)
                    here = block * tokens + t
                    place_row[k] = jnp.where(column == here, at, place_row[k])
                    choice[k] = jnp.where(token == here, ids[s, k, t], choice[k])
    total = jnp.zeros(place_ref.shape[1:], jnp.float32)
    for k in range(top):
        hit = (place_row[k] == row).astype(jnp.float32)
        place_ref[k] = hit
        choose_ref[k] = (choice[k] == expert).astype(jnp.float32)
        total = total + hit
    packed = jnp.dot(total.astype(jnp.bfloat16), normed, preferred_element_type=jnp.float32)
    for m, ref in enumerate(message_refs):
        ref[...] = packed[m * message_rows : (m + 1) * message_rows].astype(jnp.bfloat16)


def pack(slots, deltas, hidden, other, gain, copy_table, own_choice, other_choice, experts_total):
    steps, tokens, depth = hidden.shape
    top = own_choice[0].shape[1]
    messages = len(deltas)
    message_rows = 2 * steps * slots
    columns = 2 * steps * tokens
    vmem = pl.BlockSpec(memory_space=pltpu.VMEM)
    smem = pl.BlockSpec(memory_space=pltpu.SMEM)
    shape = jax.ShapeDtypeStruct
    out = pl.pallas_call(
        functools.partial(pack_kernel, slots, deltas),
        out_shape=[
            shape((columns, depth), jnp.bfloat16),
            shape((top, messages * message_rows, columns), jnp.float32),
            shape((top, experts_total, columns), jnp.float32),
        ]
        + [shape((message_rows, depth), jnp.bfloat16)] * messages,
        in_specs=[smem] * 5 + [vmem] * 3,
        out_specs=[vmem] * (3 + messages),
        scratch_shapes=[pltpu.VMEM((columns, depth), jnp.float32)],
        compiler_params=pltpu.CompilerParams(
            vmem_limit_bytes=(64 << 20) - (64 << 10)
        ),
        name="pack",
    )(copy_table, *own_choice, *other_choice, hidden, other, gain)
    return out[0], out[1], out[2], out[3:]


def weigh_kernel(normed_ref, router_ref, place_ref, choose_ref, weigh_ref):
    scores = jax.nn.sigmoid(
        lax.dot_general(
            router_ref[...],
            normed_ref[...],
            (((1,), (1,)), ((), ())),
            preferred_element_type=jnp.float32,
        )
    )
    top = place_ref.shape[0]
    picked = [jnp.sum(choose_ref[k] * scores, axis=0, keepdims=True) for k in range(top)]
    total = sum(picked[1:], picked[0])
    weigh = jnp.zeros(weigh_ref.shape, jnp.float32)
    for k in range(top):
        weigh = weigh + place_ref[k] * (routed_scale * picked[k] / total)
    weigh_ref[...] = weigh


def weigh(normed, router_t, place, choose):
    vmem = pl.BlockSpec(memory_space=pltpu.VMEM)
    return pl.pallas_call(
        weigh_kernel,
        out_shape=jax.ShapeDtypeStruct(place.shape[1:], jnp.float32),
        in_specs=[vmem] * 4,
        out_specs=vmem,
        cost_estimate=pl.CostEstimate(
            flops=2 * normed.size * 256, bytes_accessed=2 * normed.size, transcendentals=256
        ),
        compiler_params=pltpu.CompilerParams(vmem_limit_bytes=4 << 20),
        name="weigh",
    )(normed, router_t, place, choose)


def weighted(weights, part_refs):
    high = weights.astype(jnp.bfloat16)
    left = weights - high.astype(jnp.float32)
    middle = left.astype(jnp.bfloat16)
    low = (left - middle.astype(jnp.float32)).astype(jnp.bfloat16)
    rows = jnp.concatenate([ref[...].astype(jnp.float32) for ref in part_refs], axis=0)
    rows = rows.astype(jnp.bfloat16)
    pieces = [
        lax.dot_general(w, rows, (((0,), (0,)), ((), ())), preferred_element_type=jnp.float32)
        for w in (high, middle, low)
    ]
    return pieces[0] + (pieces[1] + pieces[2])


def first_half_kernel(weigh_ref, *refs):
    part_refs, out_ref = refs[:-1], refs[-1]
    out_ref[...] = weighted(weigh_ref[: weigh_ref.shape[0] // 2, :], part_refs)


def second_half_kernel(weigh_ref, first_ref, *refs):
    part_refs, own_ref, send_ref = refs[:-2], refs[-2], refs[-1]
    size = part_refs[0].shape[0]
    weights = weigh_ref[weigh_ref.shape[0] // 2 :, :]
    weights = jnp.concatenate([weights, weights[-size:]], axis=0)
    result = first_ref[...] + weighted(weights, part_refs)
    half = own_ref.shape[0]
    own_ref[...] = result[:half]
    send_ref[...] = result[half:].astype(jnp.bfloat16)


def combine(weights, parts):
    depth = parts[0].shape[1]
    tokens = weights.shape[1]
    vmem = pl.BlockSpec(memory_space=pltpu.VMEM)
    params = pltpu.CompilerParams(vmem_limit_bytes=(8 << 20) + 8 * weights.shape[0] * depth)
    middle = (len(parts) - 1) // 2
    first = pl.pallas_call(
        first_half_kernel,
        out_shape=jax.ShapeDtypeStruct((tokens, depth), jnp.float32),
        in_specs=[vmem] * (1 + middle),
        out_specs=vmem,
        compiler_params=params,
        name="combine",
    )(weights, *parts[:middle])
    return pl.pallas_call(
        second_half_kernel,
        out_shape=[
            jax.ShapeDtypeStruct((tokens // 2, depth), jnp.float32),
            jax.ShapeDtypeStruct((tokens // 2, depth), jnp.bfloat16),
        ],
        in_specs=[vmem] * (2 + len(parts) - middle),
        out_specs=[vmem] * 2,
        compiler_params=params,
        name="combine",
    )(weights, first, *parts[middle:])


def finish_kernel(own_ref, received_ref, out_ref):
    result = own_ref[...] + received_ref[...].astype(jnp.float32)
    steps, tokens, _ = out_ref.shape
    for s in range(steps):
        out_ref[s] = result[s * tokens : (s + 1) * tokens].astype(jnp.bfloat16)


def finish(own, received, shape):
    vmem = pl.BlockSpec(memory_space=pltpu.VMEM)
    return pl.pallas_call(
        finish_kernel,
        out_shape=jax.ShapeDtypeStruct(shape, jnp.bfloat16),
        in_specs=[vmem] * 2,
        out_specs=vmem,
        compiler_params=pltpu.CompilerParams(vmem_limit_bytes=4 << 20),
        name="finish",
    )(own, received)


def mixture(
    hidden, norm_gain, router, expert_ids, replica, copy_table, gate_w, up_w, down_w, attended_mark
):
    groups = lax.axis_size("ep") // SPAN
    messages = groups // 2
    tokens = hidden.shape[1]
    slots = max(2, 2 * tokens * expert_ids.shape[2] // groups)
    deltas = lanes(groups)

    def swapped(value):
        return flipped(value, 1, 1)

    own_choice = (expert_ids.transpose(0, 2, 1), replica.transpose(0, 2, 1))
    other_choice = (swapped(own_choice[0]), swapped(own_choice[1]))
    normed, place, choose, packed = pack(
        slots,
        deltas,
        hidden,
        swapped(hidden),
        norm_gain[None, :],
        copy_table.T,
        own_choice,
        other_choice,
        router.shape[1],
    )

    def rounds(parts):
        return [
            flipped(part, SPAN * low, SPAN * high) for part, (low, high) in zip(parts, deltas)
        ]

    def to_near(part):
        return flipped(part, 0, SPAN)

    def to_far(part):
        return flipped(part, 2, SPAN + 2)

    weights = weigh(normed, router.T, place, choose)
    expert_weights = (gate_w, up_w, down_w)
    half = messages // 2
    size = packed[0].shape[0]
    received = rounds(packed[:-1])
    near_last, far_last = to_near(packed[-1]), to_far(packed[-1])
    held, mark = load(expert_weights, place)
    near = join([*received, near_last], [mark, far_last])
    far = flipped(join(received, [mark, far_last]), 2, 2)
    near_out, mark = experts([near, swapped(near)], held, mark, half * size)
    near_sums = [
        *add([near_out[0], swapped(near_out[2])], half, [], jnp.float32),
        *add([near_out[1], swapped(near_out[3])], half, [], jnp.float32),
    ]
    returned_near = to_near(near_sums[-1].astype(jnp.bfloat16))
    far = join([far, far_last], [mark, weights, attended_mark, near_sums[0]])
    far_out, mark = experts([far, swapped(far)], held, mark, half * size)
    far_sums = [
        *add([far_out[0], swapped(far_out[2])], half, []),
        *add([far_out[1], swapped(far_out[3])], half, []),
    ]
    totals = []
    earlier = [mark]
    for near_sum, far_sum in zip(near_sums[:-1], far_sums[:-1]):
        totals += add([near_sum, flipped(far_sum, 2, 2)], 1, earlier)
        earlier = totals[-1:]
    returned = [*rounds(totals), returned_near, to_far(far_sums[-1])]
    own, send = combine(weights, returned)
    return finish(own, swapped(send), hidden.shape)


def per_device(
    hidden,
    norm_gain,
    router,
    expert_ids,
    replica,
    copy_table,
    gate_w,
    up_w,
    down_w,
    query,
    cache,
    lengths,
    fresh_kv,
):
    attended, attended_mark = attend(query, cache, lengths, fresh_kv)
    moe_out = mixture(
        hidden,
        norm_gain,
        router,
        expert_ids,
        replica,
        copy_table,
        gate_w,
        up_w,
        down_w,
        attended_mark,
    )
    return (attended, moe_out)


def solution(mesh):
    return jax.shard_map(
        per_device,
        mesh=mesh,
        in_specs=(
            P(None, ("groups", "ep"), None),
            P(),
            P(),
            P(None, ("groups", "ep"), None),
            P(None, ("groups", "ep"), None),
            P(),
            P(None, "ep"),
            P(None, "ep"),
            P("ep", None),
            P(None, ("groups", "ep"), None, None),
            P(("groups", "ep"), None, None),
            P(("groups", "ep")),
            P(None, ("groups", "ep"), None),
        ),
        out_specs=(P(None, ("groups", "ep"), None, None), P(None, ("groups", "ep"), None)),
        check_vma=False,
    )
```

```python
import functools

import jax
import jax.numpy as jnp
from jax import lax
from jax.experimental import pallas as pl
from jax.experimental.pallas import tpu as pltpu
from jax.sharding import PartitionSpec as P

KV = 512
SPAN = 4

softmax_scale = 192.0 ** (-0.5)
routed_scale = 2.5
norm_eps = 1e-06
masked_score = -1e30
EXPERT_PARTS = 7
MARK = jax.ShapeDtypeStruct((8, 128), jnp.float32)


def flipped(value, low_core, high_core):
    pairs = [(e, e ^ (high_core if e % 2 else low_core)) for e in range(lax.axis_size("ep"))]
    return lax.ppermute(value, "ep", pairs)


def lanes(groups):
    hops = [(d & 1) + (d >> 1) for d in range(groups)]
    chosen = ([], [])
    for d in sorted(range(2, groups), key=lambda d: (-hops[d], -d)):
        sums = [sum(hops[e] for e in lane) for lane in chosen]
        lane = 0 if sums[0] <= sums[1] else 1
        if 2 * len(chosen[lane]) == groups - 2:
            lane = 1 - lane
        chosen[lane].append(d)
    return [*zip(*chosen), (0, 1)]


def attend_kernel(lengths_ref, query_ref, cache_ref, fresh_ref, out_ref, mark_ref):
    mark_ref[...] = jnp.zeros(mark_ref.shape, mark_ref.dtype)
    steps, tokens, heads, _ = query_ref.shape
    slots = cache_ref.shape[1]
    pad = 128 - slots
    for n in range(tokens):
        row = lax.broadcasted_iota(jnp.int32, (pad, 1), 0)
        extra = jnp.zeros((pad, fresh_ref.shape[2]), jnp.float32)
        for s in range(steps):
            block = fresh_ref[s].astype(jnp.float32)
            which = lax.broadcasted_iota(jnp.int32, block.shape, 0) == n
            one = jnp.sum(jnp.where(which, block, 0.0), axis=0, keepdims=True)
            extra = jnp.where(row == s, one, extra)
        keys = jnp.concatenate([cache_ref[n], extra.astype(jnp.bfloat16)], axis=0)
        queries = jnp.concatenate([query_ref[s, n] for s in range(steps)], axis=0)
        scores = (
            lax.dot_general(
                queries, keys, (((1,), (1,)), ((), ())), preferred_element_type=jnp.float32
            )
            * softmax_scale
        )
        position = lax.broadcasted_iota(jnp.int32, scores.shape, 1)
        step = lax.broadcasted_iota(jnp.int32, scores.shape, 0) // heads
        valid = (position < lengths_ref[n]) | (
            (position >= slots) & (position - slots <= step)
        )
        scores = jnp.where(valid, scores, masked_score)
        terms = jnp.exp(scores - jnp.max(scores, axis=1, keepdims=True))
        terms = jnp.where(valid, terms, 0.0)
        probs = (terms / jnp.sum(terms, axis=1, keepdims=True)).astype(jnp.bfloat16)
        mixed = jnp.dot(probs, keys[:, :KV], preferred_element_type=jnp.float32)
        for s in range(steps):
            out_ref[s, n] = mixed[s * heads : (s + 1) * heads].astype(jnp.bfloat16)


def attend(query, cache, lengths, fresh):
    steps, tokens, heads, width = query.shape
    vmem = pl.BlockSpec(memory_space=pltpu.VMEM)
    return pl.pallas_call(
        attend_kernel,
        out_shape=[jax.ShapeDtypeStruct((steps, tokens, heads, KV), jnp.bfloat16), MARK],
        in_specs=[pl.BlockSpec(memory_space=pltpu.SMEM)] + [vmem] * 3,
        out_specs=[vmem] * 2,
        compiler_params=pltpu.CompilerParams(vmem_limit_bytes=12 << 20),
        cost_estimate=pl.CostEstimate(
            flops=4 * steps * tokens * heads * 128 * width,
            bytes_accessed=2 * (2 * query.size + cache.size),
            transcendentals=steps * tokens * heads * 128,
        ),
        name="attention",
    )(lengths, query, cache, fresh)


def load_kernel(gate_ref, up_ref, down_ref, _, gate_v, up_v, down_v, mark_ref, sems):
    copies = [
        pltpu.make_async_copy(source, target, sems.at[i])
        for i, (source, target) in enumerate(
            ((gate_ref, gate_v), (up_ref, up_v), (down_ref, down_v))
        )
    ]
    for copy in copies:
        copy.start()
    mark_ref[...] = jnp.zeros(mark_ref.shape, mark_ref.dtype)
    for copy in copies:
        copy.wait()


def load(weights, earlier):
    vmem = pl.BlockSpec(memory_space=pltpu.VMEM)
    anywhere = pl.BlockSpec(memory_space=pl.ANY)
    *held, mark = pl.pallas_call(
        load_kernel,
        out_shape=[jax.ShapeDtypeStruct(w.shape, w.dtype) for w in weights] + [MARK],
        in_specs=[anywhere] * 4,
        out_specs=[vmem] * 4,
        scratch_shapes=[pltpu.SemaphoreType.DMA((3,))],
        compiler_params=pltpu.CompilerParams(vmem_limit_bytes=40 << 20),
        name="load",
    )(*weights, earlier)
    return held, mark


def expert_kernel(count, *refs):
    part_refs, refs = refs[:count], refs[count:]
    gate_ref, up_ref, down_ref, _, *out_refs, mark_ref = refs
    size = out_refs[0].shape[0]
    step = gate_ref.shape[0] // EXPERT_PARTS
    mark_ref[...] = jnp.zeros(mark_ref.shape, mark_ref.dtype)
    gate, upper = 0.0, 0.0
    for i in range(EXPERT_PARTS):
        ds = pl.ds(i * step, step)
        x = jnp.concatenate([ref[:, ds].astype(jnp.float32) for ref in part_refs], axis=0)
        x = x.astype(jnp.bfloat16)
        gate = gate + jnp.dot(x, gate_ref[ds, :], preferred_element_type=jnp.float32)
        upper = upper + jnp.dot(x, up_ref[ds, :], preferred_element_type=jnp.float32)
    inner = (gate / (1.0 + jnp.exp(-gate)) * upper).astype(jnp.bfloat16)
    for i in range(EXPERT_PARTS):
        ds = pl.ds(i * step, step)
        partial = jnp.dot(inner, down_ref[:, ds], preferred_element_type=jnp.float32)
        for j, ref in enumerate(out_refs):
            ref[:, ds] = partial[j * size : (j + 1) * size].astype(jnp.bfloat16)


def experts(parts, weights, earlier, size):
    depth = parts[0].shape[1]
    count = len(parts)
    rows = sum(part.shape[0] for part in parts)
    outs = rows // size
    vmem = pl.BlockSpec(memory_space=pltpu.VMEM)
    out = pl.pallas_call(
        functools.partial(expert_kernel, count),
        out_shape=[jax.ShapeDtypeStruct((size, depth), jnp.bfloat16)] * outs + [MARK],
        in_specs=[vmem] * (count + 3) + [pl.BlockSpec(memory_space=pl.ANY)],
        out_specs=[vmem] * (outs + 1),
        compiler_params=pltpu.CompilerParams(
            vmem_limit_bytes=(16 << 20) + rows * depth * 8
        ),
        name="experts",
    )(*parts, *weights, earlier)
    return out[:outs], out[outs]


def join_kernel(count, *refs):
    out_ref = refs[-1]
    rows, depth = out_ref.shape
    step = depth // EXPERT_PARTS
    for i in range(EXPERT_PARTS):
        ds = pl.ds(i * step, step)
        joined = jnp.concatenate([ref[:, ds].astype(jnp.float32) for ref in refs[:count]], axis=0)
        out_ref[:, ds] = joined.astype(jnp.bfloat16)


def join(parts, earlier):
    depth = parts[0].shape[1]
    rows = sum(part.shape[0] for part in parts)
    vmem = pl.BlockSpec(memory_space=pltpu.VMEM)
    return pl.pallas_call(
        functools.partial(join_kernel, len(parts)),
        out_shape=jax.ShapeDtypeStruct((rows, depth), jnp.bfloat16),
        in_specs=[vmem] * len(parts) + [pl.BlockSpec(memory_space=pl.ANY)] * len(earlier),
        out_specs=vmem,
        compiler_params=pltpu.CompilerParams(vmem_limit_bytes=(2 << 20) + 8 * rows * depth),
        name="join",
    )(*parts, *earlier)


def add_kernel(count, messages, *refs):
    terms, part_refs = refs[:count], refs[-messages:]
    depth = terms[0].shape[1]
    size = part_refs[0].shape[0]
    step = depth // EXPERT_PARTS
    for i in range(EXPERT_PARTS):
        ds = pl.ds(i * step, step)
        total = terms[0][:, ds].astype(jnp.float32)
        for ref in terms[1:]:
            total = total + ref[:, ds].astype(jnp.float32)
        for m, ref in enumerate(part_refs):
            ref[:, ds] = total[m * size : (m + 1) * size].astype(ref.dtype)


def add(terms, messages, earlier, kind=jnp.bfloat16):
    rows, depth = terms[0].shape
    vmem = pl.BlockSpec(memory_space=pltpu.VMEM)
    return pl.pallas_call(
        functools.partial(add_kernel, len(terms), messages),
        out_shape=[jax.ShapeDtypeStruct((rows // messages, depth), kind)] * messages,
        in_specs=[vmem] * len(terms) + [pl.BlockSpec(memory_space=pl.ANY)] * len(earlier),
        out_specs=[vmem] * messages,
        compiler_params=pltpu.CompilerParams(vmem_limit_bytes=(4 << 20) + 16 * rows * depth),
        name="add",
    )(*terms, *earlier)


def pack_kernel(
    slots,
    deltas,
    table_ref,
    ids_ref,
    replica_ref,
    other_ids_ref,
    other_replica_ref,
    raw_ref,
    other_ref,
    gain_ref,
    normed_ref,
    place_ref,
    choose_ref,
    *refs,
):
    message_refs, raw_v = refs[:-1], refs[-1]
    steps, tokens, depth = raw_ref.shape
    top = ids_ref.shape[1]
    index = lax.axis_index("ep")
    core = lax.rem(index, 2)
    group = lax.div(index, SPAN)
    message_rows = 2 * steps * slots
    for b, ref in enumerate((raw_ref, other_ref)):
        for s in range(steps):
            at = (b * steps + s) * tokens
            raw_v[at : at + tokens, :] = ref[s].astype(jnp.float32)
    raw = raw_v[...]
    mean_square = jnp.mean(raw * raw, axis=1, keepdims=True)
    normed = (raw * lax.rsqrt(mean_square + norm_eps) * gain_ref[...]).astype(jnp.bfloat16)
    normed_ref[...] = normed

    row = lax.broadcasted_iota(jnp.int32, place_ref.shape[1:], 0)
    column = lax.broadcasted_iota(jnp.int32, place_ref.shape[1:], 1)
    expert = lax.broadcasted_iota(jnp.int32, choose_ref.shape[1:], 0)
    token = lax.broadcasted_iota(jnp.int32, choose_ref.shape[1:], 1)
    message = row // message_rows
    target = sum(
        [
            jnp.where(message == m, jnp.where(core == 0, low, high) - m, 0)
            for m, (low, high) in enumerate(deltas)
        ],
        message,
    )
    row = target * message_rows + row % message_rows
    place_row = [jnp.full(place_ref.shape[1:], -1, jnp.int32) for _ in range(top)]
    choice = [jnp.full(choose_ref.shape[1:], -1, jnp.int32) for _ in range(top)]
    for b, (ids, replicas) in enumerate(
        ((ids_ref, replica_ref), (other_ids_ref, other_replica_ref))
    ):
        for s in range(steps):
            block = b * steps + s
            earlier = []
            for t in range(tokens):
                for k in range(top):
                    copy = table_ref[replicas[s, k, t], ids[s, k, t]]
                    slot = sum([(copy == c).astype(jnp.int32) for c in earlier], jnp.int32(0))
                    earlier.append(copy)
                    delta = copy ^ group
                    at = delta * message_rows + block * slots + slot
                    at = jnp.where(slot < slots, at, -1)
                    here = block * tokens + t
                    place_row[k] = jnp.where(column == here, at, place_row[k])
                    choice[k] = jnp.where(token == here, ids[s, k, t], choice[k])
    total = jnp.zeros(place_ref.shape[1:], jnp.float32)
    for k in range(top):
        hit = (place_row[k] == row).astype(jnp.float32)
        place_ref[k] = hit
        choose_ref[k] = (choice[k] == expert).astype(jnp.float32)
        total = total + hit
    packed = jnp.dot(total.astype(jnp.bfloat16), normed, preferred_element_type=jnp.float32)
    for m, ref in enumerate(message_refs):
        ref[...] = packed[m * message_rows : (m + 1) * message_rows].astype(jnp.bfloat16)


def pack(slots, deltas, hidden, other, gain, copy_table, own_choice, other_choice, experts_total):
    steps, tokens, depth = hidden.shape
    top = own_choice[0].shape[1]
    messages = len(deltas)
    message_rows = 2 * steps * slots
    columns = 2 * steps * tokens
    vmem = pl.BlockSpec(memory_space=pltpu.VMEM)
    smem = pl.BlockSpec(memory_space=pltpu.SMEM)
    shape = jax.ShapeDtypeStruct
    out = pl.pallas_call(
        functools.partial(pack_kernel, slots, deltas),
        out_shape=[
            shape((columns, depth), jnp.bfloat16),
            shape((top, messages * message_rows, columns), jnp.float32),
            shape((top, experts_total, columns), jnp.float32),
        ]
        + [shape((message_rows, depth), jnp.bfloat16)] * messages,
        in_specs=[smem] * 5 + [vmem] * 3,
        out_specs=[vmem] * (3 + messages),
        scratch_shapes=[pltpu.VMEM((columns, depth), jnp.float32)],
        compiler_params=pltpu.CompilerParams(
            vmem_limit_bytes=(64 << 20) - (64 << 10)
        ),
        name="pack",
    )(copy_table, *own_choice, *other_choice, hidden, other, gain)
    return out[0], out[1], out[2], out[3:]


def weigh_kernel(normed_ref, router_ref, place_ref, choose_ref, weigh_ref):
    scores = jax.nn.sigmoid(
        lax.dot_general(
            router_ref[...],
            normed_ref[...],
            (((1,), (1,)), ((), ())),
            preferred_element_type=jnp.float32,
        )
    )
    top = place_ref.shape[0]
    picked = [jnp.sum(choose_ref[k] * scores, axis=0, keepdims=True) for k in range(top)]
    total = sum(picked[1:], picked[0])
    weigh = jnp.zeros(weigh_ref.shape, jnp.float32)
    for k in range(top):
        weigh = weigh + place_ref[k] * (routed_scale * picked[k] / total)
    weigh_ref[...] = weigh


def weigh(normed, router_t, place, choose):
    vmem = pl.BlockSpec(memory_space=pltpu.VMEM)
    return pl.pallas_call(
        weigh_kernel,
        out_shape=jax.ShapeDtypeStruct(place.shape[1:], jnp.float32),
        in_specs=[vmem] * 4,
        out_specs=vmem,
        cost_estimate=pl.CostEstimate(
            flops=2 * normed.size * 256, bytes_accessed=2 * normed.size, transcendentals=256
        ),
        compiler_params=pltpu.CompilerParams(vmem_limit_bytes=4 << 20),
        name="weigh",
    )(normed, router_t, place, choose)


def weighted(weights, part_refs):
    high = weights.astype(jnp.bfloat16)
    left = weights - high.astype(jnp.float32)
    middle = left.astype(jnp.bfloat16)
    low = (left - middle.astype(jnp.float32)).astype(jnp.bfloat16)
    rows = jnp.concatenate([ref[...].astype(jnp.float32) for ref in part_refs], axis=0)
    rows = rows.astype(jnp.bfloat16)
    pieces = [
        lax.dot_general(w, rows, (((0,), (0,)), ((), ())), preferred_element_type=jnp.float32)
        for w in (high, middle, low)
    ]
    return pieces[0] + (pieces[1] + pieces[2])


def first_half_kernel(weigh_ref, *refs):
    part_refs, out_ref = refs[:-1], refs[-1]
    out_ref[...] = weighted(weigh_ref[: weigh_ref.shape[0] // 2, :], part_refs)


def second_half_kernel(weigh_ref, first_ref, *refs):
    part_refs, own_ref, send_ref = refs[:-2], refs[-2], refs[-1]
    size = part_refs[0].shape[0]
    weights = weigh_ref[weigh_ref.shape[0] // 2 :, :]
    weights = jnp.concatenate([weights, weights[-size:]], axis=0)
    result = first_ref[...] + weighted(weights, part_refs)
    half = own_ref.shape[0]
    own_ref[...] = result[:half]
    send_ref[...] = result[half:].astype(jnp.bfloat16)


def combine(weights, parts):
    depth = parts[0].shape[1]
    tokens = weights.shape[1]
    vmem = pl.BlockSpec(memory_space=pltpu.VMEM)
    params = pltpu.CompilerParams(vmem_limit_bytes=(8 << 20) + 8 * weights.shape[0] * depth)
    middle = (len(parts) - 1) // 2
    first = pl.pallas_call(
        first_half_kernel,
        out_shape=jax.ShapeDtypeStruct((tokens, depth), jnp.float32),
        in_specs=[vmem] * (1 + middle),
        out_specs=vmem,
        compiler_params=params,
        name="combine",
    )(weights, *parts[:middle])
    return pl.pallas_call(
        second_half_kernel,
        out_shape=[
            jax.ShapeDtypeStruct((tokens // 2, depth), jnp.float32),
            jax.ShapeDtypeStruct((tokens // 2, depth), jnp.bfloat16),
        ],
        in_specs=[vmem] * (2 + len(parts) - middle),
        out_specs=[vmem] * 2,
        compiler_params=params,
        name="combine",
    )(weights, first, *parts[middle:])


def finish_kernel(own_ref, received_ref, out_ref):
    result = own_ref[...] + received_ref[...].astype(jnp.float32)
    steps, tokens, _ = out_ref.shape
    for s in range(steps):
        out_ref[s] = result[s * tokens : (s + 1) * tokens].astype(jnp.bfloat16)


def finish(own, received, shape):
    vmem = pl.BlockSpec(memory_space=pltpu.VMEM)
    return pl.pallas_call(
        finish_kernel,
        out_shape=jax.ShapeDtypeStruct(shape, jnp.bfloat16),
        in_specs=[vmem] * 2,
        out_specs=vmem,
        compiler_params=pltpu.CompilerParams(vmem_limit_bytes=4 << 20),
        name="finish",
    )(own, received)


def mixture(
    hidden, norm_gain, router, expert_ids, replica, copy_table, gate_w, up_w, down_w, attended_mark
):
    groups = lax.axis_size("ep") // SPAN
    messages = groups // 2
    tokens = hidden.shape[1]
    slots = max(2, 2 * tokens * expert_ids.shape[2] // groups)
    deltas = lanes(groups)

    def swapped(value):
        return flipped(value, 1, 1)

    own_choice = (expert_ids.transpose(0, 2, 1), replica.transpose(0, 2, 1))
    other_choice = (swapped(own_choice[0]), swapped(own_choice[1]))
    normed, place, choose, packed = pack(
        slots,
        deltas,
        hidden,
        swapped(hidden),
        norm_gain[None, :],
        copy_table.T,
        own_choice,
        other_choice,
        router.shape[1],
    )

    def rounds(parts):
        return [
            flipped(part, SPAN * low, SPAN * high) for part, (low, high) in zip(parts, deltas)
        ]

    def to_near(part):
        return flipped(part, 0, SPAN)

    def to_far(part):
        return flipped(part, 2, SPAN + 2)

    weights = weigh(normed, router.T, place, choose)
    expert_weights = (gate_w, up_w, down_w)
    half = messages // 2
    size = packed[0].shape[0]
    received = rounds(packed[:-1])
    near_last, far_last = to_near(packed[-1]), to_far(packed[-1])
    held, mark = load(expert_weights, place)
    near = join([*received, near_last], [mark, far_last])
    far = flipped(join(received, [mark, far_last]), 2, 2)
    near_out, mark = experts([near, swapped(near)], held, mark, half * size)
    near_sums = [
        *add([near_out[0], swapped(near_out[2])], half, [], jnp.float32),
        *add([near_out[1], swapped(near_out[3])], half, [], jnp.float32),
    ]
    returned_near = to_near(near_sums[-1].astype(jnp.bfloat16))
    far = join([far], [mark, weights, attended_mark, near_sums[0]])
    far_parts = [far, far_last, swapped(far), swapped(far_last)]
    far_out, mark = experts(far_parts, held, mark, half * size)
    far_sums = [
        *add([far_out[0], swapped(far_out[2])], half, []),
        *add([far_out[1], swapped(far_out[3])], half, []),
    ]
    totals = []
    earlier = [mark]
    for near_sum, far_sum in zip(near_sums[:-1], far_sums[:-1]):
        totals += add([near_sum, flipped(far_sum, 2, 2)], 1, earlier)
        earlier = totals[-1:]
    returned = [*rounds(totals), returned_near, to_far(far_sums[-1])]
    own, send = combine(weights, returned)
    return finish(own, swapped(send), hidden.shape)


def per_device(
    hidden,
    norm_gain,
    router,
    expert_ids,
    replica,
    copy_table,
    gate_w,
    up_w,
    down_w,
    query,
    cache,
    lengths,
    fresh_kv,
):
    attended, attended_mark = attend(query, cache, lengths, fresh_kv)
    moe_out = mixture(
        hidden,
        norm_gain,
        router,
        expert_ids,
        replica,
        copy_table,
        gate_w,
        up_w,
        down_w,
        attended_mark,
    )
    return (attended, moe_out)


def solution(mesh):
    return jax.shard_map(
        per_device,
        mesh=mesh,
        in_specs=(
            P(None, ("groups", "ep"), None),
            P(),
            P(),
            P(None, ("groups", "ep"), None),
            P(None, ("groups", "ep"), None),
            P(),
            P(None, "ep"),
            P(None, "ep"),
            P("ep", None),
            P(None, ("groups", "ep"), None, None),
            P(("groups", "ep"), None, None),
            P(("groups", "ep")),
            P(None, ("groups", "ep"), None),
        ),
        out_specs=(P(None, ("groups", "ep"), None, None), P(None, ("groups", "ep"), None)),
        check_vma=False,
    )
```

```python
import functools

import jax
import jax.numpy as jnp
from jax import lax
from jax.experimental import pallas as pl
from jax.experimental.pallas import tpu as pltpu
from jax.sharding import PartitionSpec as P

KV = 512
SPAN = 4

softmax_scale = 192.0 ** (-0.5)
routed_scale = 2.5
norm_eps = 1e-06
masked_score = -1e30
EXPERT_PARTS = 7
MARK = jax.ShapeDtypeStruct((8, 128), jnp.float32)


def flipped(value, low_core, high_core):
    pairs = [(e, e ^ (high_core if e % 2 else low_core)) for e in range(lax.axis_size("ep"))]
    return lax.ppermute(value, "ep", pairs)


def lanes(groups):
    hops = [(d & 1) + (d >> 1) for d in range(groups)]
    chosen = ([], [])
    for d in sorted(range(2, groups), key=lambda d: (-hops[d], -d)):
        sums = [sum(hops[e] for e in lane) for lane in chosen]
        lane = 0 if sums[0] <= sums[1] else 1
        if 2 * len(chosen[lane]) == groups - 2:
            lane = 1 - lane
        chosen[lane].append(d)
    return [*zip(*chosen), (0, 1)]


def attend_kernel(lengths_ref, query_ref, cache_ref, fresh_ref, out_ref, mark_ref):
    mark_ref[...] = jnp.zeros(mark_ref.shape, mark_ref.dtype)
    steps, tokens, heads, _ = query_ref.shape
    slots = cache_ref.shape[1]
    pad = 128 - slots
    for n in range(tokens):
        row = lax.broadcasted_iota(jnp.int32, (pad, 1), 0)
        extra = jnp.zeros((pad, fresh_ref.shape[2]), jnp.float32)
        for s in range(steps):
            block = fresh_ref[s].astype(jnp.float32)
            which = lax.broadcasted_iota(jnp.int32, block.shape, 0) == n
            one = jnp.sum(jnp.where(which, block, 0.0), axis=0, keepdims=True)
            extra = jnp.where(row == s, one, extra)
        keys = jnp.concatenate([cache_ref[n], extra.astype(jnp.bfloat16)], axis=0)
        queries = jnp.concatenate([query_ref[s, n] for s in range(steps)], axis=0)
        scores = (
            lax.dot_general(
                queries, keys, (((1,), (1,)), ((), ())), preferred_element_type=jnp.float32
            )
            * softmax_scale
        )
        position = lax.broadcasted_iota(jnp.int32, scores.shape, 1)
        step = lax.broadcasted_iota(jnp.int32, scores.shape, 0) // heads
        valid = (position < lengths_ref[n]) | (
            (position >= slots) & (position - slots <= step)
        )
        scores = jnp.where(valid, scores, masked_score)
        terms = jnp.exp(scores - jnp.max(scores, axis=1, keepdims=True))
        terms = jnp.where(valid, terms, 0.0)
        probs = (terms / jnp.sum(terms, axis=1, keepdims=True)).astype(jnp.bfloat16)
        mixed = jnp.dot(probs, keys[:, :KV], preferred_element_type=jnp.float32)
        for s in range(steps):
            out_ref[s, n] = mixed[s * heads : (s + 1) * heads].astype(jnp.bfloat16)


def attend(query, cache, lengths, fresh):
    steps, tokens, heads, width = query.shape
    vmem = pl.BlockSpec(memory_space=pltpu.VMEM)
    return pl.pallas_call(
        attend_kernel,
        out_shape=[jax.ShapeDtypeStruct((steps, tokens, heads, KV), jnp.bfloat16), MARK],
        in_specs=[pl.BlockSpec(memory_space=pltpu.SMEM)] + [vmem] * 3,
        out_specs=[vmem] * 2,
        compiler_params=pltpu.CompilerParams(vmem_limit_bytes=12 << 20),
        cost_estimate=pl.CostEstimate(
            flops=4 * steps * tokens * heads * 128 * width,
            bytes_accessed=2 * (2 * query.size + cache.size),
            transcendentals=steps * tokens * heads * 128,
        ),
        name="attention",
    )(lengths, query, cache, fresh)


def load_kernel(gate_ref, up_ref, down_ref, _, gate_v, up_v, down_v, mark_ref, sems):
    copies = [
        pltpu.make_async_copy(source, target, sems.at[i])
        for i, (source, target) in enumerate(
            ((gate_ref, gate_v), (up_ref, up_v), (down_ref, down_v))
        )
    ]
    for copy in copies:
        copy.start()
    mark_ref[...] = jnp.zeros(mark_ref.shape, mark_ref.dtype)
    for copy in copies:
        copy.wait()


def load(weights, earlier):
    vmem = pl.BlockSpec(memory_space=pltpu.VMEM)
    anywhere = pl.BlockSpec(memory_space=pl.ANY)
    *held, mark = pl.pallas_call(
        load_kernel,
        out_shape=[jax.ShapeDtypeStruct(w.shape, w.dtype) for w in weights] + [MARK],
        in_specs=[anywhere] * 4,
        out_specs=[vmem] * 4,
        scratch_shapes=[pltpu.SemaphoreType.DMA((3,))],
        compiler_params=pltpu.CompilerParams(vmem_limit_bytes=40 << 20),
        name="load",
    )(*weights, earlier)
    return held, mark


def expert_kernel(count, *refs):
    part_refs, refs = refs[:count], refs[count:]
    gate_ref, up_ref, down_ref, _, *out_refs, mark_ref = refs
    size = out_refs[0].shape[0]
    step = gate_ref.shape[0] // EXPERT_PARTS
    mark_ref[...] = jnp.zeros(mark_ref.shape, mark_ref.dtype)
    gate, upper = 0.0, 0.0
    for i in range(EXPERT_PARTS):
        ds = pl.ds(i * step, step)
        x = jnp.concatenate([ref[:, ds].astype(jnp.float32) for ref in part_refs], axis=0)
        x = x.astype(jnp.bfloat16)
        gate = gate + jnp.dot(x, gate_ref[ds, :], preferred_element_type=jnp.float32)
        upper = upper + jnp.dot(x, up_ref[ds, :], preferred_element_type=jnp.float32)
    inner = (gate / (1.0 + jnp.exp(-gate)) * upper).astype(jnp.bfloat16)
    for i in range(EXPERT_PARTS):
        ds = pl.ds(i * step, step)
        partial = jnp.dot(inner, down_ref[:, ds], preferred_element_type=jnp.float32)
        for j, ref in enumerate(out_refs):
            ref[:, ds] = partial[j * size : (j + 1) * size].astype(jnp.bfloat16)


def experts(parts, weights, earlier, size):
    depth = parts[0].shape[1]
    count = len(parts)
    rows = sum(part.shape[0] for part in parts)
    outs = rows // size
    vmem = pl.BlockSpec(memory_space=pltpu.VMEM)
    out = pl.pallas_call(
        functools.partial(expert_kernel, count),
        out_shape=[jax.ShapeDtypeStruct((size, depth), jnp.bfloat16)] * outs + [MARK],
        in_specs=[vmem] * (count + 3) + [pl.BlockSpec(memory_space=pl.ANY)],
        out_specs=[vmem] * (outs + 1),
        compiler_params=pltpu.CompilerParams(
            vmem_limit_bytes=(16 << 20) + rows * depth * 8
        ),
        name="experts",
    )(*parts, *weights, earlier)
    return out[:outs], out[outs]


def join_kernel(count, *refs):
    out_ref = refs[-1]
    rows, depth = out_ref.shape
    step = depth // EXPERT_PARTS
    for i in range(EXPERT_PARTS):
        ds = pl.ds(i * step, step)
        joined = jnp.concatenate([ref[:, ds].astype(jnp.float32) for ref in refs[:count]], axis=0)
        out_ref[:, ds] = joined.astype(jnp.bfloat16)


def join(parts, earlier):
    depth = parts[0].shape[1]
    rows = sum(part.shape[0] for part in parts)
    vmem = pl.BlockSpec(memory_space=pltpu.VMEM)
    return pl.pallas_call(
        functools.partial(join_kernel, len(parts)),
        out_shape=jax.ShapeDtypeStruct((rows, depth), jnp.bfloat16),
        in_specs=[vmem] * len(parts) + [pl.BlockSpec(memory_space=pl.ANY)] * len(earlier),
        out_specs=vmem,
        compiler_params=pltpu.CompilerParams(vmem_limit_bytes=(2 << 20) + 8 * rows * depth),
        name="join",
    )(*parts, *earlier)


def add_kernel(count, messages, *refs):
    terms, part_refs = refs[:count], refs[-messages:]
    depth = terms[0].shape[1]
    size = part_refs[0].shape[0]
    step = depth // EXPERT_PARTS
    for i in range(EXPERT_PARTS):
        ds = pl.ds(i * step, step)
        total = terms[0][:, ds].astype(jnp.float32)
        for ref in terms[1:]:
            total = total + ref[:, ds].astype(jnp.float32)
        for m, ref in enumerate(part_refs):
            ref[:, ds] = total[m * size : (m + 1) * size].astype(ref.dtype)


def add(terms, messages, earlier, kind=jnp.bfloat16):
    rows, depth = terms[0].shape
    vmem = pl.BlockSpec(memory_space=pltpu.VMEM)
    return pl.pallas_call(
        functools.partial(add_kernel, len(terms), messages),
        out_shape=[jax.ShapeDtypeStruct((rows // messages, depth), kind)] * messages,
        in_specs=[vmem] * len(terms) + [pl.BlockSpec(memory_space=pl.ANY)] * len(earlier),
        out_specs=[vmem] * messages,
        compiler_params=pltpu.CompilerParams(vmem_limit_bytes=(4 << 20) + 16 * rows * depth),
        name="add",
    )(*terms, *earlier)


def pack_kernel(
    slots,
    deltas,
    table_ref,
    ids_ref,
    replica_ref,
    other_ids_ref,
    other_replica_ref,
    raw_ref,
    other_ref,
    gain_ref,
    normed_ref,
    place_ref,
    choose_ref,
    *refs,
):
    message_refs, raw_v = refs[:-1], refs[-1]
    steps, tokens, depth = raw_ref.shape
    top = ids_ref.shape[1]
    index = lax.axis_index("ep")
    core = lax.rem(index, 2)
    group = lax.div(index, SPAN)
    message_rows = 2 * steps * slots
    for b, ref in enumerate((raw_ref, other_ref)):
        for s in range(steps):
            at = (b * steps + s) * tokens
            raw_v[at : at + tokens, :] = ref[s].astype(jnp.float32)
    raw = raw_v[...]
    mean_square = jnp.mean(raw * raw, axis=1, keepdims=True)
    normed = (raw * lax.rsqrt(mean_square + norm_eps) * gain_ref[...]).astype(jnp.bfloat16)
    normed_ref[...] = normed

    row = lax.broadcasted_iota(jnp.int32, place_ref.shape[1:], 0)
    column = lax.broadcasted_iota(jnp.int32, place_ref.shape[1:], 1)
    expert = lax.broadcasted_iota(jnp.int32, choose_ref.shape[1:], 0)
    token = lax.broadcasted_iota(jnp.int32, choose_ref.shape[1:], 1)
    message = row // message_rows
    target = sum(
        [
            jnp.where(message == m, jnp.where(core == 0, low, high) - m, 0)
            for m, (low, high) in enumerate(deltas)
        ],
        message,
    )
    row = target * message_rows + row % message_rows
    place_row = [jnp.full(place_ref.shape[1:], -1, jnp.int32) for _ in range(top)]
    choice = [jnp.full(choose_ref.shape[1:], -1, jnp.int32) for _ in range(top)]
    for b, (ids, replicas) in enumerate(
        ((ids_ref, replica_ref), (other_ids_ref, other_replica_ref))
    ):
        for s in range(steps):
            block = b * steps + s
            earlier = []
            for t in range(tokens):
                for k in range(top):
                    copy = table_ref[replicas[s, k, t], ids[s, k, t]]
                    slot = sum([(copy == c).astype(jnp.int32) for c in earlier], jnp.int32(0))
                    earlier.append(copy)
                    delta = copy ^ group
                    at = delta * message_rows + block * slots + slot
                    at = jnp.where(slot < slots, at, -1)
                    here = block * tokens + t
                    place_row[k] = jnp.where(column == here, at, place_row[k])
                    choice[k] = jnp.where(token == here, ids[s, k, t], choice[k])
    total = jnp.zeros(place_ref.shape[1:], jnp.float32)
    for k in range(top):
        hit = (place_row[k] == row).astype(jnp.float32)
        place_ref[k] = hit
        choose_ref[k] = (choice[k] == expert).astype(jnp.float32)
        total = total + hit
    packed = jnp.dot(total.astype(jnp.bfloat16), normed, preferred_element_type=jnp.float32)
    for m, ref in enumerate(message_refs):
        ref[...] = packed[m * message_rows : (m + 1) * message_rows].astype(jnp.bfloat16)


def pack(slots, deltas, hidden, other, gain, copy_table, own_choice, other_choice, experts_total):
    steps, tokens, depth = hidden.shape
    top = own_choice[0].shape[1]
    messages = len(deltas)
    message_rows = 2 * steps * slots
    columns = 2 * steps * tokens
    vmem = pl.BlockSpec(memory_space=pltpu.VMEM)
    smem = pl.BlockSpec(memory_space=pltpu.SMEM)
    shape = jax.ShapeDtypeStruct
    out = pl.pallas_call(
        functools.partial(pack_kernel, slots, deltas),
        out_shape=[
            shape((columns, depth), jnp.bfloat16),
            shape((top, messages * message_rows, columns), jnp.float32),
            shape((top, experts_total, columns), jnp.float32),
        ]
        + [shape((message_rows, depth), jnp.bfloat16)] * messages,
        in_specs=[smem] * 5 + [vmem] * 3,
        out_specs=[vmem] * (3 + messages),
        scratch_shapes=[pltpu.VMEM((columns, depth), jnp.float32)],
        compiler_params=pltpu.CompilerParams(
            vmem_limit_bytes=(64 << 20) - (64 << 10)
        ),
        name="pack",
    )(copy_table, *own_choice, *other_choice, hidden, other, gain)
    return out[0], out[1], out[2], out[3:]


def weigh_kernel(normed_ref, router_ref, place_ref, choose_ref, weigh_ref):
    scores = jax.nn.sigmoid(
        lax.dot_general(
            router_ref[...],
            normed_ref[...],
            (((1,), (1,)), ((), ())),
            preferred_element_type=jnp.float32,
        )
    )
    top = place_ref.shape[0]
    picked = [jnp.sum(choose_ref[k] * scores, axis=0, keepdims=True) for k in range(top)]
    total = sum(picked[1:], picked[0])
    weigh = jnp.zeros(weigh_ref.shape, jnp.float32)
    for k in range(top):
        weigh = weigh + place_ref[k] * (routed_scale * picked[k] / total)
    weigh_ref[...] = weigh


def weigh(normed, router_t, place, choose):
    vmem = pl.BlockSpec(memory_space=pltpu.VMEM)
    return pl.pallas_call(
        weigh_kernel,
        out_shape=jax.ShapeDtypeStruct(place.shape[1:], jnp.float32),
        in_specs=[vmem] * 4,
        out_specs=vmem,
        cost_estimate=pl.CostEstimate(
            flops=2 * normed.size * 256, bytes_accessed=2 * normed.size, transcendentals=256
        ),
        compiler_params=pltpu.CompilerParams(vmem_limit_bytes=4 << 20),
        name="weigh",
    )(normed, router_t, place, choose)


def weighted(weights, part_refs):
    high = weights.astype(jnp.bfloat16)
    low = (weights - high.astype(jnp.float32)).astype(jnp.bfloat16)
    rows = jnp.concatenate([ref[...].astype(jnp.float32) for ref in part_refs], axis=0)
    rows = rows.astype(jnp.bfloat16)
    pieces = [
        lax.dot_general(w, rows, (((0,), (0,)), ((), ())), preferred_element_type=jnp.float32)
        for w in (high, low)
    ]
    return pieces[0] + pieces[1]


def first_half_kernel(weigh_ref, *refs):
    part_refs, out_ref = refs[:-1], refs[-1]
    out_ref[...] = weighted(weigh_ref[: weigh_ref.shape[0] // 2, :], part_refs)


def second_half_kernel(weigh_ref, first_ref, *refs):
    part_refs, own_ref, send_ref = refs[:-2], refs[-2], refs[-1]
    size = part_refs[0].shape[0]
    weights = weigh_ref[weigh_ref.shape[0] // 2 :, :]
    weights = jnp.concatenate([weights, weights[-size:]], axis=0)
    result = first_ref[...] + weighted(weights, part_refs)
    half = own_ref.shape[0]
    own_ref[...] = result[:half]
    send_ref[...] = result[half:].astype(jnp.bfloat16)


def combine(weights, parts):
    depth = parts[0].shape[1]
    tokens = weights.shape[1]
    vmem = pl.BlockSpec(memory_space=pltpu.VMEM)
    params = pltpu.CompilerParams(vmem_limit_bytes=(8 << 20) + 8 * weights.shape[0] * depth)
    middle = (len(parts) - 1) // 2
    first = pl.pallas_call(
        first_half_kernel,
        out_shape=jax.ShapeDtypeStruct((tokens, depth), jnp.float32),
        in_specs=[vmem] * (1 + middle),
        out_specs=vmem,
        compiler_params=params,
        name="combine",
    )(weights, *parts[:middle])
    return pl.pallas_call(
        second_half_kernel,
        out_shape=[
            jax.ShapeDtypeStruct((tokens // 2, depth), jnp.float32),
            jax.ShapeDtypeStruct((tokens // 2, depth), jnp.bfloat16),
        ],
        in_specs=[vmem] * (2 + len(parts) - middle),
        out_specs=[vmem] * 2,
        compiler_params=params,
        name="combine",
    )(weights, first, *parts[middle:])


def finish_kernel(own_ref, received_ref, out_ref):
    result = own_ref[...] + received_ref[...].astype(jnp.float32)
    steps, tokens, _ = out_ref.shape
    for s in range(steps):
        out_ref[s] = result[s * tokens : (s + 1) * tokens].astype(jnp.bfloat16)


def finish(own, received, shape):
    vmem = pl.BlockSpec(memory_space=pltpu.VMEM)
    return pl.pallas_call(
        finish_kernel,
        out_shape=jax.ShapeDtypeStruct(shape, jnp.bfloat16),
        in_specs=[vmem] * 2,
        out_specs=vmem,
        compiler_params=pltpu.CompilerParams(vmem_limit_bytes=4 << 20),
        name="finish",
    )(own, received)


def mixture(
    hidden, norm_gain, router, expert_ids, replica, copy_table, gate_w, up_w, down_w, attended_mark
):
    groups = lax.axis_size("ep") // SPAN
    messages = groups // 2
    tokens = hidden.shape[1]
    slots = max(2, 2 * tokens * expert_ids.shape[2] // groups)
    deltas = lanes(groups)

    def swapped(value):
        return flipped(value, 1, 1)

    own_choice = (expert_ids.transpose(0, 2, 1), replica.transpose(0, 2, 1))
    other_choice = (swapped(own_choice[0]), swapped(own_choice[1]))
    normed, place, choose, packed = pack(
        slots,
        deltas,
        hidden,
        swapped(hidden),
        norm_gain[None, :],
        copy_table.T,
        own_choice,
        other_choice,
        router.shape[1],
    )

    def rounds(parts):
        return [
            flipped(part, SPAN * low, SPAN * high) for part, (low, high) in zip(parts, deltas)
        ]

    def to_near(part):
        return flipped(part, 0, SPAN)

    def to_far(part):
        return flipped(part, 2, SPAN + 2)

    weights = weigh(normed, router.T, place, choose)
    expert_weights = (gate_w, up_w, down_w)
    half = messages // 2
    size = packed[0].shape[0]
    received = rounds(packed[:-1])
    near_last, far_last = to_near(packed[-1]), to_far(packed[-1])
    held, mark = load(expert_weights, place)
    near = join([*received, near_last], [mark, far_last])
    far = flipped(join(received, [mark, far_last]), 2, 2)
    near_out, mark = experts([near, swapped(near)], held, mark, half * size)
    near_sums = [
        *add([near_out[0], swapped(near_out[2])], half, [], jnp.float32),
        *add([near_out[1], swapped(near_out[3])], half, [], jnp.float32),
    ]
    returned_near = to_near(near_sums[-1].astype(jnp.bfloat16))
    far = join([far], [mark, weights, attended_mark, near_sums[0]])
    far_parts = [far, far_last, swapped(far), swapped(far_last)]
    far_out, mark = experts(far_parts, held, mark, half * size)
    far_sums = [
        *add([far_out[0], swapped(far_out[2])], half, []),
        *add([far_out[1], swapped(far_out[3])], half, []),
    ]
    totals = []
    earlier = [mark]
    for near_sum, far_sum in zip(near_sums[:-1], far_sums[:-1]):
        totals += add([near_sum, flipped(far_sum, 2, 2)], 1, earlier)
        earlier = totals[-1:]
    returned = [*rounds(totals), returned_near, to_far(far_sums[-1])]
    own, send = combine(weights, returned)
    return finish(own, swapped(send), hidden.shape)


def per_device(
    hidden,
    norm_gain,
    router,
    expert_ids,
    replica,
    copy_table,
    gate_w,
    up_w,
    down_w,
    query,
    cache,
    lengths,
    fresh_kv,
):
    attended, attended_mark = attend(query, cache, lengths, fresh_kv)
    moe_out = mixture(
        hidden,
        norm_gain,
        router,
        expert_ids,
        replica,
        copy_table,
        gate_w,
        up_w,
        down_w,
        attended_mark,
    )
    return (attended, moe_out)


def solution(mesh):
    return jax.shard_map(
        per_device,
        mesh=mesh,
        in_specs=(
            P(None, ("groups", "ep"), None),
            P(),
            P(),
            P(None, ("groups", "ep"), None),
            P(None, ("groups", "ep"), None),
            P(),
            P(None, "ep"),
            P(None, "ep"),
            P("ep", None),
            P(None, ("groups", "ep"), None, None),
            P(("groups", "ep"), None, None),
            P(("groups", "ep")),
            P(None, ("groups", "ep"), None),
        ),
        out_specs=(P(None, ("groups", "ep"), None, None), P(None, ("groups", "ep"), None)),
        check_vma=False,
    )
```

```python
import functools

import jax
import jax.numpy as jnp
from jax import lax
from jax.experimental import pallas as pl
from jax.experimental.pallas import tpu as pltpu
from jax.sharding import PartitionSpec as P

KV = 512
SPAN = 4

softmax_scale = 192.0 ** (-0.5)
routed_scale = 2.5
norm_eps = 1e-06
masked_score = -1e30
EXPERT_PARTS = 4
MARK = jax.ShapeDtypeStruct((8, 128), jnp.float32)


def flipped(value, low_core, high_core):
    pairs = [(e, e ^ (high_core if e % 2 else low_core)) for e in range(lax.axis_size("ep"))]
    return lax.ppermute(value, "ep", pairs)


def lanes(groups):
    hops = [(d & 1) + (d >> 1) for d in range(groups)]
    chosen = ([], [])
    for d in sorted(range(2, groups), key=lambda d: (-hops[d], -d)):
        sums = [sum(hops[e] for e in lane) for lane in chosen]
        lane = 0 if sums[0] <= sums[1] else 1
        if 2 * len(chosen[lane]) == groups - 2:
            lane = 1 - lane
        chosen[lane].append(d)
    return [*zip(*chosen), (0, 1)]


def attend_kernel(lengths_ref, query_ref, cache_ref, fresh_ref, out_ref, mark_ref):
    mark_ref[...] = jnp.zeros(mark_ref.shape, mark_ref.dtype)
    steps, tokens, heads, _ = query_ref.shape
    slots = cache_ref.shape[1]
    pad = 128 - slots
    for n in range(tokens):
        row = lax.broadcasted_iota(jnp.int32, (pad, 1), 0)
        extra = jnp.zeros((pad, fresh_ref.shape[2]), jnp.float32)
        for s in range(steps):
            block = fresh_ref[s].astype(jnp.float32)
            which = lax.broadcasted_iota(jnp.int32, block.shape, 0) == n
            one = jnp.sum(jnp.where(which, block, 0.0), axis=0, keepdims=True)
            extra = jnp.where(row == s, one, extra)
        keys = jnp.concatenate([cache_ref[n], extra.astype(jnp.bfloat16)], axis=0)
        queries = jnp.concatenate([query_ref[s, n] for s in range(steps)], axis=0)
        scores = (
            lax.dot_general(
                queries, keys, (((1,), (1,)), ((), ())), preferred_element_type=jnp.float32
            )
            * softmax_scale
        )
        position = lax.broadcasted_iota(jnp.int32, scores.shape, 1)
        step = lax.broadcasted_iota(jnp.int32, scores.shape, 0) // heads
        valid = (position < lengths_ref[n]) | (
            (position >= slots) & (position - slots <= step)
        )
        scores = jnp.where(valid, scores, masked_score)
        terms = jnp.exp(scores - jnp.max(scores, axis=1, keepdims=True))
        terms = jnp.where(valid, terms, 0.0)
        probs = (terms / jnp.sum(terms, axis=1, keepdims=True)).astype(jnp.bfloat16)
        mixed = jnp.dot(probs, keys[:, :KV], preferred_element_type=jnp.float32)
        for s in range(steps):
            out_ref[s, n] = mixed[s * heads : (s + 1) * heads].astype(jnp.bfloat16)


def attend(query, cache, lengths, fresh):
    steps, tokens, heads, width = query.shape
    vmem = pl.BlockSpec(memory_space=pltpu.VMEM)
    return pl.pallas_call(
        attend_kernel,
        out_shape=[jax.ShapeDtypeStruct((steps, tokens, heads, KV), jnp.bfloat16), MARK],
        in_specs=[pl.BlockSpec(memory_space=pltpu.SMEM)] + [vmem] * 3,
        out_specs=[vmem] * 2,
        compiler_params=pltpu.CompilerParams(vmem_limit_bytes=12 << 20),
        cost_estimate=pl.CostEstimate(
            flops=4 * steps * tokens * heads * 128 * width,
            bytes_accessed=2 * (2 * query.size + cache.size),
            transcendentals=steps * tokens * heads * 128,
        ),
        name="attention",
    )(lengths, query, cache, fresh)


def load_kernel(gate_ref, up_ref, down_ref, _, gate_v, up_v, down_v, mark_ref, sems):
    copies = [
        pltpu.make_async_copy(source, target, sems.at[i])
        for i, (source, target) in enumerate(
            ((gate_ref, gate_v), (up_ref, up_v), (down_ref, down_v))
        )
    ]
    for copy in copies:
        copy.start()
    mark_ref[...] = jnp.zeros(mark_ref.shape, mark_ref.dtype)
    for copy in copies:
        copy.wait()


def load(weights, earlier):
    vmem = pl.BlockSpec(memory_space=pltpu.VMEM)
    anywhere = pl.BlockSpec(memory_space=pl.ANY)
    *held, mark = pl.pallas_call(
        load_kernel,
        out_shape=[jax.ShapeDtypeStruct(w.shape, w.dtype) for w in weights] + [MARK],
        in_specs=[anywhere] * 4,
        out_specs=[vmem] * 4,
        scratch_shapes=[pltpu.SemaphoreType.DMA((3,))],
        compiler_params=pltpu.CompilerParams(vmem_limit_bytes=40 << 20),
        name="load",
    )(*weights, earlier)
    return held, mark


def expert_kernel(count, *refs):
    part_refs, refs = refs[:count], refs[count:]
    gate_ref, up_ref, down_ref, _, *out_refs, mark_ref = refs
    size = out_refs[0].shape[0]
    step = gate_ref.shape[0] // EXPERT_PARTS
    mark_ref[...] = jnp.zeros(mark_ref.shape, mark_ref.dtype)
    gate, upper = 0.0, 0.0
    for i in range(EXPERT_PARTS):
        ds = pl.ds(i * step, step)
        x = jnp.concatenate([ref[:, ds].astype(jnp.float32) for ref in part_refs], axis=0)
        x = x.astype(jnp.bfloat16)
        gate = gate + jnp.dot(x, gate_ref[ds, :], preferred_element_type=jnp.float32)
        upper = upper + jnp.dot(x, up_ref[ds, :], preferred_element_type=jnp.float32)
    inner = (gate / (1.0 + jnp.exp(-gate)) * upper).astype(jnp.bfloat16)
    for i in range(EXPERT_PARTS):
        ds = pl.ds(i * step, step)
        partial = jnp.dot(inner, down_ref[:, ds], preferred_element_type=jnp.float32)
        for j, ref in enumerate(out_refs):
            ref[:, ds] = partial[j * size : (j + 1) * size].astype(jnp.bfloat16)


def experts(parts, weights, earlier, size):
    depth = parts[0].shape[1]
    count = len(parts)
    rows = sum(part.shape[0] for part in parts)
    outs = rows // size
    vmem = pl.BlockSpec(memory_space=pltpu.VMEM)
    out = pl.pallas_call(
        functools.partial(expert_kernel, count),
        out_shape=[jax.ShapeDtypeStruct((size, depth), jnp.bfloat16)] * outs + [MARK],
        in_specs=[vmem] * (count + 3) + [pl.BlockSpec(memory_space=pl.ANY)],
        out_specs=[vmem] * (outs + 1),
        compiler_params=pltpu.CompilerParams(
            vmem_limit_bytes=(16 << 20) + rows * depth * 8
        ),
        name="experts",
    )(*parts, *weights, earlier)
    return out[:outs], out[outs]


def join_kernel(count, *refs):
    out_ref = refs[-1]
    rows, depth = out_ref.shape
    step = depth // EXPERT_PARTS
    for i in range(EXPERT_PARTS):
        ds = pl.ds(i * step, step)
        joined = jnp.concatenate([ref[:, ds].astype(jnp.float32) for ref in refs[:count]], axis=0)
        out_ref[:, ds] = joined.astype(jnp.bfloat16)


def join(parts, earlier):
    depth = parts[0].shape[1]
    rows = sum(part.shape[0] for part in parts)
    vmem = pl.BlockSpec(memory_space=pltpu.VMEM)
    return pl.pallas_call(
        functools.partial(join_kernel, len(parts)),
        out_shape=jax.ShapeDtypeStruct((rows, depth), jnp.bfloat16),
        in_specs=[vmem] * len(parts) + [pl.BlockSpec(memory_space=pl.ANY)] * len(earlier),
        out_specs=vmem,
        compiler_params=pltpu.CompilerParams(vmem_limit_bytes=(2 << 20) + 8 * rows * depth),
        name="join",
    )(*parts, *earlier)


def add_kernel(count, messages, *refs):
    terms, part_refs = refs[:count], refs[-messages:]
    depth = terms[0].shape[1]
    size = part_refs[0].shape[0]
    step = depth // EXPERT_PARTS
    for i in range(EXPERT_PARTS):
        ds = pl.ds(i * step, step)
        total = terms[0][:, ds].astype(jnp.float32)
        for ref in terms[1:]:
            total = total + ref[:, ds].astype(jnp.float32)
        for m, ref in enumerate(part_refs):
            ref[:, ds] = total[m * size : (m + 1) * size].astype(ref.dtype)


def add(terms, messages, earlier, kind=jnp.bfloat16):
    rows, depth = terms[0].shape
    vmem = pl.BlockSpec(memory_space=pltpu.VMEM)
    return pl.pallas_call(
        functools.partial(add_kernel, len(terms), messages),
        out_shape=[jax.ShapeDtypeStruct((rows // messages, depth), kind)] * messages,
        in_specs=[vmem] * len(terms) + [pl.BlockSpec(memory_space=pl.ANY)] * len(earlier),
        out_specs=[vmem] * messages,
        compiler_params=pltpu.CompilerParams(vmem_limit_bytes=(4 << 20) + 16 * rows * depth),
        name="add",
    )(*terms, *earlier)


def pack_kernel(
    slots,
    deltas,
    table_ref,
    ids_ref,
    replica_ref,
    other_ids_ref,
    other_replica_ref,
    raw_ref,
    other_ref,
    gain_ref,
    normed_ref,
    place_ref,
    choose_ref,
    *refs,
):
    message_refs, raw_v = refs[:-1], refs[-1]
    steps, tokens, depth = raw_ref.shape
    top = ids_ref.shape[1]
    index = lax.axis_index("ep")
    core = lax.rem(index, 2)
    group = lax.div(index, SPAN)
    message_rows = 2 * steps * slots
    for b, ref in enumerate((raw_ref, other_ref)):
        for s in range(steps):
            at = (b * steps + s) * tokens
            raw_v[at : at + tokens, :] = ref[s].astype(jnp.float32)
    raw = raw_v[...]
    mean_square = jnp.mean(raw * raw, axis=1, keepdims=True)
    normed = (raw * lax.rsqrt(mean_square + norm_eps) * gain_ref[...]).astype(jnp.bfloat16)
    normed_ref[...] = normed

    row = lax.broadcasted_iota(jnp.int32, place_ref.shape[1:], 0)
    column = lax.broadcasted_iota(jnp.int32, place_ref.shape[1:], 1)
    expert = lax.broadcasted_iota(jnp.int32, choose_ref.shape[1:], 0)
    token = lax.broadcasted_iota(jnp.int32, choose_ref.shape[1:], 1)
    message = row // message_rows
    target = sum(
        [
            jnp.where(message == m, jnp.where(core == 0, low, high) - m, 0)
            for m, (low, high) in enumerate(deltas)
        ],
        message,
    )
    row = target * message_rows + row % message_rows
    place_row = [jnp.full(place_ref.shape[1:], -1, jnp.int32) for _ in range(top)]
    choice = [jnp.full(choose_ref.shape[1:], -1, jnp.int32) for _ in range(top)]
    for b, (ids, replicas) in enumerate(
        ((ids_ref, replica_ref), (other_ids_ref, other_replica_ref))
    ):
        for s in range(steps):
            block = b * steps + s
            earlier = []
            for t in range(tokens):
                for k in range(top):
                    copy = table_ref[replicas[s, k, t], ids[s, k, t]]
                    slot = sum([(copy == c).astype(jnp.int32) for c in earlier], jnp.int32(0))
                    earlier.append(copy)
                    delta = copy ^ group
                    at = delta * message_rows + block * slots + slot
                    at = jnp.where(slot < slots, at, -1)
                    here = block * tokens + t
                    place_row[k] = jnp.where(column == here, at, place_row[k])
                    choice[k] = jnp.where(token == here, ids[s, k, t], choice[k])
    total = jnp.zeros(place_ref.shape[1:], jnp.float32)
    for k in range(top):
        hit = (place_row[k] == row).astype(jnp.float32)
        place_ref[k] = hit
        choose_ref[k] = (choice[k] == expert).astype(jnp.float32)
        total = total + hit
    packed = jnp.dot(total.astype(jnp.bfloat16), normed, preferred_element_type=jnp.float32)
    for m, ref in enumerate(message_refs):
        ref[...] = packed[m * message_rows : (m + 1) * message_rows].astype(jnp.bfloat16)


def pack(slots, deltas, hidden, other, gain, copy_table, own_choice, other_choice, experts_total):
    steps, tokens, depth = hidden.shape
    top = own_choice[0].shape[1]
    messages = len(deltas)
    message_rows = 2 * steps * slots
    columns = 2 * steps * tokens
    vmem = pl.BlockSpec(memory_space=pltpu.VMEM)
    smem = pl.BlockSpec(memory_space=pltpu.SMEM)
    shape = jax.ShapeDtypeStruct
    out = pl.pallas_call(
        functools.partial(pack_kernel, slots, deltas),
        out_shape=[
            shape((columns, depth), jnp.bfloat16),
            shape((top, messages * message_rows, columns), jnp.float32),
            shape((top, experts_total, columns), jnp.float32),
        ]
        + [shape((message_rows, depth), jnp.bfloat16)] * messages,
        in_specs=[smem] * 5 + [vmem] * 3,
        out_specs=[vmem] * (3 + messages),
        scratch_shapes=[pltpu.VMEM((columns, depth), jnp.float32)],
        compiler_params=pltpu.CompilerParams(
            vmem_limit_bytes=(64 << 20) - (64 << 10)
        ),
        name="pack",
    )(copy_table, *own_choice, *other_choice, hidden, other, gain)
    return out[0], out[1], out[2], out[3:]


def weigh_kernel(normed_ref, router_ref, place_ref, choose_ref, weigh_ref):
    scores = jax.nn.sigmoid(
        lax.dot_general(
            router_ref[...],
            normed_ref[...],
            (((1,), (1,)), ((), ())),
            preferred_element_type=jnp.float32,
        )
    )
    top = place_ref.shape[0]
    picked = [jnp.sum(choose_ref[k] * scores, axis=0, keepdims=True) for k in range(top)]
    total = sum(picked[1:], picked[0])
    weigh = jnp.zeros(weigh_ref.shape, jnp.float32)
    for k in range(top):
        weigh = weigh + place_ref[k] * (routed_scale * picked[k] / total)
    weigh_ref[...] = weigh


def weigh(normed, router_t, place, choose):
    vmem = pl.BlockSpec(memory_space=pltpu.VMEM)
    return pl.pallas_call(
        weigh_kernel,
        out_shape=jax.ShapeDtypeStruct(place.shape[1:], jnp.float32),
        in_specs=[vmem] * 4,
        out_specs=vmem,
        cost_estimate=pl.CostEstimate(
            flops=2 * normed.size * 256, bytes_accessed=2 * normed.size, transcendentals=256
        ),
        compiler_params=pltpu.CompilerParams(vmem_limit_bytes=4 << 20),
        name="weigh",
    )(normed, router_t, place, choose)


def weighted(weights, part_refs):
    high = weights.astype(jnp.bfloat16)
    left = weights - high.astype(jnp.float32)
    middle = left.astype(jnp.bfloat16)
    low = (left - middle.astype(jnp.float32)).astype(jnp.bfloat16)
    rows = jnp.concatenate([ref[...].astype(jnp.float32) for ref in part_refs], axis=0)
    rows = rows.astype(jnp.bfloat16)
    pieces = [
        lax.dot_general(w, rows, (((0,), (0,)), ((), ())), preferred_element_type=jnp.float32)
        for w in (high, middle, low)
    ]
    return pieces[0] + (pieces[1] + pieces[2])


def first_half_kernel(weigh_ref, *refs):
    part_refs, out_ref = refs[:-1], refs[-1]
    out_ref[...] = weighted(weigh_ref[: weigh_ref.shape[0] // 2, :], part_refs)


def second_half_kernel(weigh_ref, first_ref, *refs):
    part_refs, own_ref, send_ref = refs[:-2], refs[-2], refs[-1]
    size = part_refs[0].shape[0]
    weights = weigh_ref[weigh_ref.shape[0] // 2 :, :]
    weights = jnp.concatenate([weights, weights[-size:]], axis=0)
    result = first_ref[...] + weighted(weights, part_refs)
    half = own_ref.shape[0]
    own_ref[...] = result[:half]
    send_ref[...] = result[half:].astype(jnp.bfloat16)


def combine(weights, parts):
    depth = parts[0].shape[1]
    tokens = weights.shape[1]
    vmem = pl.BlockSpec(memory_space=pltpu.VMEM)
    params = pltpu.CompilerParams(vmem_limit_bytes=(8 << 20) + 8 * weights.shape[0] * depth)
    middle = (len(parts) - 1) // 2
    first = pl.pallas_call(
        first_half_kernel,
        out_shape=jax.ShapeDtypeStruct((tokens, depth), jnp.float32),
        in_specs=[vmem] * (1 + middle),
        out_specs=vmem,
        compiler_params=params,
        name="combine",
    )(weights, *parts[:middle])
    return pl.pallas_call(
        second_half_kernel,
        out_shape=[
            jax.ShapeDtypeStruct((tokens // 2, depth), jnp.float32),
            jax.ShapeDtypeStruct((tokens // 2, depth), jnp.bfloat16),
        ],
        in_specs=[vmem] * (2 + len(parts) - middle),
        out_specs=[vmem] * 2,
        compiler_params=params,
        name="combine",
    )(weights, first, *parts[middle:])


def finish_kernel(own_ref, received_ref, out_ref):
    result = own_ref[...] + received_ref[...].astype(jnp.float32)
    steps, tokens, _ = out_ref.shape
    for s in range(steps):
        out_ref[s] = result[s * tokens : (s + 1) * tokens].astype(jnp.bfloat16)


def finish(own, received, shape):
    vmem = pl.BlockSpec(memory_space=pltpu.VMEM)
    return pl.pallas_call(
        finish_kernel,
        out_shape=jax.ShapeDtypeStruct(shape, jnp.bfloat16),
        in_specs=[vmem] * 2,
        out_specs=vmem,
        compiler_params=pltpu.CompilerParams(vmem_limit_bytes=4 << 20),
        name="finish",
    )(own, received)


def mixture(
    hidden, norm_gain, router, expert_ids, replica, copy_table, gate_w, up_w, down_w, attended_mark
):
    groups = lax.axis_size("ep") // SPAN
    messages = groups // 2
    tokens = hidden.shape[1]
    slots = max(2, 2 * tokens * expert_ids.shape[2] // groups)
    deltas = lanes(groups)

    def swapped(value):
        return flipped(value, 1, 1)

    own_choice = (expert_ids.transpose(0, 2, 1), replica.transpose(0, 2, 1))
    other_choice = (swapped(own_choice[0]), swapped(own_choice[1]))
    normed, place, choose, packed = pack(
        slots,
        deltas,
        hidden,
        swapped(hidden),
        norm_gain[None, :],
        copy_table.T,
        own_choice,
        other_choice,
        router.shape[1],
    )

    def rounds(parts):
        return [
            flipped(part, SPAN * low, SPAN * high) for part, (low, high) in zip(parts, deltas)
        ]

    def to_near(part):
        return flipped(part, 0, SPAN)

    def to_far(part):
        return flipped(part, 2, SPAN + 2)

    weights = weigh(normed, router.T, place, choose)
    expert_weights = (gate_w, up_w, down_w)
    half = messages // 2
    size = packed[0].shape[0]
    received = rounds(packed[:-1])
    near_last, far_last = to_near(packed[-1]), to_far(packed[-1])
    held, mark = load(expert_weights, place)
    near = join([*received, near_last], [mark, far_last])
    far = flipped(join(received, [mark, far_last]), 2, 2)
    near_out, mark = experts([near, swapped(near)], held, mark, half * size)
    near_sums = [
        *add([near_out[0], swapped(near_out[2])], half, [], jnp.float32),
        *add([near_out[1], swapped(near_out[3])], half, [], jnp.float32),
    ]
    returned_near = to_near(near_sums[-1].astype(jnp.bfloat16))
    far = join([far], [mark, weights, attended_mark, near_sums[0]])
    far_parts = [far, far_last, swapped(far), swapped(far_last)]
    far_out, mark = experts(far_parts, held, mark, half * size)
    far_sums = [
        *add([far_out[0], swapped(far_out[2])], half, []),
        *add([far_out[1], swapped(far_out[3])], half, []),
    ]
    totals = []
    earlier = [mark]
    for near_sum, far_sum in zip(near_sums[:-1], far_sums[:-1]):
        totals += add([near_sum, flipped(far_sum, 2, 2)], 1, earlier)
        earlier = totals[-1:]
    returned = [*rounds(totals), returned_near, to_far(far_sums[-1])]
    own, send = combine(weights, returned)
    return finish(own, swapped(send), hidden.shape)


def per_device(
    hidden,
    norm_gain,
    router,
    expert_ids,
    replica,
    copy_table,
    gate_w,
    up_w,
    down_w,
    query,
    cache,
    lengths,
    fresh_kv,
):
    attended, attended_mark = attend(query, cache, lengths, fresh_kv)
    moe_out = mixture(
        hidden,
        norm_gain,
        router,
        expert_ids,
        replica,
        copy_table,
        gate_w,
        up_w,
        down_w,
        attended_mark,
    )
    return (attended, moe_out)


def solution(mesh):
    return jax.shard_map(
        per_device,
        mesh=mesh,
        in_specs=(
            P(None, ("groups", "ep"), None),
            P(),
            P(),
            P(None, ("groups", "ep"), None),
            P(None, ("groups", "ep"), None),
            P(),
            P(None, "ep"),
            P(None, "ep"),
            P("ep", None),
            P(None, ("groups", "ep"), None, None),
            P(("groups", "ep"), None, None),
            P(("groups", "ep")),
            P(None, ("groups", "ep"), None),
        ),
        out_specs=(P(None, ("groups", "ep"), None, None), P(None, ("groups", "ep"), None)),
        check_vma=False,
    )
```
